32 devices in a mesh: dp: 8 (over z, y), tensor: 4 (over x, core).
Axes of the slice: x: 2, y: 2, z: 4, core: 2. Of those that a mesh axis runs over, the one named last changes fastest.
Arguments:
- tokens: bfloat16 [16384, 1536], P(('dp', 'tensor')), may hold values from -6 to 6
- w_query: bfloat16 [1536, 1536], P('dp', 'tensor'), may hold values from -0.15625 to 0.15625
- w_keyval: bfloat16 [1536, 256], P('dp'), may hold values from -0.15625 to 0.15625
- w_out: bfloat16 [1536, 1536], P('tensor', 'dp'), may hold values from -0.625 to 0.625
- w_gate: bfloat16 [1536, 4608], P('dp', 'tensor'), may hold values from -0.15625 to 0.15625
- w_up: bfloat16 [1536, 4608], P('dp', 'tensor'), may hold values from -0.15625 to 0.15625
- w_down: bfloat16 [4608, 1536], P('tensor', 'dp'), may hold values from -0.09375 to 0.09375
- norm_gains: bfloat16 [2, 1536], P(None, 'dp'), may hold values from 0.25 to 1.75
- segment_ids: int32 [16384], P('dp'), may hold values from 0 to 2048, as said below
- grad_output: float32 [16384, 1536], P(('dp', 'tensor')), may hold values from -6 to 6
Outputs:
- output: bfloat16 [16384, 1536], P(('dp', 'tensor'))
- grad_tokens: float32 [16384, 1536], P(('dp', 'tensor'))
- grad_w_query: float32 [1536, 1536], P('dp', 'tensor')
- grad_w_keyval: float32 [1536, 256], P('dp')
- grad_w_out: float32 [1536, 1536], P('tensor', 'dp')
- grad_w_gate: float32 [1536, 4608], P('dp', 'tensor')
- grad_w_up: float32 [1536, 4608], P('dp', 'tensor')
- grad_w_down: float32 [4608, 1536], P('tensor', 'dp')
- grad_norm_gains: float32 [2, 1536], P(None, 'dp')
The draws below stay inside these ranges and needn't reach their ends.
Inputs may be any that keep to these rules, and one draw needn't show every extreme that they name: `segment_ids`: within each sequence of 2048 tokens the ids never fall except to 0; 0 marks padding, which only ends a sequence; a change of id starts a new document; the last document of every sequence has id 2048.
All inputs are finite; a program needn't handle non-finite values.
Results may differ from the reference program's by a relative error of at most 0.014.
Values may be sent and summed in bfloat16 or wider, within the bound.
A program may use at most 192 MiB of HBM per device.

```python
import jax
import jax.numpy as jnp
from jax import lax

D = 1536
HEADS = 12
HEAD_DIM = 128
FF = 4608
WINDOW = 1024
LENGTH = 2048
TOKENS = 16384
N_TENSOR = 4


def one_sequence(key):
    subkeys = jax.random.split(key, 4)
    places = jnp.arange(LENGTH, dtype=jnp.int32)
    long_first = jax.random.randint(subkeys[0], (), 1, LENGTH // 8 + 1)
    long_last = jax.random.randint(subkeys[1], (), LENGTH - LENGTH // 8, LENGTH - LENGTH // 16 + 1)
    padding = jax.random.randint(subkeys[2], (), 0, LENGTH // 32 + 1)
    cuts = jax.random.randint(subkeys[3], (LENGTH,), 0, 48) == 0
    inside = (places > long_first) & (places < long_last)
    starts_here = (cuts & ~inside | (places == long_first) | (places == long_last)) & (places > 0)
    numbers = jnp.cumsum(starts_here.astype(jnp.int32)) + 1
    last_number = jnp.sum(jnp.where(places == LENGTH - padding - 1, numbers, 0))
    shifted = numbers + (LENGTH - last_number)
    return jnp.where(places >= LENGTH - padding, 0, shifted).astype(jnp.int32)


def draw_segment_ids(key, part):
    seq_count = TOKENS // LENGTH
    return jax.vmap(one_sequence)(jax.random.split(key, seq_count)).reshape(TOKENS)


def strengthened(entries, stream_key, source, target, parts, factor):
    def block_of(axis_at):
        return (jnp.arange(entries.shape[axis_at]) // (entries.shape[axis_at] // parts)).reshape((-1,) + (1,) * (entries.ndim - 1 - axis_at))

    one_side = jax.random.permutation(stream_key, parts)[block_of(target)]
    second = (block_of(target) + parts // 2) % parts
    return jnp.where((block_of(source) == one_side) | (block_of(source) == second), factor * entries, entries)


def block_scale(stream_key, extent, shards, low, largest):
    level, own = 1.0, jax.random.fold_in(stream_key, 6)
    for position, blocks in shards:
        draws = jnp.exp(jax.random.uniform(jax.random.fold_in(own, position), (blocks,), jnp.float32, low / len(shards), largest / len(shards)))
        level = level * jnp.repeat(draws, extent[position] // blocks).reshape([-1 if axis == position else 1 for axis in range(len(extent))])
    return level


def gaussian(stream_key, shape, spread, most, cuts=(), kind=jnp.bfloat16):
    drawn = jax.random.normal(stream_key, shape, jnp.float32) * spread
    if len(cuts) > 0:
        drawn = block_scale(stream_key, shape, cuts, -0.22, 0.18) * drawn
    return jnp.clip(drawn, min=-most, max=most).astype(kind)


def bell_draw_with(rng, dims, width, reach, shards, heavy, kind=jnp.bfloat16):
    entries = width * jax.random.normal(rng, dims, jnp.float32)
    if shards:
        entries = entries * block_scale(rng, dims, shards, -0.22, 0.18)
    return jnp.clip(strengthened(entries, jax.random.fold_in(rng, 3), *heavy), -reach, reach).astype(kind)


def setup_inputs(seed: int = 0) -> dict:
    streams_of = jax.random.split(jax.random.key(seed), 11)
    return {
        "tokens": bell_draw_with(streams_of[0], (TOKENS, D), 1.0, 6.0, ((0, 32),), (0, 1, 32, 2.75)),
        "w_query": gaussian(streams_of[1], (D, HEADS * HEAD_DIM), D ** -0.5, 0.15625, ((0, 8), (1, 4))),
        "w_keyval": gaussian(streams_of[2], (D, 2 * HEAD_DIM), D ** -0.5, 0.15625, ((0, 8),)),
        "w_out": gaussian(streams_of[3], (HEADS * HEAD_DIM, D), (D // 16) ** -0.5, 0.625, ((0, 4), (1, 8))),
        "w_gate": gaussian(streams_of[4], (D, FF), D ** -0.5, 0.15625, ((0, 8), (1, 4))),
        "w_up": gaussian(streams_of[5], (D, FF), D ** -0.5, 0.15625, ((0, 8), (1, 4))),
        "w_down": gaussian(streams_of[6], (FF, D), FF ** -0.5, 0.09375, ((0, 4), (1, 8))),
        "norm_gains": jnp.clip(1.0 + 0.15 * jax.random.normal(streams_of[7], (2, D), jnp.float32), 0.25, 1.75).astype(jnp.bfloat16),
        "segment_ids": draw_segment_ids(jax.random.fold_in(streams_of[10], 71), 0),
        "grad_output": bell_draw_with(streams_of[9], (TOKENS, D), 1.0, 6.0, ((0, 32),), (0, 1, 32, 2.75), jnp.float32),
    }


@jax.custom_vjp
def low(v):
    return lax.optimization_barrier(v.astype(jnp.bfloat16)).astype(jnp.float32)

@jax.custom_vjp
def low_back(v):
    return v

def low_keep(v):
    return (low(v), None)

def low_pass(kept, grad):
    return (grad,)

def back_keep(v):
    return (v, None)

def back_low(kept, grad):
    return (low(grad),)
low.defvjp(low_keep, low_pass)
low_back.defvjp(back_keep, back_low)
norm_epsilon = 1e-06
masked_score = -1e+30

def highest_dot(left, right):
    return jnp.dot(left, right, precision=lax.Precision.HIGHEST, preferred_element_type=jnp.float32)

def rms_scaled(rows_in, gain_row):
    mean_square = lax.optimization_barrier(jnp.mean(rows_in * rows_in, axis=-1, keepdims=True))
    return rows_in * lax.rsqrt(mean_square + norm_epsilon) * gain_row

def positions_of(segments):
    places = jnp.arange(segments.shape[0], dtype=jnp.int32)
    previous = jnp.concatenate([jnp.full((1,), -1, jnp.int32), segments[:-1]])
    starts = lax.cummax(jnp.where(segments != previous, places, 0), axis=0)
    return (places - starts).astype(jnp.float32)

def rotary_tables(positions, head_dim):
    half_dim = head_dim // 2
    inverse = 10000.0 ** (-jnp.arange(half_dim, dtype=jnp.float32) / half_dim)
    angles = positions[:, None] * inverse[None, :]
    return (jnp.cos(angles), jnp.sin(angles))

def rotary(vectors, cosine_table, sine_table):
    half_dim = vectors.shape[-1] // 2
    first_half = vectors[..., :half_dim]
    second_half = vectors[..., half_dim:]
    return jnp.concatenate([first_half * cosine_table - second_half * sine_table, second_half * cosine_table + first_half * sine_table], axis=-1)

def attend_group(queries, key_rows, value_rows, segments):
    length_now = queries.shape[0]
    block_rows = min(512, length_now)
    score_scale = HEAD_DIM ** (-0.5)
    pad_keys = jnp.concatenate([jnp.zeros((WINDOW, HEAD_DIM), jnp.float32), key_rows])
    pad_values = jnp.concatenate([jnp.zeros((WINDOW, HEAD_DIM), jnp.float32), value_rows])
    pad_segments = jnp.concatenate([jnp.full((WINDOW,), -1, jnp.int32), segments])

    def one_block(first_row):
        q_blk = lax.dynamic_slice_in_dim(queries, first_row, block_rows, 0)
        k_blk = lax.dynamic_slice_in_dim(pad_keys, first_row, block_rows + WINDOW, 0)
        v_blk = lax.dynamic_slice_in_dim(pad_values, first_row, block_rows + WINDOW, 0)
        seg_q = lax.dynamic_slice_in_dim(segments, first_row, block_rows, 0)
        seg_k = lax.dynamic_slice_in_dim(pad_segments, first_row, block_rows + WINDOW, 0)
        q_pos = first_row + jnp.arange(block_rows, dtype=jnp.int32)
        k_pos = first_row - WINDOW + jnp.arange(block_rows + WINDOW, dtype=jnp.int32)
        row_gap = q_pos[:, None] - k_pos[None, :]
        allowed = (row_gap >= 0) & (row_gap < WINDOW) & (seg_q[:, None] == seg_k[None, :])
        raw_scores = jnp.einsum('qhd,kd->hqk', q_blk, k_blk, precision=lax.Precision.HIGHEST)
        scores = low_back(raw_scores) * score_scale
        scores = jnp.where(allowed[None], scores, masked_score)
        row_peak = lax.optimization_barrier(jnp.max(scores, axis=-1, keepdims=True))
        block_probs = jnp.exp(scores - row_peak)
        block_probs = block_probs / lax.optimization_barrier(jnp.sum(block_probs, axis=-1, keepdims=True))
        return jnp.einsum('hqk,kd->qhd', low(block_probs), v_blk, precision=lax.Precision.HIGHEST)
    starts_all = jnp.arange(length_now // block_rows, dtype=jnp.int32) * block_rows
    pieces = lax.map(jax.checkpoint(one_block), starts_all)
    return pieces.reshape(length_now, queries.shape[1], HEAD_DIM)

def layer_forward(x_rows, w_query, w_keyval, w_out, w_gate, w_up, w_down, norm_gains, segments):
    length_now = x_rows.shape[0]
    normed = low(rms_scaled(x_rows, norm_gains[0]))
    q_pre = low_back(highest_dot(normed, w_query))
    kv_pre = highest_dot(normed, w_keyval)
    cosine_table, sine_table = rotary_tables(positions_of(segments), HEAD_DIM)
    queries = low(rotary(q_pre.reshape(length_now, HEADS, HEAD_DIM), cosine_table[:, None, :], sine_table[:, None, :]))
    group_heads = HEADS // N_TENSOR
    outputs = []
    for head_group in range(N_TENSOR):
        kv_group = low_back(kv_pre)
        key_rows = low(rotary(kv_group[:, :HEAD_DIM], cosine_table, sine_table))
        value_rows = low(kv_group[:, HEAD_DIM:])
        group_queries = queries[:, head_group * group_heads:(head_group + 1) * group_heads]
        outputs.append(attend_group(group_queries, key_rows, value_rows, segments))
    attended = jnp.concatenate(outputs, axis=1)
    valid_rows = (segments != 0).astype(jnp.float32)[:, None]
    mixed_heads = low(low_back(attended).reshape(length_now, HEADS * HEAD_DIM) * valid_rows)
    residual = x_rows + low_back(highest_dot(mixed_heads, w_out))
    normed_two = low(rms_scaled(residual, norm_gains[1]))
    gate_act = low_back(highest_dot(normed_two, w_gate))
    up_act = low_back(highest_dot(normed_two, w_up))
    hidden = low(jax.nn.gelu(gate_act, approximate=True) * up_act)
    return residual + low_back(highest_dot(hidden, w_down))

def reference(tokens, w_query, w_keyval, w_out, w_gate, w_up, w_down, norm_gains, segment_ids, grad_output):
    weights = tuple((w.astype(jnp.float32) for w in (w_query, w_keyval, w_out, w_gate, w_up, w_down, norm_gains)))
    sequences = tokens.astype(jnp.float32).reshape(-1, LENGTH, D)
    seg_all = segment_ids.reshape(-1, LENGTH)
    cotangents = grad_output.astype(jnp.float32).reshape(-1, LENGTH, D)

    def per_sequence(accumulated, inputs):
        x_rows, segments, cotangent = inputs

        def forward(x_in, w_q, w_kv, w_o, w_g, w_u, w_d, gains_in):
            return layer_forward(x_in, w_q, w_kv, w_o, w_g, w_u, w_d, gains_in, segments)
        result, pullback = jax.vjp(forward, x_rows, weights[0], weights[1], weights[2], weights[3], weights[4], weights[5], weights[6])
        weight_grads = pullback(cotangent)
        new_acc = tuple((a + g for a, g in zip(accumulated, weight_grads[1:])))
        return (new_acc, (result.astype(jnp.bfloat16), weight_grads[0]))
    zero_grads = tuple((jnp.zeros_like(w) for w in weights))
    totals, (outputs, input_grads) = lax.scan(per_sequence, zero_grads, (sequences, seg_all, cotangents))
    return (outputs.reshape(TOKENS, D), input_grads.reshape(TOKENS, D), totals[0], totals[1], totals[2], totals[3], totals[4], totals[5], totals[6])
```

```python
import functools

import jax
import jax.numpy as jnp
from jax import lax
from jax.experimental import pallas as pl
from jax.experimental.pallas import tpu as pltpu
from jax.sharding import PartitionSpec as P

WINDOW = 1024
EPS = 1e-6
MASKED = -1e30
HEAD = 128
BLK = 256
LOG2E = 1.4426950408889634
F32 = jnp.float32
BF16 = jnp.bfloat16
MIB = 1 << 20

NT = (((1,), (1,)), ((), ()))
TN = (((0,), (0,)), ((), ()))


def dot(left, right):
    return jnp.dot(left, right, preferred_element_type=F32)


def dot_nt(left, right):
    return lax.dot_general(left, right, NT, preferred_element_type=F32)


def dot_tn(left, right):
    return lax.dot_general(left, right, TN, preferred_element_type=F32)


def qkv_kernel(x0, x1, x2, x3, gain, w, cos, sin, normed, q, k, v, held):
    i = pl.program_id(0)
    per = pl.num_programs(0) // 4
    for j, ref in enumerate((x0, x1, x2, x3)):

        @pl.when(i // per == j)
        def _(ref=ref):
            held[...] = ref[...]

    rows = held[...].astype(F32)
    scale = lax.rsqrt(jnp.mean(rows * rows, axis=-1, keepdims=True) + EPS)
    n = (rows * scale * gain[...]).astype(BF16)
    normed[...] = n
    y = dot(n, w[...])
    c, s = cos[...], sin[...]
    heads = q.shape[1] // HEAD

    def turned(a):
        return (a * c + pltpu.roll(a, HEAD // 2, 1) * s).astype(BF16)

    for h in range(heads):
        q[:, h * HEAD : (h + 1) * HEAD] = turned(y[:, h * HEAD : (h + 1) * HEAD])
    at = heads * HEAD
    k[...] = turned(y[:, at : at + HEAD])
    v[...] = y[:, at + HEAD : at + 2 * HEAD].astype(BF16)


def project(parts, gain, weights, cos, sin, q_cols):
    quarter, width = parts[0].shape
    rows = 4 * quarter
    per = quarter // BLK
    cols = q_cols + 2 * HEAD

    def part_spec(j):
        return pl.BlockSpec((BLK, width), lambda i: (jnp.clip(i - j * per, 0, per - 1), 0))

    def row_spec(n):
        return pl.BlockSpec((BLK, n), lambda i: (i, 0))

    return pl.pallas_call(
        qkv_kernel,
        grid=(rows // BLK,),
        in_specs=[part_spec(j) for j in range(4)]
        + [
            pl.BlockSpec((1, width), lambda i: (0, 0)),
            pl.BlockSpec((width, cols), lambda i: (0, 0)),
            row_spec(HEAD),
            row_spec(HEAD),
        ],
        out_specs=[row_spec(width), row_spec(q_cols), row_spec(HEAD), row_spec(HEAD)],
        out_shape=[
            jax.ShapeDtypeStruct((rows, width), BF16),
            jax.ShapeDtypeStruct((rows, q_cols), BF16),
            jax.ShapeDtypeStruct((rows, HEAD), BF16),
            jax.ShapeDtypeStruct((rows, HEAD), BF16),
        ],
        scratch_shapes=[pltpu.VMEM((BLK, width), BF16)],
        compiler_params=pltpu.CompilerParams(vmem_limit_bytes=32 * MIB),
        cost_estimate=pl.CostEstimate(
            flops=2 * rows * width * cols, bytes_accessed=4 * rows * width, transcendentals=0
        ),
        name="project",
    )(*parts, gain, weights, cos, sin)


def stacked(block, heads):
    return jnp.concatenate([block[:, h * HEAD : (h + 1) * HEAD] for h in range(heads)], axis=0)


def key_row(t, kb):
    per = 512 // BLK
    return pl.multiple_of(((t ^ (kb // per)) * per + kb % per) * BLK, BLK)


def query_block(t, i):
    per = 512 // BLK
    return (t ^ (i // per)) * per + i % per


def tiled3(row, heads):
    return jnp.concatenate([row] * heads, axis=1)


def attn_fwd_kernel(first, t_ref, q, k, v, pos, valid, mixed, lse):
    heads = q.shape[1] // HEAD
    wide = heads * BLK
    t = t_ref[0]
    qb = query_block(t, pl.program_id(0) + first)
    q3 = stacked(q[...], heads)
    at = qb * BLK + lax.broadcasted_iota(jnp.int32, (1, BLK), 1)
    low = at - jnp.minimum(pos[0], WINDOW - 1)
    at3, low3 = tiled3(at, heads), tiled3(low, heads)
    factor = HEAD**-0.5 * LOG2E

    def step(kb, carry):
        peak, total, acc = carry
        row = key_row(t, kb)
        s = dot_nt(k[pl.ds(row, BLK), :], q3) * factor
        u = kb * BLK + lax.broadcasted_iota(jnp.int32, (BLK, wide), 0)
        s = jnp.where((u <= at3) & (u >= low3), s, MASKED)
        new_peak = jnp.maximum(peak, jnp.max(s, axis=0, keepdims=True))
        p = jnp.exp2(s - new_peak)
        shrink = jnp.exp2(peak - new_peak)
        total = total * shrink + jnp.sum(p, axis=0, keepdims=True)
        acc = acc * shrink + dot_tn(v[pl.ds(row, BLK), :], p.astype(BF16))
        return new_peak, total, acc

    peak, total, acc = lax.fori_loop(
        jnp.maximum(qb - WINDOW // BLK, 0),
        qb + 1,
        step,
        (
            jnp.full((1, wide), MASKED, F32),
            jnp.zeros((1, wide), F32),
            jnp.zeros((HEAD, wide), F32),
        ),
    )
    lse[0] = peak + jnp.log2(total)
    acc = acc * (tiled3(valid[0], heads) / total)
    for h in range(heads):
        mixed[:, h * HEAD : (h + 1) * HEAD] = acc[:, h * BLK : (h + 1) * BLK].T.astype(BF16)


def attention_forward(t, q, k, v, pos, valid, first_row, rows):
    cols = q.shape[1]
    heads = cols // HEAD
    first = first_row // BLK
    blocks = rows // BLK
    full = pl.BlockSpec((k.shape[0], HEAD), lambda i, t: (0, 0))
    lane = pl.BlockSpec((1, 1, BLK), lambda i, t: (i + first, 0, 0))
    return pl.pallas_call(
        functools.partial(attn_fwd_kernel, first),
        grid_spec=pltpu.PrefetchScalarGridSpec(
            num_scalar_prefetch=1,
            grid=(blocks,),
            in_specs=[
                pl.BlockSpec((BLK, cols), lambda i, t: (i + first, 0)),
                full,
                full,
                lane,
                lane,
            ],
            out_specs=[
                pl.BlockSpec((BLK, cols), lambda i, t: (i, 0)),
                pl.BlockSpec((1, 1, heads * BLK), lambda i, t: (i, 0, 0)),
            ],
        ),
        out_shape=[
            jax.ShapeDtypeStruct((rows, cols), BF16),
            jax.ShapeDtypeStruct((blocks, 1, heads * BLK), F32),
        ],
        compiler_params=pltpu.CompilerParams(vmem_limit_bytes=32 * MIB),
        cost_estimate=pl.CostEstimate(
            flops=8 * rows * WINDOW * cols, bytes_accessed=8 * rows * cols, transcendentals=rows * WINDOW * heads
        ),
        name="attention_forward",
    )(t, q, k, v, pos, valid)


def attn_bwd_kernel(t_ref, q, do, mixed, lse, k, v, pos, cos, sin, cos_all, sin_all, dq, dkv, dk_acc, dv_acc):
    heads = q.shape[1] // HEAD
    wide = heads * BLK
    t = t_ref[0]
    i = pl.program_id(0)
    qb = query_block(t, i)

    @pl.when(i == 0)
    def _():
        dk_acc[...] = jnp.zeros_like(dk_acc)
        dv_acc[...] = jnp.zeros_like(dv_acc)

    q3 = stacked(q[...], heads)
    do3 = stacked(do[...], heads)
    centre3 = do3.astype(F32) * stacked(mixed[...], heads).astype(F32)
    centre = jnp.sum(centre3.T, axis=0, keepdims=True)
    at = qb * BLK + lax.broadcasted_iota(jnp.int32, (1, BLK), 1)
    low = at - jnp.minimum(pos[0], WINDOW - 1)
    at3, low3 = tiled3(at, heads), tiled3(low, heads)
    total = lse[0]
    factor = HEAD**-0.5 * LOG2E

    def step(kb, acc):
        row = key_row(t, kb)
        kblk = k[pl.ds(row, BLK), :]
        vblk = v[pl.ds(row, BLK), :]
        s = dot_nt(kblk, q3) * factor - total
        u = kb * BLK + lax.broadcasted_iota(jnp.int32, (BLK, wide), 0)
        p = jnp.exp2(jnp.where((u <= at3) & (u >= low3), s, MASKED))
        gp = dot_nt(vblk, do3)
        ds = (p * (gp - centre)).astype(BF16)
        dv_acc[pl.ds(row, BLK), :] += dot(p.astype(BF16), do3)
        dk_acc[pl.ds(row, BLK), :] += dot(ds, q3)
        return acc + dot_tn(kblk, ds)

    acc = lax.fori_loop(
        jnp.maximum(qb - WINDOW // BLK, 0), qb + 1, step, jnp.zeros((HEAD, wide), F32)
    )
    scale = HEAD**-0.5
    c, s = cos[...] * scale, sin[...] * scale
    for h in range(heads):
        a = acc[:, h * BLK : (h + 1) * BLK].T
        dq[:, h * HEAD : (h + 1) * HEAD] = (a * c - pltpu.roll(a, HEAD // 2, 1) * s).astype(BF16)

    @pl.when(i == pl.num_programs(0) - 1)
    def _():
        a = dk_acc[...] * scale
        dkv[:, :HEAD] = (a * cos_all[...] - pltpu.roll(a, HEAD // 2, 1) * sin_all[...]).astype(BF16)
        dkv[:, HEAD:] = dv_acc[...].astype(BF16)


def attention_backward(t, q, do, mixed, lse, k, v, pos, cos, sin):
    rows, cols = q.shape
    heads = cols // HEAD
    full = pl.BlockSpec((rows, HEAD), lambda i, t: (0, 0))
    row_q = pl.BlockSpec((BLK, cols), lambda i, t: (i, 0))
    row_h = pl.BlockSpec((BLK, HEAD), lambda i, t: (i, 0))
    return pl.pallas_call(
        attn_bwd_kernel,
        grid_spec=pltpu.PrefetchScalarGridSpec(
            num_scalar_prefetch=1,
            grid=(rows // BLK,),
            in_specs=[
                row_q,
                row_q,
                row_q,
                pl.BlockSpec((1, 1, heads * BLK), lambda i, t: (i, 0, 0)),
                full,
                full,
                pl.BlockSpec((1, 1, BLK), lambda i, t: (i, 0, 0)),
                row_h,
                row_h,
                full,
                full,
            ],
            out_specs=[row_q, pl.BlockSpec((rows, 2 * HEAD), lambda i, t: (0, 0))],
            scratch_shapes=[pltpu.VMEM((rows, HEAD), F32), pltpu.VMEM((rows, HEAD), F32)],
        ),
        out_shape=[
            jax.ShapeDtypeStruct((rows, cols), BF16),
            jax.ShapeDtypeStruct((rows, 2 * HEAD), BF16),
        ],
        compiler_params=pltpu.CompilerParams(vmem_limit_bytes=40 * MIB),
        cost_estimate=pl.CostEstimate(
            flops=20 * rows * WINDOW * cols, bytes_accessed=12 * rows * cols, transcendentals=rows * WINDOW * heads
        ),
        name="attention_backward",
    )(t, q, do, mixed, lse, k, v, pos, cos, sin, cos, sin)


def ffn_kernel(n, w, grad_hidden, hidden, grads):
    half = hidden.shape[1]
    y = dot(n[...], w[...])
    gate, up = y[:, :half], y[:, half:]
    gh = grad_hidden[...]
    root = (2.0 / jnp.pi) ** 0.5
    square = gate * gate
    th = jnp.tanh(root * gate * (1.0 + 0.044715 * square))
    one = 0.5 * (1.0 + th)
    act = gate * one
    slope = one + 0.5 * gate * (1.0 - th * th) * (root * (1.0 + 3.0 * 0.044715 * square))
    hidden[...] = (act * up).astype(BF16)
    grads[:, :half] = (gh * up * slope).astype(BF16)
    grads[:, half:] = (gh * act).astype(BF16)


def ffn_middle(n, w, grad_hidden):
    rows, width = n.shape
    half = grad_hidden.shape[1]

    def row_spec(c):
        return pl.BlockSpec((BLK, c), lambda i: (i, 0))

    return pl.pallas_call(
        ffn_kernel,
        grid=(rows // BLK,),
        in_specs=[row_spec(width), pl.BlockSpec((width, 2 * half), lambda i: (0, 0)), row_spec(half)],
        out_specs=[row_spec(half), row_spec(2 * half)],
        out_shape=[
            jax.ShapeDtypeStruct((rows, half), BF16),
            jax.ShapeDtypeStruct((rows, 2 * half), BF16),
        ],
        compiler_params=pltpu.CompilerParams(vmem_limit_bytes=50 * MIB),
        cost_estimate=pl.CostEstimate(
            flops=4 * rows * width * half, bytes_accessed=14 * rows * width, transcendentals=rows * half
        ),
        name="ffn_middle",
    )(n, w, grad_hidden)


def positions_of(segments):
    places = jnp.arange(segments.shape[0], dtype=jnp.int32)
    previous = jnp.concatenate([jnp.full((1,), -1, jnp.int32), segments[:-1]])
    starts = lax.cummax(jnp.where(segments != previous, places, 0), axis=0)
    return places - starts


def ring_order(n):
    return list(range(0, n, 2)) + list(range(n - 1, 0, -2))


def dp_gather(shard, n):
    if n != 8:
        return lax.all_gather(shard, "dp", axis=0, tiled=True)
    order = ring_order(n)
    place = {d: i for i, d in enumerate(order)}
    me = lax.axis_index("dp")
    rows = shard.shape[0]
    forth = [(order[i], order[(i + 1) % n]) for i in range(n)]
    back = [(order[(i + 1) % n], order[i]) for i in range(n)]

    def put(full, block, offset):
        table = jnp.array([order[(place[d] + offset) % n] for d in range(n)], jnp.int32)
        return lax.dynamic_update_slice_in_dim(full, block, table[me] * rows, 0)

    full = put(jnp.zeros((n * rows, shard.shape[1]), shard.dtype), shard, 0)
    ahead = behind = shard
    for s in range(1, n // 2 + 1):
        ahead = lax.ppermute(ahead, "dp", forth)
        full = put(full, ahead, -s)
        if s < n - n // 2:
            behind = lax.ppermute(behind, "dp", back)
            full = put(full, behind, s)
    return full


def dp_scatter(full, n, flip=False):
    if n != 8:
        return lax.psum_scatter(full, "dp", scatter_dimension=0, tiled=True).astype(F32)
    order = ring_order(n)
    if flip:
        order = order[::-1]
    place = {d: i for i, d in enumerate(order)}
    me = lax.axis_index("dp")
    rows = full.shape[0] // n
    forth = [(order[i], order[(i + 1) % n]) for i in range(n)]
    back = [(order[(i + 1) % n], order[i]) for i in range(n)]

    def part(offset):
        table = jnp.array([order[(place[d] + offset) % n] for d in range(n)], jnp.int32)
        return lax.dynamic_slice_in_dim(full, table[me] * rows, rows, 0)

    far = n // 2
    ahead = lax.ppermute(part(far), "dp", forth)
    behind = lax.ppermute(part(-(far - 1)), "dp", back)
    for s in range(1, far):
        ahead = lax.ppermute(ahead + part(far - s), "dp", forth)
        if s < far - 1:
            behind = lax.ppermute(behind + part(-(far - 1 - s)), "dp", back)
    return part(0).astype(F32) + ahead.astype(F32) + behind.astype(F32)


def per_device(
    n_dp,
    tokens,
    w_query,
    w_keyval,
    w_out,
    w_gate,
    w_up,
    w_down,
    norm_gains,
    segment_ids,
    grad_output,
):
    t = lax.axis_index("tensor").astype(jnp.int32)
    quarter, width = tokens.shape
    length = 4 * quarter
    q_cols = w_query.shape[1]
    units = w_gate.shape[1]

    def core(v):
        return lax.ppermute(v, "tensor", [(i, i ^ 1) for i in range(4)])

    def across(v):
        return lax.ppermute(v, "tensor", [(i, i ^ 2) for i in range(4)])

    def gather4(own):
        far = across(own)
        return own, core(own), far, core(far)

    def reduce4(own, other):
        half = own.shape[0] // 2
        chip = other[:half].astype(F32) + core(other[half:]).astype(F32)
        far = across(chip.astype(BF16))
        near = core(own[half:])
        return own[:half].astype(F32) + near.astype(F32) + far.astype(F32)

    gain_cols = jnp.pad(norm_gains.T, ((0, 0), (0, HEAD - 2)))
    attn_shard = jnp.concatenate([w_query, w_keyval, w_out.T, gain_cols], axis=1)
    ffn_shard = jnp.concatenate([w_gate, w_up, w_down.T], axis=1)
    attn_w = dp_gather(attn_shard, n_dp)
    ffn_shard, _ = lax.optimization_barrier((ffn_shard, attn_w))
    ffn_w = dp_gather(ffn_shard, n_dp)
    out_at = q_cols + 2 * HEAD
    w_out_t = attn_w[:, out_at : out_at + q_cols]
    gains = attn_w[:, out_at + q_cols : out_at + q_cols + 2].astype(F32).T
    gain_one_row, gain_two_row = gains[0:1], gains[1:2]
    w_gu, w_down_t = ffn_w[:, : 2 * units], ffn_w[:, 2 * units :]

    turn = t ^ jnp.arange(4, dtype=jnp.int32)
    positions = positions_of(segment_ids).reshape(4, quarter)[turn].reshape(length)
    valid = (segment_ids != 0).reshape(4, quarter)[turn].reshape(length).astype(F32)
    inverse = 10000.0 ** (-jnp.arange(HEAD // 2, dtype=F32) / (HEAD // 2))
    angles = positions.astype(F32)[:, None] * inverse[None, :]
    cos_half, sin_half = jnp.cos(angles), jnp.sin(angles)
    cos = jnp.concatenate([cos_half, cos_half], axis=1)
    sin = jnp.concatenate([-sin_half, sin_half], axis=1)
    pos3 = positions.reshape(length // BLK, 1, BLK)
    valid3 = valid.reshape(length // BLK, 1, BLK)
    t1 = t.reshape(1)

    parts = gather4(tokens)
    normed, q, k, v = project(parts, gain_one_row, attn_w, cos, sin, q_cols)
    half = length // 2
    mixed_far, lse_far = attention_forward(t1, q, k, v, pos3, valid3, half, half)
    mixed_near, lse_near = attention_forward(t1, q, k, v, pos3, valid3, 0, half)
    attn_far = dot_nt(mixed_far, w_out_t).astype(BF16)
    attn_near = dot_nt(mixed_near, w_out_t).astype(BF16)
    x_rows = tokens.astype(F32)
    residual = x_rows + reduce4(attn_near, attn_far)

    go = grad_output.astype(BF16)
    go, _ = lax.optimization_barrier((go, parts[2]))
    go_parts = gather4(go)
    go_near = jnp.concatenate(go_parts[:2])
    go_far = jnp.concatenate(go_parts[2:])
    gh_near = dot(go_near, w_down_t)
    gh_far = dot(go_far, w_down_t)

    scale_two = lax.rsqrt(jnp.mean(residual * residual, axis=-1, keepdims=True) + EPS)
    n2 = gather4((residual * scale_two * gain_two_row).astype(BF16))
    n2_near = jnp.concatenate(n2[:2])
    n2_far = jnp.concatenate(n2[2:])
    hidden_near, dgu_near = ffn_middle(n2_near, ffn_w, gh_near)
    hidden_far, dgu_far = ffn_middle(n2_far, ffn_w, gh_far)
    dn2_far = dot_nt(dgu_far, w_gu).astype(BF16)
    dn2_near = dot_nt(dgu_near, w_gu).astype(BF16)
    grad_n2 = reduce4(dn2_near, dn2_far)

    ffn_far = dot_nt(hidden_far, w_down_t).astype(BF16)
    ffn_near = dot_nt(hidden_near, w_down_t).astype(BF16)
    output = (residual + reduce4(ffn_near, ffn_far)).astype(BF16)

    dgu = jnp.concatenate([dgu_near, dgu_far])
    n2_all = jnp.concatenate([n2_near, n2_far])
    hidden = jnp.concatenate([hidden_near, hidden_far])
    go_all = jnp.concatenate([go_near, go_far])
    grad_w_gu = dot_tn(n2_all, dgu).astype(BF16)
    grad_w_down_t = dot_tn(go_all, hidden).astype(BF16)

    weighted = grad_n2 * gain_two_row
    inner = jnp.mean(residual * weighted, axis=-1, keepdims=True)
    grad_residual = grad_output + scale_two * weighted - residual * (scale_two**3 * inner)
    gain_two = jnp.sum(grad_n2 * residual * scale_two, axis=0)

    ga = jnp.concatenate(gather4(grad_residual.astype(BF16)))
    grad_mixed = (dot(ga, w_out_t) * valid[:, None]).astype(BF16)
    mixed = jnp.concatenate([mixed_near, mixed_far])
    lse = jnp.concatenate([lse_near, lse_far])
    dq, dkv = attention_backward(t1, q, grad_mixed, mixed, lse, k, v, pos3, cos, sin)
    dqkv = jnp.concatenate([dq, dkv], axis=1)
    w_qkv = attn_w[:, :out_at]
    dn_far = dot_nt(dqkv[half:], w_qkv).astype(BF16)
    dn_near = dot_nt(dqkv[:half], w_qkv).astype(BF16)
    grad_normed = reduce4(dn_near, dn_far)
    grad_w_out_t = dot_tn(ga, mixed).astype(BF16)
    grad_w_qkv = dot_tn(normed, dqkv).astype(BF16)

    scale_one = lax.rsqrt(jnp.mean(x_rows * x_rows, axis=-1, keepdims=True) + EPS)
    weighted = grad_normed * gain_one_row
    inner = jnp.mean(x_rows * weighted, axis=-1, keepdims=True)
    grad_tokens = grad_residual + scale_one * weighted - x_rows * (scale_one**3 * inner)
    gain_one = jnp.sum(grad_normed * x_rows * scale_one, axis=0)

    gu_shard = dp_scatter(grad_w_gu, n_dp)
    down_shard = dp_scatter(grad_w_down_t, n_dp, True)
    out_shard = dp_scatter(grad_w_out_t, n_dp, True)
    qkv_shard = dp_scatter(grad_w_qkv, n_dp)
    gain_cols = jnp.pad(jnp.stack([gain_one, gain_two], axis=1), ((0, 0), (0, HEAD - 2)))
    gain_shard = dp_scatter(gain_cols.astype(BF16), n_dp)
    small = jnp.concatenate([qkv_shard[:, q_cols:], gain_shard], axis=1)
    small = small + core(small)
    small = small + across(small)

    return (
        output,
        grad_tokens,
        qkv_shard[:, :q_cols],
        small[:, : 2 * HEAD],
        out_shard.T,
        gu_shard[:, :units],
        gu_shard[:, units:],
        down_shard.T,
        small[:, 2 * HEAD : 2 * HEAD + 2].T,
    )


def solution(mesh):
    return jax.shard_map(
        functools.partial(per_device, mesh.shape["dp"]),
        mesh=mesh,
        in_specs=(
            P(("dp", "tensor"), None),
            P("dp", "tensor"),
            P("dp", None),
            P("tensor", "dp"),
            P("dp", "tensor"),
            P("dp", "tensor"),
            P("tensor", "dp"),
            P(None, "dp"),
            P("dp"),
            P(("dp", "tensor"), None),
        ),
        out_specs=(
            P(("dp", "tensor"), None),
            P(("dp", "tensor"), None),
            P("dp", "tensor"),
            P("dp", None),
            P("tensor", "dp"),
            P("dp", "tensor"),
            P("dp", "tensor"),
            P("tensor", "dp"),
            P(None, "dp"),
        ),
        check_vma=False,
    )
```

```python
import functools

import jax
import jax.numpy as jnp
from jax import lax
from jax.experimental import pallas as pl
from jax.experimental.pallas import tpu as pltpu
from jax.sharding import PartitionSpec as P

WINDOW = 1024
EPS = 1e-6
MASKED = -1e30
HEAD = 128
BLK = 256
LOG2E = 1.4426950408889634
F32 = jnp.float32
BF16 = jnp.bfloat16
MIB = 1 << 20

NT = (((1,), (1,)), ((), ()))
TN = (((0,), (0,)), ((), ()))


def dot(left, right):
    return jnp.dot(left, right, preferred_element_type=F32)


def dot_nt(left, right):
    return lax.dot_general(left, right, NT, preferred_element_type=F32)


def dot_tn(left, right):
    return lax.dot_general(left, right, TN, preferred_element_type=F32)


def stacked(block, heads):
    return jnp.concatenate([block[:, h * HEAD : (h + 1) * HEAD] for h in range(heads)], axis=0)


def partner(t, j):
    rem, div = lax.rem, lax.div
    two = jnp.int32(2)
    j = jnp.int32(j)
    return rem(div(t, two) + div(j, two), two) * 2 + rem(rem(t, two) + rem(j, two), two)


def key_row(t, kb):
    per = 512 // BLK
    return pl.multiple_of((partner(t, lax.div(kb, per)) * per + lax.rem(kb, per)) * BLK, BLK)


def query_block(t, i):
    per = 512 // BLK
    i = jnp.int32(i)
    return partner(t, lax.div(i, per)) * per + lax.rem(i, per)


def tiled3(row, heads):
    return jnp.concatenate([row] * heads, axis=1)


def attend(t, i, q, k, v, pos, valid, mixed, lse):
    cols = q.shape[1]
    heads = cols // HEAD
    wide = heads * BLK
    qb = query_block(t, i)
    mine = pl.ds(pl.multiple_of(i * BLK, BLK), BLK)
    q3 = stacked(q[mine, :], heads)
    at = qb * BLK + lax.broadcasted_iota(jnp.int32, (1, BLK), 1)
    low = at - jnp.minimum(pos[i], WINDOW - 1)
    at3, low3 = tiled3(at, heads), tiled3(low, heads)
    factor = HEAD**-0.5 * LOG2E

    def step(kb, carry):
        peak, total, acc = carry
        row = key_row(t, kb)
        s = dot_nt(k[pl.ds(row, BLK), :], q3) * factor
        u = kb * BLK + lax.broadcasted_iota(jnp.int32, (BLK, wide), 0)
        s = jnp.where((u <= at3) & (u >= low3), s, MASKED)
        new_peak = jnp.maximum(peak, jnp.max(s, axis=0, keepdims=True))
        p = jnp.exp2(s - new_peak)
        shrink = jnp.exp2(peak - new_peak)
        total = total * shrink + jnp.sum(p, axis=0, keepdims=True)
        acc = acc * shrink + dot_tn(v[pl.ds(row, BLK), :], p.astype(BF16))
        return new_peak, total, acc

    peak, total, acc = lax.fori_loop(
        jnp.maximum(qb - WINDOW // BLK, 0),
        qb + 1,
        step,
        (
            jnp.full((1, wide), MASKED, F32),
            jnp.zeros((1, wide), F32),
            jnp.zeros((HEAD, wide), F32),
        ),
    )
    lse[i] = peak + jnp.log2(total)
    acc = acc * (tiled3(valid[i], heads) / total)
    mixed[mine, :] = jnp.concatenate(
        [acc[:, h * BLK : (h + 1) * BLK].T for h in range(heads)], axis=1
    ).astype(BF16)


def ring_device(p, n):
    p = lax.rem(p + n, jnp.int32(n))
    down = lax.div(p, jnp.int32(n // 2))
    return (1 - down) * 2 * p + down * (2 * (n - 1 - p) + 1)


def ring_place(d, n):
    z, y = lax.div(d, jnp.int32(2)), lax.rem(d, jnp.int32(2))
    return z + y * (n - 1 - 2 * z)


def send(src, dst, sems, at, device):
    return pltpu.make_async_remote_copy(
        src_ref=src,
        dst_ref=dst,
        send_sem=sems.at[0, at],
        recv_sem=sems.at[1, at],
        device_id=device,
        device_id_type=pl.DeviceIdType.MESH,
    )


class Ring:
    def __init__(self, shard, full, sems, first_sem, own, n, direction):
        self.shard, self.full, self.sems, self.at, self.own = shard, full, sems, first_sem, own
        self.n, self.dir = n, direction
        self.copies = {}

    def block(self, offset, place):
        rows = self.shard.shape[0]
        at = ring_device(place + offset * self.dir, self.n) * rows
        return self.full.at[pl.ds(pl.multiple_of(at, rows & -rows), rows), :]

    def begin(self, place):
        self.place = place
        if self.n == 8:
            target = self.block(0, place)
        else:
            target = self.full
        self.local = pltpu.make_async_copy(self.shard, target, self.own)
        self.local.start()
        self.start(1)

    def start(self, s):
        if self.n != 8:
            return
        for way in (0, 1):
            if s > self.n // 2 - way:
                continue
            sign = 1 - 2 * way
            block = self.block(-sign * (s - 1), self.place)
            device = ring_device(self.place + sign * self.dir, self.n)
            src = self.shard if s == 1 else block
            at = self.at + 2 * (s - 1) + way
            copy = send(src, block, self.sems, at, {"dp": device})
            copy.start()
            self.copies[s, way] = copy

    def arrived(self, s):
        for way in (0, 1):
            if (s, way) in self.copies:
                self.copies[s, way].wait_recv()

    def next(self, s):
        self.arrived(s)
        self.start(s + 1)

    def end(self):
        for copy in self.copies.values():
            copy.wait_send()
        self.local.wait()


def front_kernel(
    n_dp,
    tokens,
    grad_output,
    shard_a,
    shard_d,
    shard_g,
    pos,
    valid,
    cos,
    sin,
    w_a_out,
    w_d_out,
    w_g,
    gains,
    normed_out,
    q_out,
    k_out,
    v_out,
    mixed_out,
    lse,
    residual_out,
    n2_out,
    go_out,
    gh_out,
    w_a,
    w_d,
    x4,
    normed,
    q,
    k,
    v,
    mixed,
    near_recv,
    far_recv,
    x_recv,
    sum_buf,
    n2_own,
    go_buf,
    gh_buf,
    res,
    ring_sems,
    pair_sems,
    local_sems,
):
    quarter, width = tokens.shape
    q_cols = q.shape[1]
    heads = q_cols // HEAD
    kv_at = q_cols + 2 * HEAD
    gain_at = kv_at + q_cols
    t = lax.axis_index("tensor").astype(jnp.int32)
    place = ring_place(lax.axis_index("dp").astype(jnp.int32), n_dp)
    near_id, far_id = {"tensor": partner(t, 1)}, {"tensor": partner(t, 2)}

    barrier = pltpu.get_barrier_semaphore()
    partners = [near_id, far_id]
    if n_dp == 8:
        partners += [{"dp": ring_device(place + 1, n_dp)}, {"dp": ring_device(place - 1, n_dp)}]
    for device in partners:
        pl.semaphore_signal(barrier, inc=1, device_id=device, device_id_type=pl.DeviceIdType.MESH)
    pl.semaphore_wait(barrier, len(partners))

    def rows_of(ref, j, size=1):
        return ref.at[pl.ds(j * quarter, size * quarter), :]

    used = [0]

    def local(src, dst):
        copy = pltpu.make_async_copy(src, dst, local_sems.at[used[0]])
        used[0] += 1
        copy.start()
        return copy

    ring_a = Ring(shard_a, w_a, ring_sems, 0, local_sems.at[24], n_dp, 1)
    ring_d = Ring(shard_d, w_d, ring_sems, 8, local_sems.at[25], n_dp, 1)
    ring_g = Ring(shard_g, w_g, ring_sems, 16, local_sems.at[26], n_dp, -1)

    ring_a.begin(place)
    x_far = send(tokens, rows_of(x4, 2), pair_sems, 0, far_id)
    x_far.start()
    x_near = send(tokens, rows_of(x4, 1), pair_sems, 1, near_id)
    x_near.start()
    x_own = local(tokens, rows_of(x4, 0))
    go_in = local(grad_output, res)
    for s in (1, 2, 3):
        ring_a.next(s)
    ring_d.begin(place)
    ring_g.begin(place)
    ring_a.arrived(4)
    ring_a.local.wait()

    gain_rows = w_a[:, gain_at : gain_at + HEAD].astype(F32).T
    gains[...] = gain_rows[:8]

    def project(i, carry):
        mine = pl.ds(pl.multiple_of(i * BLK, BLK), BLK)
        rows = x4[mine, :].astype(F32)
        scale = lax.rsqrt(jnp.mean(rows * rows, axis=-1, keepdims=True) + EPS)
        n = (rows * scale * gains[0:1, :]).astype(BF16)
        normed[mine, :] = n
        y = dot(n, w_a[:, :kv_at])
        c, s = cos[mine, :], sin[mine, :]

        def turned(a):
            return (a * c + pltpu.roll(a, HEAD // 2, 1) * s).astype(BF16)

        q[mine, :] = jnp.concatenate(
            [turned(y[:, h * HEAD : (h + 1) * HEAD]) for h in range(heads)], axis=1
        )
        k[mine, :] = turned(y[:, q_cols : q_cols + HEAD])
        v[mine, :] = y[:, q_cols + HEAD : kv_at].astype(BF16)
        return carry

    per = quarter // BLK
    x_own.wait()
    x_near.wait_recv()
    lax.fori_loop(0, 2 * per, project, 0)
    x_far.wait_recv()
    x_last = send(rows_of(x4, 2), rows_of(x4, 3), pair_sems, 2, near_id)
    x_last.start()
    go_in.wait()
    go_buf[...] = res[...].astype(BF16)
    go_far = send(go_buf, rows_of(go_out, 2), pair_sems, 3, far_id)
    go_far.start()
    go_near = send(go_buf, rows_of(go_out, 1), pair_sems, 4, near_id)
    go_near.start()
    go_own = local(go_buf, rows_of(go_out, 0))
    x_last.wait_recv()
    lax.fori_loop(2 * per, 4 * per, project, 0)
    copies = [
        local(normed, normed_out),
        local(q, q_out),
        local(k, k_out),
        local(v, v_out),
        local(w_a, w_a_out),
    ]

    def attention(i, carry):
        attend(t, i, q, k, v, pos, valid, mixed, lse)
        return carry

    part = x4

    def out_product(i, carry):
        mine = pl.ds(pl.multiple_of(i * BLK, BLK), BLK)
        part[mine, :] = dot_nt(mixed[mine, :], w_a[:, kv_at:gain_at]).astype(BF16)
        return carry

    x_last.wait_send()
    lax.fori_loop(2 * per, 4 * per, attention, 0)
    ring_d.next(1)
    lax.fori_loop(2 * per, 4 * per, out_product, 0)
    part_far = send(rows_of(part, 3), far_recv, pair_sems, 5, near_id)
    part_far.start()
    lax.fori_loop(0, 1, attention, 0)
    part_far.wait_recv()
    sum_buf[...] = (part[pl.ds(2 * quarter, quarter), :].astype(F32) + far_recv[...].astype(F32)).astype(BF16)
    sum_far = send(sum_buf, x_recv, pair_sems, 6, far_id)
    sum_far.start()
    ring_g.next(1)
    lax.fori_loop(1, 2 * per, attention, 0)
    lax.fori_loop(0, 2 * per, out_product, 0)
    part_near = send(rows_of(part, 1), near_recv, pair_sems, 7, near_id)
    part_near.start()
    copies.append(local(mixed, mixed_out))
    ring_d.next(2)
    ring_d.next(3)
    ring_g.next(2)
    go_far.wait_recv()
    go_last = send(rows_of(go_out, 2), rows_of(go_out, 3), pair_sems, 8, near_id)
    go_last.start()
    part_near.wait_recv()
    sum_far.wait_recv()

    res[...] = (
        tokens[...].astype(F32)
        + part[pl.ds(0, quarter), :].astype(F32)
        + near_recv[...].astype(F32)
        + x_recv[...].astype(F32)
    )
    scale_two = lax.rsqrt(jnp.mean(res[...] * res[...], axis=-1, keepdims=True) + EPS)
    n2_own[...] = (res[...] * scale_two * gains[1:2, :]).astype(BF16)
    n2_far = send(n2_own, rows_of(n2_out, 2), pair_sems, 9, far_id)
    n2_far.start()
    n2_near = send(n2_own, rows_of(n2_out, 1), pair_sems, 10, near_id)
    n2_near.start()
    copies.append(local(n2_own, rows_of(n2_out, 0)))
    copies.append(local(res, residual_out))

    ring_d.arrived(4)
    ring_d.local.wait()
    copies.append(local(w_d, w_d_out))
    go_far.wait_send()
    go_near.wait_send()
    go_own.wait()

    def grad_hidden(i, carry):
        mine = pl.ds(pl.multiple_of(i * BLK, BLK), BLK)
        gh_buf[mine, :] = dot(go_buf[mine, :], w_d[...]).astype(BF16)
        return carry

    for j in range(4):
        if j == 1:
            go_near.wait_recv()
        if j == 3:
            go_last.wait_recv()
        if j > 0:
            load = local(rows_of(go_out, j), go_buf)
            load.wait()
        if j > 0:
            store.wait()
        lax.fori_loop(0, per, grad_hidden, 0)
        store = local(gh_buf, rows_of(gh_out, j))
        if j == 1:
            ring_g.next(3)

    n2_far.wait_recv()
    n2_last = send(rows_of(n2_out, 2), rows_of(n2_out, 3), pair_sems, 11, near_id)
    n2_last.start()
    ring_g.arrived(4)
    store.wait()
    for copy in copies:
        copy.wait()
    for copy in (x_far, x_near, part_far, sum_far, part_near, go_last, n2_far, n2_near, n2_last):
        copy.wait_send()
    n2_near.wait_recv()
    n2_last.wait_recv()
    ring_a.copies and [c.wait_send() for c in ring_a.copies.values()]
    ring_d.copies and [c.wait_send() for c in ring_d.copies.values()]
    ring_g.end()


def front(n_dp, tokens, grad_output, shard_a, shard_d, shard_g, pos, valid, cos, sin, q_cols):
    quarter, width = tokens.shape
    length = 4 * quarter
    heads = q_cols // HEAD
    units = shard_d.shape[1]
    cols_a = shard_a.shape[1]
    vmem = pl.BlockSpec(memory_space=pltpu.VMEM)
    hbm = pl.BlockSpec(memory_space=pl.ANY)
    blocks = length // BLK

    def out(rows, cols, kind=BF16):
        return jax.ShapeDtypeStruct((rows, cols), kind)

    return pl.pallas_call(
        functools.partial(front_kernel, n_dp),
        in_specs=[vmem, hbm, hbm, hbm, hbm, vmem, vmem, vmem, vmem],
        out_specs=[hbm, hbm, hbm, vmem, hbm, hbm, hbm, hbm, hbm, vmem, hbm, hbm, hbm, hbm],
        out_shape=[
            out(width, cols_a),
            out(width, units),
            out(width, 2 * units),
            out(8, width, F32),
            out(length, width),
            out(length, q_cols),
            out(length, HEAD),
            out(length, HEAD),
            out(length, q_cols),
            jax.ShapeDtypeStruct((blocks, 1, heads * BLK), F32),
            out(quarter, width, F32),
            out(length, width),
            out(length, width),
            out(length, units),
        ],
        scratch_shapes=[
            pltpu.VMEM((width, cols_a), BF16),
            pltpu.VMEM((width, units), BF16),
            pltpu.VMEM((length, width), BF16),
            pltpu.VMEM((length, width), BF16),
            pltpu.VMEM((length, q_cols), BF16),
            pltpu.VMEM((length, HEAD), BF16),
            pltpu.VMEM((length, HEAD), BF16),
            pltpu.VMEM((length, q_cols), BF16),
            pltpu.VMEM((quarter, width), BF16),
            pltpu.VMEM((quarter, width), BF16),
            pltpu.VMEM((quarter, width), BF16),
            pltpu.VMEM((quarter, width), BF16),
            pltpu.VMEM((quarter, width), BF16),
            pltpu.VMEM((quarter, width), BF16),
            pltpu.VMEM((quarter, units), BF16),
            pltpu.VMEM((quarter, width), F32),
            pltpu.SemaphoreType.DMA((2, 24)),
            pltpu.SemaphoreType.DMA((2, 12)),
            pltpu.SemaphoreType.DMA((32,)),
        ],
        compiler_params=pltpu.CompilerParams(
            collective_id=0, has_side_effects=True, vmem_limit_bytes=58 * MIB
        ),
        cost_estimate=pl.CostEstimate(
            flops=12 * length * width * q_cols, bytes_accessed=64 * MIB, transcendentals=0
        ),
        name="front",
    )(tokens, grad_output, shard_a, shard_d, shard_g, pos, valid, cos, sin)


def attn_bwd_kernel(t_ref, q, do, mixed, lse, k, v, pos, cos, sin, cos_all, sin_all, dq, dkv, dk_acc, dv_acc):
    heads = q.shape[1] // HEAD
    wide = heads * BLK
    t = t_ref[0]
    i = pl.program_id(0)
    qb = query_block(t, i)

    @pl.when(i == 0)
    def _():
        dk_acc[...] = jnp.zeros_like(dk_acc)
        dv_acc[...] = jnp.zeros_like(dv_acc)

    q3 = stacked(q[...], heads)
    do3 = stacked(do[...], heads)
    centre3 = do3.astype(F32) * stacked(mixed[...], heads).astype(F32)
    centre = jnp.sum(centre3.T, axis=0, keepdims=True)
    at = qb * BLK + lax.broadcasted_iota(jnp.int32, (1, BLK), 1)
    low = at - jnp.minimum(pos[0], WINDOW - 1)
    at3, low3 = tiled3(at, heads), tiled3(low, heads)
    total = lse[0]
    factor = HEAD**-0.5 * LOG2E

    def step(kb, acc):
        row = key_row(t, kb)
        kblk = k[pl.ds(row, BLK), :]
        vblk = v[pl.ds(row, BLK), :]
        s = dot_nt(kblk, q3) * factor - total
        u = kb * BLK + lax.broadcasted_iota(jnp.int32, (BLK, wide), 0)
        p = jnp.exp2(jnp.where((u <= at3) & (u >= low3), s, MASKED))
        gp = dot_nt(vblk, do3)
        ds = (p * (gp - centre)).astype(BF16)
        dv_acc[pl.ds(row, BLK), :] += dot(p.astype(BF16), do3)
        dk_acc[pl.ds(row, BLK), :] += dot(ds, q3)
        return acc + dot_tn(kblk, ds)

    acc = lax.fori_loop(
        jnp.maximum(qb - WINDOW // BLK, 0), qb + 1, step, jnp.zeros((HEAD, wide), F32)
    )
    scale = HEAD**-0.5
    c, s = cos[...] * scale, sin[...] * scale
    for h in range(heads):
        a = acc[:, h * BLK : (h + 1) * BLK].T
        dq[:, h * HEAD : (h + 1) * HEAD] = (a * c - pltpu.roll(a, HEAD // 2, 1) * s).astype(BF16)

    @pl.when(i == pl.num_programs(0) - 1)
    def _():
        a = dk_acc[...] * scale
        dkv[:, :HEAD] = (a * cos_all[...] - pltpu.roll(a, HEAD // 2, 1) * sin_all[...]).astype(BF16)
        dkv[:, HEAD:] = dv_acc[...].astype(BF16)


def attention_backward(t, q, do, mixed, lse, k, v, pos, cos, sin):
    rows, cols = q.shape
    heads = cols // HEAD
    full = pl.BlockSpec((rows, HEAD), lambda i, t: (0, 0))
    row_q = pl.BlockSpec((BLK, cols), lambda i, t: (i, 0))
    row_h = pl.BlockSpec((BLK, HEAD), lambda i, t: (i, 0))
    return pl.pallas_call(
        attn_bwd_kernel,
        grid_spec=pltpu.PrefetchScalarGridSpec(
            num_scalar_prefetch=1,
            grid=(rows // BLK,),
            in_specs=[
                row_q,
                row_q,
                row_q,
                pl.BlockSpec((1, 1, heads * BLK), lambda i, t: (i, 0, 0)),
                full,
                full,
                pl.BlockSpec((1, 1, BLK), lambda i, t: (i, 0, 0)),
                row_h,
                row_h,
                full,
                full,
            ],
            out_specs=[row_q, pl.BlockSpec((rows, 2 * HEAD), lambda i, t: (0, 0))],
            scratch_shapes=[pltpu.VMEM((rows, HEAD), F32), pltpu.VMEM((rows, HEAD), F32)],
        ),
        out_shape=[
            jax.ShapeDtypeStruct((rows, cols), BF16),
            jax.ShapeDtypeStruct((rows, 2 * HEAD), BF16),
        ],
        compiler_params=pltpu.CompilerParams(vmem_limit_bytes=40 * MIB),
        cost_estimate=pl.CostEstimate(
            flops=20 * rows * WINDOW * cols, bytes_accessed=12 * rows * cols, transcendentals=rows * WINDOW * heads
        ),
        name="attention_backward",
    )(t, q, do, mixed, lse, k, v, pos, cos, sin, cos, sin)


def ffn_kernel(n, w, grad_hidden, hidden, grads):
    half = hidden.shape[1]
    y = dot(n[...], w[...])
    gate, up = y[:, :half], y[:, half:]
    gh = grad_hidden[...].astype(F32)
    root = (2.0 / jnp.pi) ** 0.5
    square = gate * gate
    th = jnp.tanh(root * gate * (1.0 + 0.044715 * square))
    one = 0.5 * (1.0 + th)
    act = gate * one
    slope = one + 0.5 * gate * (1.0 - th * th) * (root * (1.0 + 3.0 * 0.044715 * square))
    hidden[...] = (act * up).astype(BF16)
    grads[:, :half] = (gh * up * slope).astype(BF16)
    grads[:, half:] = (gh * act).astype(BF16)


def ffn_middle(n, w, grad_hidden, first_row, rows, earlier):
    length, width = n.shape
    half = grad_hidden.shape[1]
    first = first_row // BLK

    def row_spec(c):
        return pl.BlockSpec((BLK, c), lambda i: (i + first, 0))

    def body(n_ref, w_ref, gh_ref, *refs):
        ffn_kernel(n_ref, w_ref, gh_ref, *refs[-2:])

    return pl.pallas_call(
        body,
        grid=(rows // BLK,),
        in_specs=[row_spec(width), pl.BlockSpec((width, 2 * half), lambda i: (0, 0)), row_spec(half)]
        + [pl.BlockSpec(memory_space=pl.ANY)] * len(earlier),
        out_specs=[row_spec(half), row_spec(2 * half)],
        out_shape=[
            jax.ShapeDtypeStruct((length, half), BF16),
            jax.ShapeDtypeStruct((length, 2 * half), BF16),
        ],
        input_output_aliases={3: 0, 4: 1} if earlier else {},
        compiler_params=pltpu.CompilerParams(vmem_limit_bytes=50 * MIB),
        cost_estimate=pl.CostEstimate(
            flops=4 * rows * width * half, bytes_accessed=14 * rows * width, transcendentals=rows * half
        ),
        name="ffn_middle",
    )(n, w, grad_hidden, *earlier)


def positions_of(segments):
    places = jnp.arange(segments.shape[0], dtype=jnp.int32)
    previous = jnp.concatenate([jnp.full((1,), -1, jnp.int32), segments[:-1]])
    starts = lax.cummax(jnp.where(segments != previous, places, 0), axis=0)
    return places - starts


def ring_order(n):
    return list(range(0, n, 2)) + list(range(n - 1, 0, -2))


def dp_scatter(full, n, flip=False):
    if n != 8:
        return lax.psum_scatter(full, "dp", scatter_dimension=0, tiled=True).astype(F32)
    order = ring_order(n)
    if flip:
        order = order[::-1]
    place = {d: i for i, d in enumerate(order)}
    me = lax.axis_index("dp")
    rows = full.shape[0] // n
    forth = [(order[i], order[(i + 1) % n]) for i in range(n)]
    back = [(order[(i + 1) % n], order[i]) for i in range(n)]

    def part(offset):
        table = jnp.array([order[(place[d] + offset) % n] for d in range(n)], jnp.int32)
        return lax.dynamic_slice_in_dim(full, table[me] * rows, rows, 0)

    far = n // 2
    ahead = lax.ppermute(part(far), "dp", forth)
    behind = lax.ppermute(part(-(far - 1)), "dp", back)
    for s in range(1, far):
        ahead = lax.ppermute(ahead + part(far - s), "dp", forth)
        if s < far - 1:
            behind = lax.ppermute(behind + part(-(far - 1 - s)), "dp", back)
    return part(0).astype(F32) + ahead.astype(F32) + behind.astype(F32)


def per_device(
    n_dp,
    tokens,
    w_query,
    w_keyval,
    w_out,
    w_gate,
    w_up,
    w_down,
    norm_gains,
    segment_ids,
    grad_output,
):
    t = lax.axis_index("tensor").astype(jnp.int32)
    quarter, width = tokens.shape
    length = 4 * quarter
    q_cols = w_query.shape[1]
    units = w_gate.shape[1]

    def core(v):
        return lax.ppermute(v, "tensor", [(i, i ^ 1) for i in range(4)])

    def across(v):
        return lax.ppermute(v, "tensor", [(i, i ^ 2) for i in range(4)])

    def gather4(own):
        far = across(own)
        return own, core(own), far, core(far)

    def reduce4(own, other):
        half = own.shape[0] // 2
        chip = other[:half].astype(F32) + core(other[half:]).astype(F32)
        far = across(chip.astype(BF16))
        near = core(own[half:])
        return own[:half].astype(F32) + near.astype(F32) + far.astype(F32)

    gain_cols = jnp.pad(norm_gains.T, ((0, 0), (0, HEAD - 2)))
    shard_a = jnp.concatenate([w_query, w_keyval, w_out.T, gain_cols], axis=1)
    shard_d = w_down.T
    shard_g = jnp.concatenate([w_gate, w_up], axis=1)
    if n_dp != 8:
        shard_a, shard_d, shard_g = (
            lax.all_gather(w, "dp", axis=0, tiled=True) for w in (shard_a, shard_d, shard_g)
        )

    turn = t ^ jnp.arange(4, dtype=jnp.int32)
    positions = positions_of(segment_ids).reshape(4, quarter)[turn].reshape(length)
    valid = (segment_ids != 0).reshape(4, quarter)[turn].reshape(length).astype(F32)
    inverse = 10000.0 ** (-jnp.arange(HEAD // 2, dtype=F32) / (HEAD // 2))
    angles = positions.astype(F32)[:, None] * inverse[None, :]
    cos_half, sin_half = jnp.cos(angles), jnp.sin(angles)
    cos = jnp.concatenate([cos_half, cos_half], axis=1)
    sin = jnp.concatenate([-sin_half, sin_half], axis=1)
    pos3 = positions.reshape(length // BLK, 1, BLK)
    valid3 = valid.reshape(length // BLK, 1, BLK)
    t1 = t.reshape(1)

    (w_a, w_down_t, w_gu, gains, normed, q, k, v, mixed, lse, residual, n2, go_all, gh) = front(
        n_dp, tokens, grad_output, shard_a, shard_d, shard_g, pos3, valid3, cos, sin, q_cols
    )
    kv_at = q_cols + 2 * HEAD
    w_out_t = w_a[:, kv_at : kv_at + q_cols]
    gain_one_row, gain_two_row = gains[0:1], gains[1:2]
    x_rows = tokens.astype(F32)
    scale_two = lax.rsqrt(jnp.mean(residual * residual, axis=-1, keepdims=True) + EPS)
    half = length // 2

    hidden, dgu = ffn_middle(n2, w_gu, gh, half, half, ())
    dn2_far = dot_nt(dgu[half:], w_gu).astype(BF16)
    hidden, dgu = ffn_middle(n2, w_gu, gh, 0, half, (hidden, dgu))
    dn2_near = dot_nt(dgu[:half], w_gu).astype(BF16)
    grad_n2 = reduce4(dn2_near, dn2_far)

    ffn_far = dot_nt(hidden[half:], w_down_t).astype(BF16)
    ffn_near = dot_nt(hidden[:half], w_down_t).astype(BF16)
    output = (residual + reduce4(ffn_near, ffn_far)).astype(BF16)

    grad_w_gu = dot_tn(n2, dgu).astype(BF16)
    grad_w_down_t = dot_tn(go_all, hidden).astype(BF16)

    weighted = grad_n2 * gain_two_row
    inner = jnp.mean(residual * weighted, axis=-1, keepdims=True)
    grad_residual = grad_output + scale_two * weighted - residual * (scale_two**3 * inner)
    gain_two = jnp.sum(grad_n2 * residual * scale_two, axis=0)

    ga = jnp.concatenate(gather4(grad_residual.astype(BF16)))
    grad_mixed = (dot(ga, w_out_t) * valid[:, None]).astype(BF16)
    dq, dkv = attention_backward(t1, q, grad_mixed, mixed, lse, k, v, pos3, cos, sin)
    dqkv = jnp.concatenate([dq, dkv], axis=1)
    w_qkv = w_a[:, :kv_at]
    dn_far = dot_nt(dqkv[half:], w_qkv).astype(BF16)
    dn_near = dot_nt(dqkv[:half], w_qkv).astype(BF16)
    grad_normed = reduce4(dn_near, dn_far)
    grad_w_out_t = dot_tn(ga, mixed).astype(BF16)
    grad_w_qkv = dot_tn(normed, dqkv).astype(BF16)

    scale_one = lax.rsqrt(jnp.mean(x_rows * x_rows, axis=-1, keepdims=True) + EPS)
    weighted = grad_normed * gain_one_row
    inner = jnp.mean(x_rows * weighted, axis=-1, keepdims=True)
    grad_tokens = grad_residual + scale_one * weighted - x_rows * (scale_one**3 * inner)
    gain_one = jnp.sum(grad_normed * x_rows * scale_one, axis=0)

    gu_shard = dp_scatter(grad_w_gu, n_dp)
    down_shard = dp_scatter(grad_w_down_t, n_dp, True)
    out_shard = dp_scatter(grad_w_out_t, n_dp, True)
    qkv_shard = dp_scatter(grad_w_qkv, n_dp)
    gain_cols = jnp.pad(jnp.stack([gain_one, gain_two], axis=1), ((0, 0), (0, HEAD - 2)))
    gain_shard = dp_scatter(gain_cols.astype(BF16), n_dp)
    small = jnp.concatenate([qkv_shard[:, q_cols:], gain_shard], axis=1)
    small = small + core(small)
    small = small + across(small)

    return (
        output,
        grad_tokens,
        qkv_shard[:, :q_cols],
        small[:, : 2 * HEAD],
        out_shard.T,
        gu_shard[:, :units],
        gu_shard[:, units:],
        down_shard.T,
        small[:, 2 * HEAD : 2 * HEAD + 2].T,
    )


def solution(mesh):
    return jax.shard_map(
        functools.partial(per_device, mesh.shape["dp"]),
        mesh=mesh,
        in_specs=(
            P(("dp", "tensor"), None),
            P("dp", "tensor"),
            P("dp", None),
            P("tensor", "dp"),
            P("dp", "tensor"),
            P("dp", "tensor"),
            P("tensor", "dp"),
            P(None, "dp"),
            P("dp"),
            P(("dp", "tensor"), None),
        ),
        out_specs=(
            P(("dp", "tensor"), None),
            P(("dp", "tensor"), None),
            P("dp", "tensor"),
            P("dp", None),
            P("tensor", "dp"),
            P("dp", "tensor"),
            P("dp", "tensor"),
            P("tensor", "dp"),
            P(None, "dp"),
        ),
        check_vma=False,
    )
```

```python
import functools

import jax
import jax.numpy as jnp
from jax import lax
from jax.experimental import pallas as pl
from jax.experimental.pallas import tpu as pltpu
from jax.sharding import PartitionSpec as P

WINDOW = 1024
EPS = 1e-6
MASKED = -1e30
HEAD = 128
BLK = 256
LOG2E = 1.4426950408889634
F32 = jnp.float32
BF16 = jnp.bfloat16
MIB = 1 << 20

NT = (((1,), (1,)), ((), ()))
TN = (((0,), (0,)), ((), ()))


def dot(left, right):
    return jnp.dot(left, right, preferred_element_type=F32)


def dot_nt(left, right):
    return lax.dot_general(left, right, NT, preferred_element_type=F32)


def dot_tn(left, right):
    return lax.dot_general(left, right, TN, preferred_element_type=F32)


def stacked(block, heads):
    return jnp.concatenate([block[:, h * HEAD : (h + 1) * HEAD] for h in range(heads)], axis=0)


def partner(t, j):
    rem, div = lax.rem, lax.div
    two = jnp.int32(2)
    j = jnp.int32(j)
    return rem(div(t, two) + div(j, two), two) * 2 + rem(rem(t, two) + rem(j, two), two)


def block_rows(i):
    return pl.ds(pl.multiple_of(i * BLK, BLK), BLK)


def key_row(t, kb):
    per = 512 // BLK
    return pl.multiple_of((partner(t, lax.div(kb, per)) * per + lax.rem(kb, per)) * BLK, BLK)


def query_block(t, i):
    per = 512 // BLK
    i = jnp.int32(i)
    return partner(t, lax.div(i, per)) * per + lax.rem(i, per)


def tiled3(row, heads):
    return jnp.concatenate([row] * heads, axis=1)


def attend(t, i, q, k, v, pos, valid, mixed, lse):
    cols = q.shape[1]
    heads = cols // HEAD
    wide = heads * BLK
    qb = query_block(t, i)
    mine = pl.ds(pl.multiple_of(i * BLK, BLK), BLK)
    q3 = stacked(q[mine, :], heads)
    at = qb * BLK + lax.broadcasted_iota(jnp.int32, (1, BLK), 1)
    low = at - jnp.minimum(pos[i], WINDOW - 1)
    at3, low3 = tiled3(at, heads), tiled3(low, heads)
    factor = HEAD**-0.5 * LOG2E

    def step(kb, carry):
        peak, total, acc = carry
        row = key_row(t, kb)
        s = dot_nt(k[pl.ds(row, BLK), :], q3) * factor
        u = kb * BLK + lax.broadcasted_iota(jnp.int32, (BLK, wide), 0)
        s = jnp.where((u <= at3) & (u >= low3), s, MASKED)
        new_peak = jnp.maximum(peak, jnp.max(s, axis=0, keepdims=True))
        p = jnp.exp2(s - new_peak)
        shrink = jnp.exp2(peak - new_peak)
        total = total * shrink + jnp.sum(p, axis=0, keepdims=True)
        acc = acc * shrink + dot_tn(v[pl.ds(row, BLK), :], p.astype(BF16))
        return new_peak, total, acc

    peak, total, acc = lax.fori_loop(
        jnp.maximum(qb - WINDOW // BLK, 0),
        qb + 1,
        step,
        (
            jnp.full((1, wide), MASKED, F32),
            jnp.zeros((1, wide), F32),
            jnp.zeros((HEAD, wide), F32),
        ),
    )
    lse[i] = peak + jnp.log2(total)
    acc = acc * (tiled3(valid[i], heads) / total)
    mixed[mine, :] = jnp.concatenate(
        [acc[:, h * BLK : (h + 1) * BLK].T for h in range(heads)], axis=1
    ).astype(BF16)


def ring_device(p, n):
    p = lax.rem(p + n, jnp.int32(n))
    down = lax.div(p, jnp.int32(n // 2))
    return (1 - down) * 2 * p + down * (2 * (n - 1 - p) + 1)


def ring_place(d, n):
    z, y = lax.div(d, jnp.int32(2)), lax.rem(d, jnp.int32(2))
    return z + y * (n - 1 - 2 * z)


def send(src, dst, sems, at, device):
    return pltpu.make_async_remote_copy(
        src_ref=src,
        dst_ref=dst,
        send_sem=sems.at[0, at],
        recv_sem=sems.at[1, at],
        device_id=device,
        device_id_type=pl.DeviceIdType.MESH,
    )


class Ring:
    def __init__(self, shard, full, sems, first_sem, own, n, direction):
        self.shard, self.full, self.sems, self.at, self.own = shard, full, sems, first_sem, own
        self.n, self.dir = n, direction
        self.copies = {}

    def block(self, offset, place):
        rows = self.shard.shape[0]
        at = ring_device(place + offset * self.dir, self.n) * rows
        return self.full.at[pl.ds(pl.multiple_of(at, rows & -rows), rows), :]

    def begin(self, place):
        self.place = place
        if self.n == 8:
            target = self.block(0, place)
        else:
            target = self.full
        self.local = pltpu.make_async_copy(self.shard, target, self.own)
        self.local.start()
        self.start(1)

    def start(self, s):
        if self.n != 8:
            return
        for way in (0, 1):
            if s > self.n // 2 - way:
                continue
            sign = 1 - 2 * way
            block = self.block(-sign * (s - 1), self.place)
            device = ring_device(self.place + sign * self.dir, self.n)
            src = self.shard if s == 1 else block
            at = self.at + 2 * (s - 1) + way
            copy = send(src, block, self.sems, at, {"dp": device})
            copy.start()
            self.copies[s, way] = copy

    def arrived(self, s):
        for way in (0, 1):
            if (s, way) in self.copies:
                self.copies[s, way].wait_recv()

    def next(self, s):
        self.arrived(s)
        self.start(s + 1)

    def end(self):
        for copy in self.copies.values():
            copy.wait_send()
        self.local.wait()


class RingSum:
    def __init__(self, full, recv, stage, sems, first_sem, loads, n, direction, place):
        self.full, self.recv, self.stage, self.sems, self.at = full, recv, stage, sems, first_sem
        self.loads, self.n, self.dir, self.place = loads, n, direction, place
        self.rows = full.shape[0] // n
        self.copies = {}

    def block(self, offset):
        at = ring_device(self.place + offset * self.dir, self.n) * self.rows
        return pl.ds(pl.multiple_of(at, self.rows & -self.rows), self.rows)

    def last(self, way):
        return self.n // 2 - way

    def copy(self, s, way):
        far = self.last(way)
        sign = 1 - 2 * way
        device = ring_device(self.place + sign * self.dir, self.n)
        slot = way * 4 + s - 1
        src = self.full.at[self.block(sign * (far + 1 - s)), :]
        return send(src, self.recv.at[slot], self.sems, self.at + slot, {"dp": device})

    def start(self, s, ways=(0, 1)):
        for way in ways:
            if self.n == 8 and s <= self.last(way):
                self.copies[s, way] = self.copy(s, way)
                self.copies[s, way].start()

    def arrived(self, s, way):
        slot = way * 4 + s - 1
        if (s, way) in self.copies:
            self.copies[s, way].wait_recv()
        else:
            self.copy(s, way).wait_recv()
        if self.stage is None:
            return self.recv[slot]
        cols = self.full.shape[1]
        load = pltpu.make_async_copy(
            self.recv.at[slot], self.stage.at[:, :cols], self.loads.at[self.at + slot]
        )
        load.start()
        load.wait()
        return self.stage[:, :cols]

    def add(self, s, start=False):
        for way in (0, 1):
            if self.n == 8 and s < self.last(way):
                far = self.last(way)
                mine = self.block((1 - 2 * way) * (far - s))
                self.full[mine, :] = self.full[mine, :] + self.arrived(s, way)
                if start:
                    self.start(s + 1, (way,))

    def next(self, s):
        self.add(s, True)

    def result(self):
        acc = self.full[self.block(0), :].astype(F32)
        for way in (0, 1):
            acc = acc + self.arrived(self.last(way), way).astype(F32)
        return acc

    def end(self):
        for copy in self.copies.values():
            copy.wait_send()


def front_kernel(
    n_dp,
    tokens,
    grad_output,
    shard_a,
    shard_d,
    shard_g,
    pos,
    valid,
    cos,
    sin,
    w_a_out,
    w_d_out,
    w_g,
    gains,
    normed_out,
    q_out,
    k_out,
    v_out,
    mixed_out,
    lse,
    residual_out,
    n2_out,
    go_out,
    gh_out,
    w_a,
    w_d,
    x4,
    normed,
    q,
    k,
    v,
    mixed,
    near_recv,
    far_recv,
    x_recv,
    sum_buf,
    n2_own,
    go_buf,
    gh_buf,
    res,
    ring_sems,
    pair_sems,
    local_sems,
):
    quarter, width = tokens.shape
    q_cols = q.shape[1]
    heads = q_cols // HEAD
    kv_at = q_cols + 2 * HEAD
    gain_at = kv_at + q_cols
    t = lax.axis_index("tensor").astype(jnp.int32)
    place = ring_place(lax.axis_index("dp").astype(jnp.int32), n_dp)
    near_id, far_id = {"tensor": partner(t, 1)}, {"tensor": partner(t, 2)}

    barrier = pltpu.get_barrier_semaphore()
    partners = [near_id, far_id]
    if n_dp == 8:
        partners += [{"dp": ring_device(place + 1, n_dp)}, {"dp": ring_device(place - 1, n_dp)}]
    for device in partners:
        pl.semaphore_signal(barrier, inc=1, device_id=device, device_id_type=pl.DeviceIdType.MESH)
    pl.semaphore_wait(barrier, len(partners))

    def rows_of(ref, j, size=1):
        return ref.at[pl.ds(j * quarter, size * quarter), :]

    used = [0]

    def local(src, dst):
        copy = pltpu.make_async_copy(src, dst, local_sems.at[used[0]])
        used[0] += 1
        copy.start()
        return copy

    ring_a = Ring(shard_a, w_a, ring_sems, 0, local_sems.at[24], n_dp, 1)
    ring_d = Ring(shard_d, w_d, ring_sems, 8, local_sems.at[25], n_dp, 1)
    ring_g = Ring(shard_g, w_g, ring_sems, 16, local_sems.at[26], n_dp, -1)

    ring_a.begin(place)
    x_far = send(tokens, rows_of(x4, 2), pair_sems, 0, far_id)
    x_far.start()
    x_near = send(tokens, rows_of(x4, 1), pair_sems, 1, near_id)
    x_near.start()
    x_own = local(tokens, rows_of(x4, 0))
    go_in = local(grad_output, res)
    for s in (1, 2, 3):
        ring_a.next(s)
    ring_d.begin(place)
    ring_g.begin(place)
    ring_a.arrived(4)
    ring_a.local.wait()

    gain_rows = w_a[:, gain_at : gain_at + HEAD].astype(F32).T
    gains[...] = gain_rows[:8]

    def project(i, carry):
        mine = pl.ds(pl.multiple_of(i * BLK, BLK), BLK)
        rows = x4[mine, :].astype(F32)
        scale = lax.rsqrt(jnp.mean(rows * rows, axis=-1, keepdims=True) + EPS)
        n = (rows * scale * gains[0:1, :]).astype(BF16)
        normed[mine, :] = n
        y = dot(n, w_a[:, :kv_at])
        c, s = cos[mine, :], sin[mine, :]

        def turned(a):
            return (a * c + pltpu.roll(a, HEAD // 2, 1) * s).astype(BF16)

        q[mine, :] = jnp.concatenate(
            [turned(y[:, h * HEAD : (h + 1) * HEAD]) for h in range(heads)], axis=1
        )
        k[mine, :] = turned(y[:, q_cols : q_cols + HEAD])
        v[mine, :] = y[:, q_cols + HEAD : kv_at].astype(BF16)
        return carry

    per = quarter // BLK
    x_own.wait()
    x_near.wait_recv()
    lax.fori_loop(0, 2 * per, project, 0)
    x_far.wait_recv()
    x_last = send(rows_of(x4, 2), rows_of(x4, 3), pair_sems, 2, near_id)
    x_last.start()
    go_in.wait()
    go_buf[...] = res[...].astype(BF16)
    go_far = send(go_buf, rows_of(go_out, 2), pair_sems, 3, far_id)
    go_far.start()
    go_near = send(go_buf, rows_of(go_out, 1), pair_sems, 4, near_id)
    go_near.start()
    go_own = local(go_buf, rows_of(go_out, 0))
    x_last.wait_recv()
    lax.fori_loop(2 * per, 4 * per, project, 0)
    copies = [
        local(normed, normed_out),
        local(q, q_out),
        local(k, k_out),
        local(v, v_out),
        local(w_a, w_a_out),
    ]

    def attention(i, carry):
        attend(t, i, q, k, v, pos, valid, mixed, lse)
        return carry

    part = x4

    def out_product(i, carry):
        mine = pl.ds(pl.multiple_of(i * BLK, BLK), BLK)
        part[mine, :] = dot_nt(mixed[mine, :], w_a[:, kv_at:gain_at]).astype(BF16)
        return carry

    x_last.wait_send()
    lax.fori_loop(2 * per, 4 * per, attention, 0)
    ring_d.next(1)
    lax.fori_loop(2 * per, 4 * per, out_product, 0)
    part_far = send(rows_of(part, 3), far_recv, pair_sems, 5, near_id)
    part_far.start()
    lax.fori_loop(0, 1, attention, 0)
    part_far.wait_recv()
    sum_buf[...] = (part[pl.ds(2 * quarter, quarter), :].astype(F32) + far_recv[...].astype(F32)).astype(BF16)
    sum_far = send(sum_buf, x_recv, pair_sems, 6, far_id)
    sum_far.start()
    ring_g.next(1)
    lax.fori_loop(1, 2 * per, attention, 0)
    lax.fori_loop(0, 2 * per, out_product, 0)
    part_near = send(rows_of(part, 1), near_recv, pair_sems, 7, near_id)
    part_near.start()
    copies.append(local(mixed, mixed_out))
    ring_d.next(2)
    ring_d.next(3)
    ring_g.next(2)
    go_far.wait_recv()
    go_last = send(rows_of(go_out, 2), rows_of(go_out, 3), pair_sems, 8, near_id)
    go_last.start()
    part_near.wait_recv()
    sum_far.wait_recv()

    res[...] = (
        tokens[...].astype(F32)
        + part[pl.ds(0, quarter), :].astype(F32)
        + near_recv[...].astype(F32)
        + x_recv[...].astype(F32)
    )
    scale_two = lax.rsqrt(jnp.mean(res[...] * res[...], axis=-1, keepdims=True) + EPS)
    n2_own[...] = (res[...] * scale_two * gains[1:2, :]).astype(BF16)
    n2_far = send(n2_own, rows_of(n2_out, 2), pair_sems, 9, far_id)
    n2_far.start()
    n2_near = send(n2_own, rows_of(n2_out, 1), pair_sems, 10, near_id)
    n2_near.start()
    copies.append(local(n2_own, rows_of(n2_out, 0)))
    copies.append(local(res, residual_out))

    ring_d.arrived(4)
    ring_d.local.wait()
    copies.append(local(w_d, w_d_out))
    go_far.wait_send()
    go_near.wait_send()
    go_own.wait()

    def grad_hidden(i, carry):
        mine = pl.ds(pl.multiple_of(i * BLK, BLK), BLK)
        gh_buf[mine, :] = dot(go_buf[mine, :], w_d[...]).astype(BF16)
        return carry

    for j in range(4):
        if j == 1:
            go_near.wait_recv()
        if j == 3:
            go_last.wait_recv()
        if j > 0:
            load = local(rows_of(go_out, j), go_buf)
            load.wait()
        if j > 0:
            store.wait()
        lax.fori_loop(0, per, grad_hidden, 0)
        store = local(gh_buf, rows_of(gh_out, j))
        if j == 1:
            ring_g.next(3)

    n2_far.wait_recv()
    n2_last = send(rows_of(n2_out, 2), rows_of(n2_out, 3), pair_sems, 11, near_id)
    n2_last.start()
    ring_g.arrived(4)
    store.wait()
    for copy in copies:
        copy.wait()
    for copy in (x_far, x_near, part_far, sum_far, part_near, go_last, n2_far, n2_near, n2_last):
        copy.wait_send()
    n2_near.wait_recv()
    n2_last.wait_recv()
    ring_a.copies and [c.wait_send() for c in ring_a.copies.values()]
    ring_d.copies and [c.wait_send() for c in ring_d.copies.values()]
    ring_g.end()


def front(n_dp, tokens, grad_output, shard_a, shard_d, shard_g, pos, valid, cos, sin, q_cols):
    quarter, width = tokens.shape
    length = 4 * quarter
    heads = q_cols // HEAD
    units = shard_d.shape[1]
    cols_a = shard_a.shape[1]
    vmem = pl.BlockSpec(memory_space=pltpu.VMEM)
    hbm = pl.BlockSpec(memory_space=pl.ANY)
    blocks = length // BLK

    def out(rows, cols, kind=BF16):
        return jax.ShapeDtypeStruct((rows, cols), kind)

    return pl.pallas_call(
        functools.partial(front_kernel, n_dp),
        in_specs=[vmem, hbm, hbm, hbm, hbm, vmem, vmem, vmem, vmem],
        out_specs=[hbm, hbm, hbm, vmem, hbm, hbm, hbm, hbm, hbm, vmem, hbm, hbm, hbm, hbm],
        out_shape=[
            out(width, cols_a),
            out(width, units),
            out(width, 2 * units),
            out(8, width, F32),
            out(length, width),
            out(length, q_cols),
            out(length, HEAD),
            out(length, HEAD),
            out(length, q_cols),
            jax.ShapeDtypeStruct((blocks, 1, heads * BLK), F32),
            out(quarter, width, F32),
            out(length, width),
            out(length, width),
            out(length, units),
        ],
        scratch_shapes=[
            pltpu.VMEM((width, cols_a), BF16),
            pltpu.VMEM((width, units), BF16),
            pltpu.VMEM((length, width), BF16),
            pltpu.VMEM((length, width), BF16),
            pltpu.VMEM((length, q_cols), BF16),
            pltpu.VMEM((length, HEAD), BF16),
            pltpu.VMEM((length, HEAD), BF16),
            pltpu.VMEM((length, q_cols), BF16),
            pltpu.VMEM((quarter, width), BF16),
            pltpu.VMEM((quarter, width), BF16),
            pltpu.VMEM((quarter, width), BF16),
            pltpu.VMEM((quarter, width), BF16),
            pltpu.VMEM((quarter, width), BF16),
            pltpu.VMEM((quarter, width), BF16),
            pltpu.VMEM((quarter, units), BF16),
            pltpu.VMEM((quarter, width), F32),
            pltpu.SemaphoreType.DMA((2, 24)),
            pltpu.SemaphoreType.DMA((2, 12)),
            pltpu.SemaphoreType.DMA((32,)),
        ],
        compiler_params=pltpu.CompilerParams(
            collective_id=0, has_side_effects=True, vmem_limit_bytes=58 * MIB
        ),
        cost_estimate=pl.CostEstimate(
            flops=12 * length * width * q_cols, bytes_accessed=64 * MIB, transcendentals=0
        ),
        name="front",
    )(tokens, grad_output, shard_a, shard_d, shard_g, pos, valid, cos, sin)


def attend_back(t, i, q, do, mixed, lse, k, v, pos, valid, cos, sin, dqkv, dk_acc, dv_acc):
    cols = q.shape[1]
    heads = cols // HEAD
    wide = heads * BLK
    qb = query_block(t, i)
    mine = block_rows(i)
    q3 = stacked(q[mine, :], heads)
    do3 = stacked(do[mine, :], heads)
    centre3 = do3.astype(F32) * stacked(mixed[mine, :], heads).astype(F32)
    centre = jnp.sum(centre3.T, axis=0, keepdims=True)
    at = qb * BLK + lax.broadcasted_iota(jnp.int32, (1, BLK), 1)
    low = jnp.where(valid[i] > 0.0, at - jnp.minimum(pos[i], WINDOW - 1), at + 1)
    at3, low3 = tiled3(at, heads), tiled3(low, heads)
    total = lse[i]
    factor = HEAD**-0.5 * LOG2E

    def step(kb, acc):
        row = key_row(t, kb)
        kblk = k[pl.ds(row, BLK), :]
        vblk = v[pl.ds(row, BLK), :]
        s = dot_nt(kblk, q3) * factor - total
        u = kb * BLK + lax.broadcasted_iota(jnp.int32, (BLK, wide), 0)
        p = jnp.exp2(jnp.where((u <= at3) & (u >= low3), s, MASKED))
        gp = dot_nt(vblk, do3)
        ds = (p * (gp - centre)).astype(BF16)
        dv_acc[pl.ds(row, BLK), :] += dot(p.astype(BF16), do3)
        dk_acc[pl.ds(row, BLK), :] += dot(ds, q3)
        return acc + dot_tn(kblk, ds)

    acc = lax.fori_loop(
        jnp.maximum(qb - WINDOW // BLK, 0), qb + 1, step, jnp.zeros((HEAD, wide), F32)
    )
    scale = HEAD**-0.5
    c, sn = cos[mine, :] * scale, sin[mine, :] * scale

    def turned(a):
        return (a * c - pltpu.roll(a, HEAD // 2, 1) * sn).astype(BF16)

    dqkv[mine, :cols] = jnp.concatenate(
        [turned(acc[:, h * BLK : (h + 1) * BLK].T) for h in range(heads)], axis=1
    )


def gated(y, gh, half):
    gate, up = y[:, :half], y[:, half:]
    root = (2.0 / jnp.pi) ** 0.5
    square = gate * gate
    th = jnp.tanh(root * gate * (1.0 + 0.044715 * square))
    one = 0.5 * (1.0 + th)
    act = gate * one
    slope = one + 0.5 * gate * (1.0 - th * th) * (root * (1.0 + 3.0 * 0.044715 * square))
    return (act * up).astype(BF16), (gh * up * slope).astype(BF16), (gh * act).astype(BF16)


def greet(partners):
    barrier = pltpu.get_barrier_semaphore()
    for device in partners:
        pl.semaphore_signal(barrier, inc=1, device_id=device, device_id_type=pl.DeviceIdType.MESH)
    pl.semaphore_wait(barrier, len(partners))


def neighbours(n_dp, t, place):
    near_id, far_id = {"tensor": partner(t, 1)}, {"tensor": partner(t, 2)}
    others = []
    if n_dp == 8:
        others = [{"dp": ring_device(place + 1, n_dp)}, {"dp": ring_device(place - 1, n_dp)}]
    return near_id, far_id, [near_id, far_id] + others


class Local:
    def __init__(self, sems):
        self.sems, self.used = sems, 0

    def __call__(self, src, dst):
        copy = pltpu.make_async_copy(src, dst, self.sems.at[self.used])
        self.used += 1
        copy.start()
        return copy


def middle_kernel(
    n_dp,
    n2_in,
    gh_in,
    go_in,
    w_gu_in,
    w_d_in,
    residual,
    grad_output,
    gains,
    grads_gu_out,
    down_out,
    grad_residual,
    gain_two,
    ga_out,
    ffn_sum_out,
    out_part,
    far_recv,
    x_recv,
    near_recv,
    far_recv2,
    near_recv2,
    recv_d,
    recv_g,
    w_gu,
    n2,
    go,
    hidden,
    dgu,
    part,
    grads_d,
    grads_gu,
    stage,
    sum_buf,
    ga_own,
    ring_stage,
    rows_a,
    rows_b,
    down_f32,
    ring_sems,
    pair_sems,
    load_sems,
    local_sems,
):
    length, width = n2.shape
    units = hidden.shape[1]
    quarter = length // 4
    half = length // 2
    t = lax.axis_index("tensor").astype(jnp.int32)
    place = ring_place(lax.axis_index("dp").astype(jnp.int32), n_dp)
    near_id, far_id, partners = neighbours(n_dp, t, place)
    local = Local(local_sems)
    ring_d = RingSum(grads_d, recv_d, ring_stage, ring_sems, 0, load_sems, n_dp, -1, place)
    ring_g = RingSum(grads_gu, recv_g, ring_stage, ring_sems, 8, load_sems, n_dp, 1, place)

    far_rows, near_rows = pl.ds(half, half), pl.ds(0, half)
    load_w = local(w_gu_in, w_gu)
    load_far = [local(n2_in.at[far_rows, :], n2.at[far_rows, :]), local(gh_in.at[far_rows, :], hidden.at[far_rows, :])]
    load_near = [local(n2_in.at[near_rows, :], n2.at[near_rows, :]), local(gh_in.at[near_rows, :], hidden.at[near_rows, :])]
    greet(partners)

    def ffn(i, carry):
        mine = block_rows(i)
        y = dot(n2[mine, :], w_gu[...])
        gh = hidden[mine, :].astype(F32)
        hidden[mine, :], dgu[mine, :units], dgu[mine, units:] = gated(y, gh, units)
        return carry

    def back(first):
        def body(i, carry):
            part[block_rows(i), :] = dot_nt(dgu[block_rows(i + first), :], w_gu[...]).astype(BF16)
            return carry

        return body

    def fetch(src, dst):
        local(src, dst).wait()

    upper = pl.ds(quarter, quarter)
    per = half // BLK
    load_w.wait()
    for copy in load_far:
        copy.wait()
    lax.fori_loop(per, 2 * per, ffn, 0)
    lax.fori_loop(0, per, back(per), 0)
    part_far = send(part.at[upper, :], far_recv, pair_sems, 0, near_id)
    part_far.start()
    for copy in load_near:
        copy.wait()
    lax.fori_loop(0, 1, ffn, 0)
    part_far.wait_recv()
    fetch(far_recv, stage)
    sum_buf[...] = (part[:quarter, :].astype(F32) + stage[...].astype(F32)).astype(BF16)
    sum_far = send(sum_buf, x_recv, pair_sems, 1, far_id)
    sum_far.start()
    blocks = width // BLK

    def load_go(i):
        return local(go_in.at[:, pl.ds(i * BLK, BLK)], go.at[i % 2])

    coming = load_go(0)
    lax.fori_loop(1, per, ffn, 0)

    for i in range(blocks):
        coming.wait()
        if i + 1 < blocks:
            coming = load_go(i + 1)
        grads_d[i * BLK : (i + 1) * BLK, :] = dot_tn(go[i % 2], hidden[...]).astype(BF16)
    ring_d.start(1)

    def gu_grad(i, carry):
        grads_gu[block_rows(i), :] = dot_tn(n2[:, block_rows(i)], dgu[...]).astype(BF16)
        return carry

    lax.fori_loop(0, blocks * 2 // 3, gu_grad, 0)
    ring_d.next(1)
    lax.fori_loop(blocks * 2 // 3, blocks, gu_grad, 0)
    ring_g.start(1)
    part_far.wait_send()
    lax.fori_loop(0, per, back(0), 0)
    part_near = send(part.at[upper, :], near_recv, pair_sems, 2, near_id)
    part_near.start()
    load_d = local(w_d_in, w_gu.at[:, :units])
    ring_d.next(2)

    gain_two[...] = jnp.zeros_like(gain_two)
    sum_far.wait_send()
    sum_far.wait_recv()
    fetch(x_recv, sum_buf)
    part_near.wait_recv()
    fetch(near_recv, stage)
    stores = []
    size = rows_a.shape[1]
    steps = quarter // size

    def rows_at(i):
        return pl.ds(i * size, size)

    def load_rows(i):
        return (
            local(residual.at[rows_at(i), :], rows_a.at[i % 2]),
            local(grad_output.at[rows_at(i), :], rows_b.at[i % 2]),
        )

    coming = load_rows(0)
    for i in range(steps):
        for copy in coming:
            copy.wait()
        if i + 1 < steps:
            if i > 0:
                stores[-1].wait()
            coming = load_rows(i + 1)
        mine = slice(i * size, (i + 1) * size)
        rows = rows_a[i % 2]
        grad_n = part[mine, :].astype(F32) + stage[mine, :].astype(F32) + sum_buf[mine, :].astype(F32)
        scale = lax.rsqrt(jnp.mean(rows * rows, axis=-1, keepdims=True) + EPS)
        weighted = grad_n * gains[1:2, :]
        inner = jnp.mean(rows * weighted, axis=-1, keepdims=True)
        grad = rows_b[i % 2] + scale * weighted - rows * (scale * scale * scale * inner)
        rows_b[i % 2] = grad
        ga_own[mine, :] = grad.astype(BF16)
        gain_two[0:1, :] += jnp.sum(grad_n * rows * scale, axis=0, keepdims=True)
        stores.append(local(rows_b.at[i % 2], grad_residual.at[rows_at(i), :]))

    def quarter_of(ref, j):
        return ref.at[pl.ds(j * quarter, quarter), :]

    ga_far = send(ga_own, quarter_of(ga_out, 2), pair_sems, 3, far_id)
    ga_far.start()
    ga_near = send(ga_own, quarter_of(ga_out, 1), pair_sems, 4, near_id)
    ga_near.start()
    stores_late = [local(ga_own, quarter_of(ga_out, 0))]
    part_near.wait_send()
    load_d.wait()

    def down_product(first):
        def body(i, carry):
            part[block_rows(i), :] = dot_nt(hidden[block_rows(i + first), :], w_gu[:, :units]).astype(BF16)
            return carry

        return body

    lax.fori_loop(0, per, down_product(per), 0)
    part_far2 = send(part.at[upper, :], far_recv2, pair_sems, 5, near_id)
    part_far2.start()
    ring_d.next(3)
    ring_g.next(1)
    part_far2.wait_recv()
    fetch(far_recv2, stage)
    sum_buf[...] = (part[:quarter, :].astype(F32) + stage[...].astype(F32)).astype(BF16)
    stores_late.append(local(sum_buf, ffn_sum_out))
    part_far2.wait_send()
    lax.fori_loop(0, per, down_product(0), 0)
    part_near2 = send(part.at[upper, :], near_recv2, pair_sems, 6, near_id)
    part_near2.start()
    part_near2.wait_recv()
    fetch(near_recv2, stage)
    for copy in stores[-2:]:
        copy.wait()
    stores = []
    coming = local(residual.at[rows_at(0), :], rows_a.at[0])
    for i in range(steps):
        coming.wait()
        if i + 1 < steps:
            if i > 0:
                stores[-1].wait()
            coming = local(residual.at[rows_at(i + 1), :], rows_a.at[(i + 1) % 2])
        mine = slice(i * size, (i + 1) * size)
        rows_a[i % 2] = rows_a[i % 2] + part[mine, :].astype(F32) + stage[mine, :].astype(F32)
        stores.append(local(rows_a.at[i % 2], out_part.at[rows_at(i), :]))
    stores_late += stores[-2:]

    if n_dp == 8:
        down_f32[...] = ring_d.result()
        stores_late.append(local(down_f32, down_out))
    else:
        stores_late.append(local(grads_d, down_out))
    ga_far.wait_recv()
    ga_last = send(quarter_of(ga_out, 2), quarter_of(ga_out, 3), pair_sems, 7, near_id)
    ga_last.start()
    ring_g.add(2)
    ring_d.end()
    ring_g.end()
    stores_late.append(local(grads_gu, grads_gu_out))
    ga_near.wait_recv()
    ga_last.wait_recv()
    for copy in stores_late:
        copy.wait()
    for copy in (ga_far, ga_near, ga_last, part_near2):
        copy.wait_send()


def middle(n_dp, n2, gh, go, w_gu, w_d, residual, grad_output, gains):
    length, width = n2.shape
    units = gh.shape[1]
    quarter = length // 4
    rows = width // 8
    vmem = pl.BlockSpec(memory_space=pltpu.VMEM)
    hbm = pl.BlockSpec(memory_space=pl.ANY)
    shape = jax.ShapeDtypeStruct
    pair = shape((quarter, width), BF16)
    return pl.pallas_call(
        functools.partial(middle_kernel, n_dp),
        in_specs=[hbm] * 7 + [vmem],
        out_specs=[hbm] * 3 + [vmem] + [hbm] * 10,
        out_shape=[
            shape((width, 2 * units), BF16),
            shape((rows, units), F32) if n_dp == 8 else shape((width, units), BF16),
            shape((quarter, width), F32),
            shape((8, width), F32),
            shape((length, width), BF16),
            pair,
            shape((quarter, width), F32),
            pair,
            pair,
            pair,
            pair,
            pair,
            shape((8, rows, units), BF16),
            shape((8, rows, 2 * units), BF16),
        ],
        scratch_shapes=[
            pltpu.VMEM((width, 2 * units), BF16),
            pltpu.VMEM((length, width), BF16),
            pltpu.VMEM((2, length, BLK), BF16),
            pltpu.VMEM((length, units), BF16),
            pltpu.VMEM((length, 2 * units), BF16),
            pltpu.VMEM((length // 2, width), BF16),
            pltpu.VMEM((width, units), BF16),
            pltpu.VMEM((width, 2 * units), BF16),
            pltpu.VMEM((quarter, width), BF16),
            pltpu.VMEM((quarter, width), BF16),
            pltpu.VMEM((quarter, width), BF16),
            pltpu.VMEM((rows, 2 * units), BF16),
            pltpu.VMEM((2, 64, width), F32),
            pltpu.VMEM((2, 64, width), F32),
            pltpu.VMEM((rows, units), F32),
            pltpu.SemaphoreType.DMA((2, 16)),
            pltpu.SemaphoreType.DMA((2, 8)),
            pltpu.SemaphoreType.DMA((16,)),
            pltpu.SemaphoreType.DMA((72,)),
        ],
        compiler_params=pltpu.CompilerParams(
            collective_id=1, has_side_effects=True, vmem_limit_bytes=63 * MIB
        ),
        cost_estimate=pl.CostEstimate(
            flops=14 * length * width * units, bytes_accessed=64 * MIB, transcendentals=0
        ),
        name="middle",
    )(n2, gh, go, w_gu, w_d, residual, grad_output, gains)[:7]


def back_kernel(
    n_dp,
    grad_residual,
    ga_in,
    grads_gu_in,
    ffn_sum,
    out_part,
    tokens,
    w_a_in,
    q_in,
    k_in,
    v_in,
    mixed_in,
    normed_in,
    lse,
    pos,
    valid,
    cos,
    sin,
    gains,
    gain_two,
    output,
    grad_tokens,
    gate_out,
    up_out,
    grads_a_out,
    gain_out,
    far_recv,
    x_recv,
    near_recv,
    x_recv2,
    recv_g,
    recv_q,
    acts,
    w_a,
    q,
    k,
    v,
    mixed,
    do,
    dqkv,
    dk_acc,
    dv_acc,
    grads_a,
    grads_gu,
    part,
    stage,
    sum_buf,
    ring_stage,
    result_gu,
    result_a,
    rows_a,
    rows_b,
    out_rows,
    gain_acc,
    gain_cols,
    recv_s,
    small,
    small_near,
    small_far,
    ring_sems,
    pair_sems,
    load_sems,
    local_sems,
):
    length, width = acts.shape
    quarter = length // 4
    half = length // 2
    q_cols = q.shape[1]
    kv_at = q_cols + 2 * HEAD
    out_at = kv_at + q_cols
    units = grads_gu.shape[1] // 2
    ring = n_dp == 8
    t = lax.axis_index("tensor").astype(jnp.int32)
    place = ring_place(lax.axis_index("dp").astype(jnp.int32), n_dp)
    near_id, far_id, partners = neighbours(n_dp, t, place)
    local = Local(local_sems)
    ring_g = RingSum(grads_gu, recv_g, ring_stage, ring_sems, 0, load_sems, n_dp, 1, place)
    ring_a = RingSum(grads_a, recv_q, ring_stage, ring_sems, 8, load_sems, n_dp, -1, place)
    ring_s = RingSum(gain_cols, recv_s, None, ring_sems, 16, load_sems, n_dp, 1, place)

    if ring:
        load_g = local(grads_gu_in, grads_gu)
    load_ga, load_w = local(ga_in, acts), local(w_a_in, w_a)
    loads = [local(src, dst) for src, dst in ((mixed_in, mixed), (q_in, q), (k_in, k), (v_in, v))]
    greet(partners)
    sum_far2 = send(ffn_sum, x_recv2, pair_sems, 0, far_id)
    sum_far2.start()
    if ring:
        load_g.wait()
    ring_g.start(3)
    load_ga.wait()
    load_w.wait()
    for copy in loads:
        copy.wait()

    def grad_mixed(i, carry):
        do[block_rows(i), :] = dot(acts[block_rows(i), :], w_a[:, kv_at:out_at]).astype(BF16)
        return carry

    def out_grad(i, carry):
        grads_a[block_rows(i), kv_at:out_at] = dot_tn(acts[:, block_rows(i)], mixed[...]).astype(BF16)
        return carry

    blocks = length // BLK
    lax.fori_loop(0, blocks, grad_mixed, 0)
    lax.fori_loop(0, width // BLK, out_grad, 0)
    load_normed = local(normed_in, acts)

    dk_acc[...] = jnp.zeros_like(dk_acc)
    dv_acc[...] = jnp.zeros_like(dv_acc)

    def attention(i, carry):
        attend_back(t, i, q, do, mixed, lse, k, v, pos, valid, cos, sin, dqkv, dk_acc, dv_acc)
        return carry

    lax.fori_loop(0, blocks // 2 + 1, attention, 0)
    ring_g.next(3)
    lax.fori_loop(blocks // 2 + 1, blocks, attention, 0)
    a = dk_acc[...] * HEAD**-0.5
    dqkv[:, q_cols : q_cols + HEAD] = (a * cos[...] - pltpu.roll(a, HEAD // 2, 1) * sin[...]).astype(BF16)
    dqkv[:, q_cols + HEAD : kv_at] = dv_acc[...].astype(BF16)
    load_normed.wait()

    def qkv_grad(i, carry):
        grads_a[block_rows(i), :kv_at] = dot_tn(acts[:, block_rows(i)], dqkv[...]).astype(BF16)
        return carry

    lax.fori_loop(0, width // BLK, qkv_grad, 0)
    ring_a.start(1)

    gain_acc[...] = jnp.zeros_like(gain_acc)

    def grad_normed(first):
        def body(i, carry):
            mine = block_rows(i + first)
            y = dot_nt(dqkv[mine, :], w_a[:, :kv_at])
            part[block_rows(i), :] = y.astype(BF16)
            gain_acc[0:1, :] += jnp.sum(y * acts[mine, :].astype(F32), axis=0, keepdims=True)
            return carry

        return body

    def fetch(src, dst):
        local(src, dst).wait()

    upper = pl.ds(quarter, quarter)
    per = half // BLK
    lax.fori_loop(0, per, grad_normed(per), 0)
    part_far = send(part.at[upper, :], far_recv, pair_sems, 1, near_id)
    part_far.start()
    part_far.wait_recv()
    fetch(far_recv, stage)
    sum_buf[...] = (part[:quarter, :].astype(F32) + stage[...].astype(F32)).astype(BF16)
    sum_far = send(sum_buf, x_recv, pair_sems, 2, far_id)
    sum_far.start()
    part_far.wait_send()
    lax.fori_loop(0, per, grad_normed(0), 0)
    part_near = send(part.at[upper, :], near_recv, pair_sems, 3, near_id)
    part_near.start()

    both = jnp.concatenate(
        [gain_acc[0:1, :] / gains[0:1, :], gain_two[0:1, :], jnp.zeros((HEAD - 2, width), F32)], axis=0
    )
    gain_cols[...] = both.T
    ring_s.start(1)
    ring_a.next(1)
    ring_s.next(1)
    if ring:
        result_gu[...] = ring_g.result()
        stores = [local(result_gu.at[:, :units], gate_out), local(result_gu.at[:, units:], up_out)]
    else:
        stores = []
    ring_a.next(2)
    ring_s.next(2)

    size = rows_a.shape[1]
    steps = quarter // size

    def rows_at(i):
        return pl.ds(i * size, size)

    sum_far2.wait_recv()
    fetch(x_recv2, stage)
    for i in range(steps):
        fetch(out_part.at[rows_at(i), :], rows_a.at[0])
        if i > 1:
            stores[-2].wait()
        out_rows[i % 2] = (rows_a[0] + stage[i * size : (i + 1) * size, :].astype(F32)).astype(BF16)
        stores.append(local(out_rows.at[i % 2], output.at[rows_at(i), :]))
    for copy in stores[-2:]:
        copy.wait()
    stores = stores[:-steps]
    ring_a.next(3)
    ring_s.next(3)

    part_near.wait_recv()
    fetch(near_recv, stage)
    if ring:
        shard = ring_a.result()
        result_a[...] = shard
        small[:, : 2 * HEAD] = shard[:, q_cols:kv_at]
        small[:, 2 * HEAD :] = ring_s.result()
        small_one = send(small, small_near, pair_sems, 4, near_id)
        small_one.start()
        small_one.wait_send()
        small_one.wait_recv()
        small[...] = small[...] + small_near[...]
        small_two = send(small, small_far, pair_sems, 5, far_id)
        small_two.start()

    sum_far.wait_send()
    sum_far.wait_recv()
    fetch(x_recv, sum_buf)

    def load_rows(i):
        return (
            local(tokens.at[rows_at(i), :], out_rows.at[i % 2]),
            local(grad_residual.at[rows_at(i), :], rows_b.at[i % 2]),
        )

    done = []
    coming = load_rows(0)
    for i in range(steps):
        for copy in coming:
            copy.wait()
        if i + 1 < steps:
            if i > 0:
                done[-1].wait()
            coming = load_rows(i + 1)
        mine = slice(i * size, (i + 1) * size)
        rows = out_rows[i % 2].astype(F32)
        grad_n = part[mine, :].astype(F32) + stage[mine, :].astype(F32) + sum_buf[mine, :].astype(F32)
        scale = lax.rsqrt(jnp.mean(rows * rows, axis=-1, keepdims=True) + EPS)
        weighted = grad_n * gains[0:1, :]
        inner = jnp.mean(rows * weighted, axis=-1, keepdims=True)
        rows_b[i % 2] = rows_b[i % 2] + scale * weighted - rows * (scale * scale * scale * inner)
        done.append(local(rows_b.at[i % 2], grad_tokens.at[rows_at(i), :]))
    for copy in done[-2:]:
        copy.wait()

    if ring:
        small_two.wait_send()
        small_two.wait_recv()
        small[...] = small[...] + small_far[...]
        result_a[:, q_cols:kv_at] = small[:, : 2 * HEAD]
        stores.append(local(result_a, grads_a_out))
        stores.append(local(small.at[:, 2 * HEAD :], gain_out))
    else:
        stores.append(local(grads_a, grads_a_out))
        stores.append(local(gain_cols, gain_out))
    for copy in stores:
        copy.wait()
    ring_g.end()
    ring_a.end()
    ring_s.end()
    for copy in (sum_far2, part_near):
        copy.wait_send()


def back(n_dp, grad_residual, ga, grads_gu, ffn_sum, out_part, tokens, w_a, q, k, v, mixed, normed, *rest):
    length, width = ga.shape
    units = grads_gu.shape[1] // 2
    quarter = length // 4
    rows = width // 8
    q_cols = q.shape[1]
    cols = 2 * q_cols + 2 * HEAD
    vmem = pl.BlockSpec(memory_space=pltpu.VMEM)
    hbm = pl.BlockSpec(memory_space=pl.ANY)
    shape = jax.ShapeDtypeStruct
    pair = shape((quarter, width), BF16)
    ring = n_dp == 8
    return pl.pallas_call(
        functools.partial(back_kernel, n_dp),
        in_specs=[hbm] * 12 + [vmem] * 7,
        out_specs=[hbm] * 12,
        out_shape=[
            pair,
            shape((quarter, width), F32),
            shape((rows, units), F32),
            shape((rows, units), F32),
            shape((rows, cols), F32) if ring else shape((width, cols), BF16),
            shape((rows if ring else width, HEAD), F32),
            pair,
            pair,
            pair,
            pair,
            shape((8, rows, 2 * units), BF16),
            shape((8, rows, cols), BF16),
        ],
        scratch_shapes=[
            pltpu.VMEM((length, width), BF16),
            pltpu.VMEM(w_a.shape, BF16),
            pltpu.VMEM((length, q_cols), BF16),
            pltpu.VMEM((length, HEAD), BF16),
            pltpu.VMEM((length, HEAD), BF16),
            pltpu.VMEM((length, q_cols), BF16),
            pltpu.VMEM((length, q_cols), BF16),
            pltpu.VMEM((length, q_cols + 2 * HEAD), BF16),
            pltpu.VMEM((length, HEAD), F32),
            pltpu.VMEM((length, HEAD), F32),
            pltpu.VMEM((width, cols), BF16),
            pltpu.VMEM((width, 2 * units), BF16),
            pltpu.VMEM((length // 2, width), BF16),
            pltpu.VMEM((quarter, width), BF16),
            pltpu.VMEM((quarter, width), BF16),
            pltpu.VMEM((rows, 2 * units), BF16),
            pltpu.VMEM((rows, 2 * units), F32),
            pltpu.VMEM((rows, cols), F32),
            pltpu.VMEM((2, 64, width), F32),
            pltpu.VMEM((2, 64, width), F32),
            pltpu.VMEM((2, 64, width), BF16),
            pltpu.VMEM((8, width), F32),
            pltpu.VMEM((width, HEAD), F32),
            pltpu.VMEM((8, rows, HEAD), F32),
            pltpu.VMEM((rows, 3 * HEAD), F32),
            pltpu.VMEM((rows, 3 * HEAD), F32),
            pltpu.VMEM((rows, 3 * HEAD), F32),
            pltpu.SemaphoreType.DMA((2, 24)),
            pltpu.SemaphoreType.DMA((2, 8)),
            pltpu.SemaphoreType.DMA((24,)),
            pltpu.SemaphoreType.DMA((72,)),
        ],
        compiler_params=pltpu.CompilerParams(
            collective_id=2, has_side_effects=True, vmem_limit_bytes=60 * MIB
        ),
        cost_estimate=pl.CostEstimate(
            flops=14 * length * width * q_cols, bytes_accessed=64 * MIB, transcendentals=0
        ),
        name="back",
    )(grad_residual, ga, grads_gu, ffn_sum, out_part, tokens, w_a, q, k, v, mixed, normed, *rest)[:6]


def positions_of(segments):
    places = jnp.arange(segments.shape[0], dtype=jnp.int32)
    previous = jnp.concatenate([jnp.full((1,), -1, jnp.int32), segments[:-1]])
    starts = lax.cummax(jnp.where(segments != previous, places, 0), axis=0)
    return places - starts


def per_device(
    n_dp,
    tokens,
    w_query,
    w_keyval,
    w_out,
    w_gate,
    w_up,
    w_down,
    norm_gains,
    segment_ids,
    grad_output,
):
    t = lax.axis_index("tensor").astype(jnp.int32)
    quarter, width = tokens.shape
    length = 4 * quarter
    q_cols = w_query.shape[1]
    units = w_gate.shape[1]

    gain_cols = jnp.pad(norm_gains.T, ((0, 0), (0, HEAD - 2)))
    shard_a = jnp.concatenate([w_query, w_keyval, w_out.T, gain_cols], axis=1)
    shard_d = w_down.T
    shard_g = jnp.concatenate([w_gate, w_up], axis=1)
    if n_dp != 8:
        shard_a, shard_d, shard_g = (
            lax.all_gather(w, "dp", axis=0, tiled=True) for w in (shard_a, shard_d, shard_g)
        )

    turn = t ^ jnp.arange(4, dtype=jnp.int32)
    positions = positions_of(segment_ids).reshape(4, quarter)[turn].reshape(length)
    valid = (segment_ids != 0).reshape(4, quarter)[turn].reshape(length).astype(F32)
    inverse = 10000.0 ** (-jnp.arange(HEAD // 2, dtype=F32) / (HEAD // 2))
    angles = positions.astype(F32)[:, None] * inverse[None, :]
    cos_half, sin_half = jnp.cos(angles), jnp.sin(angles)
    cos = jnp.concatenate([cos_half, cos_half], axis=1)
    sin = jnp.concatenate([-sin_half, sin_half], axis=1)
    pos3 = positions.reshape(length // BLK, 1, BLK)
    valid3 = valid.reshape(length // BLK, 1, BLK)

    (w_a, w_down_t, w_gu, gains, normed, q, k, v, mixed, lse, residual, n2, go_all, gh) = front(
        n_dp, tokens, grad_output, shard_a, shard_d, shard_g, pos3, valid3, cos, sin, q_cols
    )
    grads_gu, down, grad_residual, gain_two, ga, ffn_sum, out_part = middle(
        n_dp, n2, gh, go_all, w_gu, w_down_t, residual, grad_output, gains
    )
    output, grad_tokens, gate, up, grads_a, gain_grads = back(
        n_dp, grad_residual, ga, grads_gu, ffn_sum, out_part, tokens, w_a, q, k, v, mixed, normed,
        lse, pos3, valid3, cos, sin, gains, gain_two
    )
    kv_at = q_cols + 2 * HEAD
    if n_dp != 8:

        def spread(full):
            return lax.psum_scatter(full.astype(F32), "dp", scatter_dimension=0, tiled=True)

        down, gate, up, grads_a, gain_grads = (
            spread(w)
            for w in (down, grads_gu[:, :units], grads_gu[:, units:], grads_a, gain_grads)
        )
        keyval, gain_grads = lax.psum((grads_a[:, q_cols:kv_at], gain_grads), "tensor")
    else:
        keyval = grads_a[:, q_cols:kv_at]

    return (
        output,
        grad_tokens,
        grads_a[:, :q_cols],
        keyval,
        grads_a[:, kv_at:].T,
        gate,
        up,
        down.T,
        gain_grads[:, :2].T,
    )


def solution(mesh):
    return jax.shard_map(
        functools.partial(per_device, mesh.shape["dp"]),
        mesh=mesh,
        in_specs=(
            P(("dp", "tensor"), None),
            P("dp", "tensor"),
            P("dp", None),
            P("tensor", "dp"),
            P("dp", "tensor"),
            P("dp", "tensor"),
            P("tensor", "dp"),
            P(None, "dp"),
            P("dp"),
            P(("dp", "tensor"), None),
        ),
        out_specs=(
            P(("dp", "tensor"), None),
            P(("dp", "tensor"), None),
            P("dp", "tensor"),
            P("dp", None),
            P("tensor", "dp"),
            P("dp", "tensor"),
            P("dp", "tensor"),
            P("tensor", "dp"),
            P(None, "dp"),
        ),
        check_vma=False,
    )
```

```python
import functools

import jax
import jax.numpy as jnp
from jax import lax
from jax.experimental import pallas as pl
from jax.experimental.pallas import tpu as pltpu
from jax.sharding import PartitionSpec as P

WINDOW = 1024
EPS = 1e-6
MASKED = -1e30
HEAD = 128
BLK = 256
LOG2E = 1.4426950408889634
F32 = jnp.float32
BF16 = jnp.bfloat16
MIB = 1 << 20
EARLY = 2

NT = (((1,), (1,)), ((), ()))
TN = (((0,), (0,)), ((), ()))


def dot(left, right):
    return jnp.dot(left, right, preferred_element_type=F32)


def dot_nt(left, right):
    return lax.dot_general(left, right, NT, preferred_element_type=F32)


def dot_tn(left, right):
    return lax.dot_general(left, right, TN, preferred_element_type=F32)


def stacked(block, heads):
    return jnp.concatenate([block[:, h * HEAD : (h + 1) * HEAD] for h in range(heads)], axis=0)


def partner(t, j):
    rem, div = lax.rem, lax.div
    two = jnp.int32(2)
    j = jnp.int32(j)
    return rem(div(t, two) + div(j, two), two) * 2 + rem(rem(t, two) + rem(j, two), two)


def block_rows(i):
    return pl.ds(pl.multiple_of(i * BLK, BLK), BLK)


def key_row(t, kb):
    per = 512 // BLK
    return pl.multiple_of((partner(t, lax.div(kb, per)) * per + lax.rem(kb, per)) * BLK, BLK)


def query_block(t, i):
    per = 512 // BLK
    i = jnp.int32(i)
    return partner(t, lax.div(i, per)) * per + lax.rem(i, per)


def tiled3(row, heads):
    return jnp.concatenate([row] * heads, axis=1)


def attend(t, i, q, k, v, pos, valid, mixed, lse):
    cols = q.shape[1]
    heads = cols // HEAD
    wide = heads * BLK
    qb = query_block(t, i)
    mine = pl.ds(pl.multiple_of(i * BLK, BLK), BLK)
    q3 = stacked(q[mine, :], heads)
    at = qb * BLK + lax.broadcasted_iota(jnp.int32, (1, BLK), 1)
    low = at - jnp.minimum(pos[i], WINDOW - 1)
    at3, low3 = tiled3(at, heads), tiled3(low, heads)
    factor = HEAD**-0.5 * LOG2E

    def step(kb, carry):
        peak, total, acc = carry
        row = key_row(t, kb)
        s = dot_nt(k[pl.ds(row, BLK), :], q3) * factor
        u = kb * BLK + lax.broadcasted_iota(jnp.int32, (BLK, wide), 0)
        s = jnp.where((u <= at3) & (u >= low3), s, MASKED)
        new_peak = jnp.maximum(peak, jnp.max(s, axis=0, keepdims=True))
        p = jnp.exp2(s - new_peak)
        shrink = jnp.exp2(peak - new_peak)
        total = total * shrink + jnp.sum(p, axis=0, keepdims=True)
        acc = acc * shrink + dot_tn(v[pl.ds(row, BLK), :], p.astype(BF16))
        return new_peak, total, acc

    peak, total, acc = lax.fori_loop(
        jnp.maximum(qb - WINDOW // BLK, 0),
        qb + 1,
        step,
        (
            jnp.full((1, wide), MASKED, F32),
            jnp.zeros((1, wide), F32),
            jnp.zeros((HEAD, wide), F32),
        ),
    )
    lse[i] = peak + jnp.log2(total)
    acc = acc * (tiled3(valid[i], heads) / total)
    mixed[mine, :] = jnp.concatenate(
        [acc[:, h * BLK : (h + 1) * BLK].T for h in range(heads)], axis=1
    ).astype(BF16)


def ring_device(p, n):
    p = lax.rem(p + n, jnp.int32(n))
    down = lax.div(p, jnp.int32(n // 2))
    return (1 - down) * 2 * p + down * (2 * (n - 1 - p) + 1)


def ring_place(d, n):
    z, y = lax.div(d, jnp.int32(2)), lax.rem(d, jnp.int32(2))
    return z + y * (n - 1 - 2 * z)


def send(src, dst, sems, at, device):
    return pltpu.make_async_remote_copy(
        src_ref=src,
        dst_ref=dst,
        send_sem=sems.at[0, at],
        recv_sem=sems.at[1, at],
        device_id=device,
        device_id_type=pl.DeviceIdType.MESH,
    )


class Ring:
    def __init__(self, shard, full, sems, first_sem, own, n, direction):
        self.shard, self.full, self.sems, self.at, self.own = shard, full, sems, first_sem, own
        self.n, self.dir = n, direction
        self.copies = {}

    def block(self, offset, place):
        rows = self.shard.shape[0]
        at = ring_device(place + offset * self.dir, self.n) * rows
        return self.full.at[pl.ds(pl.multiple_of(at, rows & -rows), rows), :]

    def begin(self, place):
        self.place = place
        if self.n == 8:
            target = self.block(0, place)
        else:
            target = self.full
        self.local = pltpu.make_async_copy(self.shard, target, self.own)
        self.local.start()
        self.start(1)

    def start(self, s):
        if self.n != 8:
            return
        for way in (0, 1):
            if s > self.n // 2 - way:
                continue
            sign = 1 - 2 * way
            block = self.block(-sign * (s - 1), self.place)
            device = ring_device(self.place + sign * self.dir, self.n)
            src = self.shard if s == 1 else block
            at = self.at + 2 * (s - 1) + way
            copy = send(src, block, self.sems, at, {"dp": device})
            copy.start()
            self.copies[s, way] = copy

    def arrived(self, s):
        for way in (0, 1):
            if (s, way) in self.copies:
                self.copies[s, way].wait_recv()

    def next(self, s):
        self.arrived(s)
        self.start(s + 1)

    def end(self):
        for copy in self.copies.values():
            copy.wait_send()
        self.local.wait()


class RingSum:
    def __init__(self, full, recv, sems, first_sem, n, direction, place, first_hop=1):
        self.full, self.recv, self.sems, self.at = full, recv, sems, first_sem
        self.n, self.dir, self.place, self.first_hop = n, direction, place, first_hop
        self.rows = full.shape[0] // n
        self.copies = {}

    def block(self, offset):
        at = ring_device(self.place + offset * self.dir, self.n) * self.rows
        return pl.ds(pl.multiple_of(at, self.rows & -self.rows), self.rows)

    def last(self, way):
        return self.n // 2 - way

    def slot(self, s, way):
        return way * (self.recv.shape[0] // 2) + s - self.first_hop

    def start(self, s, ways=(0, 1), source=None):
        for way in ways:
            if self.n == 8 and s <= self.last(way):
                sign = 1 - 2 * way
                device = ring_device(self.place + sign * self.dir, self.n)
                rows = self.block(sign * (self.last(way) + 1 - s))
                src = (self.full if source is None else source).at[rows, :]
                slot = self.slot(s, way)
                copy = send(src, self.recv.at[slot], self.sems, self.at + slot, {"dp": device})
                copy.start()
                self.copies[s, way] = copy

    def arrived(self, s, way):
        self.copies[s, way].wait_recv()
        return self.recv[self.slot(s, way)]

    def add(self, s, start=False):
        for way in (0, 1):
            if self.n == 8 and s < self.last(way):
                far = self.last(way)
                mine = self.block((1 - 2 * way) * (far - s))
                self.full[mine, :] = self.full[mine, :] + self.arrived(s, way)
                if start:
                    self.start(s + 1, (way,))

    def next(self, s):
        self.add(s, True)

    def close(self, way):
        if self.n == 8:
            mine = self.block(0)
            self.full[mine, :] = self.full[mine, :] + self.arrived(self.last(way), way)

    def result(self, ways=(0, 1)):
        acc = self.full[self.block(0), :].astype(F32)
        for way in ways:
            acc = acc + self.arrived(self.last(way), way).astype(F32)
        return acc

    def save(self, offsets, target, local):
        if self.n != 8:
            return []
        blocks = [self.block(offset) for offset in offsets]
        return [local(self.full.at[rows, :], target.at[rows, :]) for rows in blocks]

    def end(self):
        for copy in self.copies.values():
            copy.wait_send()


def front_kernel(
    n_dp,
    tokens,
    grad_output,
    shard_a,
    shard_d,
    shard_g,
    pos,
    valid,
    inverse,
    cos_out,
    sin_out,
    w_a_out,
    w_d_out,
    w_g,
    gains,
    normed_out,
    q_out,
    k_out,
    v_out,
    mixed_out,
    lse,
    residual_out,
    n2_out,
    go_out,
    gh_out,
    cos,
    sin,
    w_a,
    w_d,
    x4,
    normed,
    q,
    k,
    v,
    mixed,
    near_recv,
    far_recv,
    x_recv,
    sum_buf,
    n2_own,
    go_buf,
    gh_buf,
    res,
    ring_sems,
    pair_sems,
    local_sems,
):
    quarter, width = tokens.shape
    q_cols = q.shape[1]
    heads = q_cols // HEAD
    kv_at = q_cols + 2 * HEAD
    gain_at = kv_at + q_cols
    t = lax.axis_index("tensor").astype(jnp.int32)
    place = ring_place(lax.axis_index("dp").astype(jnp.int32), n_dp)
    near_id, far_id = {"tensor": partner(t, 1)}, {"tensor": partner(t, 2)}

    barrier = pltpu.get_barrier_semaphore()
    partners = [near_id, far_id]
    if n_dp == 8:
        partners += [{"dp": ring_device(place + 1, n_dp)}, {"dp": ring_device(place - 1, n_dp)}]
    for device in partners:
        pl.semaphore_signal(barrier, inc=1, device_id=device, device_id_type=pl.DeviceIdType.MESH)
    pl.semaphore_wait(barrier, len(partners))

    def rows_of(ref, j, size=1):
        return ref.at[pl.ds(j * quarter, size * quarter), :]

    used = [0]

    def local(src, dst):
        copy = pltpu.make_async_copy(src, dst, local_sems.at[used[0]])
        used[0] += 1
        copy.start()
        return copy

    ring_a = Ring(shard_a, w_a, ring_sems, 0, local_sems.at[24], n_dp, 1)
    ring_d = Ring(shard_d, w_d, ring_sems, 8, local_sems.at[25], n_dp, 1)
    ring_g = Ring(shard_g, w_g, ring_sems, 16, local_sems.at[26], n_dp, -1)

    ring_a.begin(place)
    x_far = send(tokens, rows_of(x4, 2), pair_sems, 0, far_id)
    x_far.start()
    x_near = send(tokens, rows_of(x4, 1), pair_sems, 1, near_id)
    x_near.start()
    x_own = local(tokens, rows_of(x4, 0))
    go_in = local(grad_output, res)
    def tables(i, carry):
        places = jnp.broadcast_to(pos[i].astype(F32), (HEAD, BLK)).T
        angles = places * inverse[...]
        sine = jnp.sin(angles)
        lane = lax.broadcasted_iota(jnp.int32, sine.shape, 1)
        cos[block_rows(i), :] = jnp.cos(angles)
        sin[block_rows(i), :] = jnp.where(lane < HEAD // 2, -sine, sine)
        return carry

    count = pos.shape[0]
    for s in (1, 2, 3):
        lax.fori_loop(count * (s - 1) // 3, count * s // 3, tables, 0)
        ring_a.next(s)
    ring_d.begin(place)
    ring_g.begin(place)
    ring_a.arrived(4)
    ring_a.local.wait()

    gain_rows = w_a[:, gain_at : gain_at + HEAD].astype(F32).T
    gains[...] = gain_rows[:8]

    def project(i, carry):
        mine = pl.ds(pl.multiple_of(i * BLK, BLK), BLK)
        rows = x4[mine, :].astype(F32)
        scale = lax.rsqrt(jnp.mean(rows * rows, axis=-1, keepdims=True) + EPS)
        n = (rows * scale * gains[0:1, :]).astype(BF16)
        normed[mine, :] = n
        y = dot(n, w_a[:, :kv_at])
        c, s = cos[mine, :], sin[mine, :]

        def turned(a):
            return (a * c + pltpu.roll(a, HEAD // 2, 1) * s).astype(BF16)

        q[mine, :] = jnp.concatenate(
            [turned(y[:, h * HEAD : (h + 1) * HEAD]) for h in range(heads)], axis=1
        )
        k[mine, :] = turned(y[:, q_cols : q_cols + HEAD])
        v[mine, :] = y[:, q_cols + HEAD : kv_at].astype(BF16)
        return carry

    per = quarter // BLK
    x_own.wait()
    x_near.wait_recv()
    lax.fori_loop(0, 2 * per, project, 0)
    x_far.wait_recv()
    x_last = send(rows_of(x4, 2), rows_of(x4, 3), pair_sems, 2, near_id)
    x_last.start()
    go_in.wait()
    go_buf[...] = res[...].astype(BF16)
    go_far = send(go_buf, rows_of(go_out, 2), pair_sems, 3, far_id)
    go_far.start()
    go_near = send(go_buf, rows_of(go_out, 1), pair_sems, 4, near_id)
    go_near.start()
    go_own = local(go_buf, rows_of(go_out, 0))
    x_last.wait_recv()
    lax.fori_loop(2 * per, 4 * per, project, 0)
    copies = [
        local(cos, cos_out),
        local(sin, sin_out),
        local(normed, normed_out),
        local(q, q_out),
        local(k, k_out),
        local(v, v_out),
        local(w_a, w_a_out),
    ]

    def attention(i, carry):
        attend(t, i, q, k, v, pos, valid, mixed, lse)
        return carry

    part = x4

    def out_product(i, carry):
        mine = pl.ds(pl.multiple_of(i * BLK, BLK), BLK)
        part[mine, :] = dot_nt(mixed[mine, :], w_a[:, kv_at:gain_at]).astype(BF16)
        return carry

    x_last.wait_send()
    lax.fori_loop(2 * per, 4 * per, attention, 0)
    ring_d.next(1)
    lax.fori_loop(2 * per, 4 * per, out_product, 0)
    part_far = send(rows_of(part, 3), far_recv, pair_sems, 5, near_id)
    part_far.start()
    lax.fori_loop(0, 1, attention, 0)
    part_far.wait_recv()
    sum_buf[...] = (part[pl.ds(2 * quarter, quarter), :].astype(F32) + far_recv[...].astype(F32)).astype(BF16)
    sum_far = send(sum_buf, x_recv, pair_sems, 6, far_id)
    sum_far.start()
    ring_g.next(1)
    lax.fori_loop(1, 2 * per, attention, 0)
    lax.fori_loop(0, 2 * per, out_product, 0)
    part_near = send(rows_of(part, 1), near_recv, pair_sems, 7, near_id)
    part_near.start()
    copies.append(local(mixed, mixed_out))
    ring_d.next(2)
    ring_d.next(3)
    ring_g.next(2)
    go_far.wait_recv()
    go_last = send(rows_of(go_out, 2), rows_of(go_out, 3), pair_sems, 8, near_id)
    go_last.start()
    part_near.wait_recv()
    sum_far.wait_recv()

    res[...] = (
        tokens[...].astype(F32)
        + part[pl.ds(0, quarter), :].astype(F32)
        + near_recv[...].astype(F32)
        + x_recv[...].astype(F32)
    )
    scale_two = lax.rsqrt(jnp.mean(res[...] * res[...], axis=-1, keepdims=True) + EPS)
    n2_own[...] = (res[...] * scale_two * gains[1:2, :]).astype(BF16)
    n2_far = send(n2_own, rows_of(n2_out, 2), pair_sems, 9, far_id)
    n2_far.start()
    n2_near = send(n2_own, rows_of(n2_out, 1), pair_sems, 10, near_id)
    n2_near.start()
    copies.append(local(n2_own, rows_of(n2_out, 0)))
    copies.append(local(res, residual_out))

    ring_d.arrived(4)
    ring_d.local.wait()
    copies.append(local(w_d, w_d_out))
    go_far.wait_send()
    go_near.wait_send()
    go_own.wait()

    def grad_hidden(i, carry):
        mine = pl.ds(pl.multiple_of(i * BLK, BLK), BLK)
        gh_buf[mine, :] = dot(go_buf[mine, :], w_d[...]).astype(BF16)
        return carry

    for j in range(4):
        if j == 1:
            go_near.wait_recv()
        if j == 3:
            go_last.wait_recv()
        if j > 0:
            load = local(rows_of(go_out, j), go_buf)
            load.wait()
        if j > 0:
            store.wait()
        lax.fori_loop(0, per, grad_hidden, 0)
        store = local(gh_buf, rows_of(gh_out, j))
        if j == 1:
            ring_g.next(3)

    n2_far.wait_recv()
    n2_last = send(rows_of(n2_out, 2), rows_of(n2_out, 3), pair_sems, 11, near_id)
    n2_last.start()
    ring_g.arrived(4)
    store.wait()
    for copy in copies:
        copy.wait()
    for copy in (x_far, x_near, part_far, sum_far, part_near, go_last, n2_far, n2_near, n2_last):
        copy.wait_send()
    n2_near.wait_recv()
    n2_last.wait_recv()
    ring_a.copies and [c.wait_send() for c in ring_a.copies.values()]
    ring_d.copies and [c.wait_send() for c in ring_d.copies.values()]
    ring_g.end()


def front(n_dp, tokens, grad_output, shard_a, shard_d, shard_g, pos, valid, inverse, q_cols):
    quarter, width = tokens.shape
    length = 4 * quarter
    heads = q_cols // HEAD
    units = shard_d.shape[1]
    cols_a = shard_a.shape[1]
    vmem = pl.BlockSpec(memory_space=pltpu.VMEM)
    hbm = pl.BlockSpec(memory_space=pl.ANY)
    blocks = length // BLK

    def out(rows, cols, kind=BF16):
        return jax.ShapeDtypeStruct((rows, cols), kind)

    return pl.pallas_call(
        functools.partial(front_kernel, n_dp),
        in_specs=[vmem, hbm, hbm, hbm, hbm, vmem, vmem, vmem],
        out_specs=[hbm, hbm, hbm, hbm, hbm, vmem, hbm, hbm, hbm, hbm, hbm, vmem, hbm, hbm, hbm, hbm],
        out_shape=[
            out(length, HEAD, F32),
            out(length, HEAD, F32),
            out(width, cols_a),
            out(width, units),
            out(width, 2 * units),
            out(8, width, F32),
            out(length, width),
            out(length, q_cols),
            out(length, HEAD),
            out(length, HEAD),
            out(length, q_cols),
            jax.ShapeDtypeStruct((blocks, 1, heads * BLK), F32),
            out(quarter, width, F32),
            out(length, width),
            out(length, width),
            out(length, units),
        ],
        scratch_shapes=[
            pltpu.VMEM((length, HEAD), F32),
            pltpu.VMEM((length, HEAD), F32),
            pltpu.VMEM((width, cols_a), BF16),
            pltpu.VMEM((width, units), BF16),
            pltpu.VMEM((length, width), BF16),
            pltpu.VMEM((length, width), BF16),
            pltpu.VMEM((length, q_cols), BF16),
            pltpu.VMEM((length, HEAD), BF16),
            pltpu.VMEM((length, HEAD), BF16),
            pltpu.VMEM((length, q_cols), BF16),
            pltpu.VMEM((quarter, width), BF16),
            pltpu.VMEM((quarter, width), BF16),
            pltpu.VMEM((quarter, width), BF16),
            pltpu.VMEM((quarter, width), BF16),
            pltpu.VMEM((quarter, width), BF16),
            pltpu.VMEM((quarter, width), BF16),
            pltpu.VMEM((quarter, units), BF16),
            pltpu.VMEM((quarter, width), F32),
            pltpu.SemaphoreType.DMA((2, 24)),
            pltpu.SemaphoreType.DMA((2, 12)),
            pltpu.SemaphoreType.DMA((32,)),
        ],
        compiler_params=pltpu.CompilerParams(
            collective_id=0, has_side_effects=True, vmem_limit_bytes=58 * MIB
        ),
        cost_estimate=pl.CostEstimate(
            flops=12 * length * width * q_cols, bytes_accessed=64 * MIB, transcendentals=0
        ),
        name="front",
    )(tokens, grad_output, shard_a, shard_d, shard_g, pos, valid, inverse)


def attend_back(t, i, q, do, mixed, lse, k, v, pos, valid, cos, sin, dqkv, dk_acc, dv_acc):
    cols = q.shape[1]
    heads = cols // HEAD
    wide = heads * BLK
    qb = query_block(t, i)
    mine = block_rows(i)
    q3 = stacked(q[mine, :], heads)
    do3 = stacked(do[mine, :], heads)
    centre3 = do3.astype(F32) * stacked(mixed[mine, :], heads).astype(F32)
    centre = jnp.sum(centre3.T, axis=0, keepdims=True)
    at = qb * BLK + lax.broadcasted_iota(jnp.int32, (1, BLK), 1)
    low = jnp.where(valid[i] > 0.0, at - jnp.minimum(pos[i], WINDOW - 1), at + 1)
    at3, low3 = tiled3(at, heads), tiled3(low, heads)
    total = lse[i]
    factor = HEAD**-0.5 * LOG2E

    def step(kb, acc):
        row = key_row(t, kb)
        kblk = k[pl.ds(row, BLK), :]
        vblk = v[pl.ds(row, BLK), :]
        s = dot_nt(kblk, q3) * factor - total
        u = kb * BLK + lax.broadcasted_iota(jnp.int32, (BLK, wide), 0)
        p = jnp.exp2(jnp.where((u <= at3) & (u >= low3), s, MASKED))
        gp = dot_nt(vblk, do3)
        ds = (p * (gp - centre)).astype(BF16)
        dv_acc[pl.ds(row, BLK), :] += dot(p.astype(BF16), do3)
        dk_acc[pl.ds(row, BLK), :] += dot(ds, q3)
        return acc + dot_tn(kblk, ds)

    acc = lax.fori_loop(
        jnp.maximum(qb - WINDOW // BLK, 0), qb + 1, step, jnp.zeros((HEAD, wide), F32)
    )
    scale = HEAD**-0.5
    c, sn = cos[mine, :] * scale, sin[mine, :] * scale

    def turned(a):
        return (a * c - pltpu.roll(a, HEAD // 2, 1) * sn).astype(BF16)

    dqkv[mine, :cols] = jnp.concatenate(
        [turned(acc[:, h * BLK : (h + 1) * BLK].T) for h in range(heads)], axis=1
    )


def gated(y, gh, half):
    gate, up = y[:, :half], y[:, half:]
    root = (2.0 / jnp.pi) ** 0.5
    square = gate * gate
    th = jnp.tanh(root * gate * (1.0 + 0.044715 * square))
    one = 0.5 * (1.0 + th)
    act = gate * one
    slope = one + 0.5 * gate * (1.0 - th * th) * (root * (1.0 + 3.0 * 0.044715 * square))
    return (act * up).astype(BF16), (gh * up * slope).astype(BF16), (gh * act).astype(BF16)


def greet(partners):
    barrier = pltpu.get_barrier_semaphore()
    for device in partners:
        pl.semaphore_signal(barrier, inc=1, device_id=device, device_id_type=pl.DeviceIdType.MESH)
    pl.semaphore_wait(barrier, len(partners))


def neighbours(n_dp, t, place):
    near_id, far_id = {"tensor": partner(t, 1)}, {"tensor": partner(t, 2)}
    others = []
    if n_dp == 8:
        others = [{"dp": ring_device(place + 1, n_dp)}, {"dp": ring_device(place - 1, n_dp)}]
    return near_id, far_id, [near_id, far_id] + others


class Local:
    def __init__(self, sems):
        self.sems, self.used = sems, 0

    def __call__(self, src, dst):
        copy = pltpu.make_async_copy(src, dst, self.sems.at[self.used])
        self.used += 1
        copy.start()
        return copy


def middle_kernel(
    n_dp,
    n2_in,
    gh_in,
    go_in,
    w_gu_in,
    w_d_in,
    residual,
    grad_output,
    gains,
    grads_gu_out,
    down_out,
    grad_residual,
    gain_two,
    ga_out,
    ffn_sum_out,
    out_part,
    far_recv,
    x_recv,
    near_recv,
    far_recv2,
    near_recv2,
    w_gu,
    n2,
    go,
    hidden,
    dgu,
    part,
    grads_d,
    grads_gu,
    stage,
    sum_buf,
    ga_own,
    recv_d,
    recv_g,
    rows_a,
    rows_b,
    ring_sems,
    pair_sems,
    local_sems,
):
    length, width = n2.shape
    units = hidden.shape[1]
    quarter = length // 4
    half = length // 2
    t = lax.axis_index("tensor").astype(jnp.int32)
    place = ring_place(lax.axis_index("dp").astype(jnp.int32), n_dp)
    near_id, far_id, partners = neighbours(n_dp, t, place)
    local = Local(local_sems)
    ring_d = RingSum(grads_d, recv_d, ring_sems, 0, n_dp, -1, place)
    ring_g = RingSum(grads_gu, recv_g, ring_sems, 8, n_dp, 1, place)

    far_rows, near_rows = pl.ds(half, half), pl.ds(0, half)
    load_w = local(w_gu_in, w_gu)
    load_far = [local(n2_in.at[far_rows, :], n2.at[far_rows, :]), local(gh_in.at[far_rows, :], hidden.at[far_rows, :])]
    load_near = [local(n2_in.at[near_rows, :], n2.at[near_rows, :]), local(gh_in.at[near_rows, :], hidden.at[near_rows, :])]
    greet(partners)

    def ffn(i, carry):
        mine = block_rows(i)
        y = dot(n2[mine, :], w_gu[...])
        gh = hidden[mine, :].astype(F32)
        hidden[mine, :], dgu[mine, :units], dgu[mine, units:] = gated(y, gh, units)
        return carry

    def back(first):
        def body(i, carry):
            part[block_rows(i), :] = dot_nt(dgu[block_rows(i + first), :], w_gu[...]).astype(BF16)
            return carry

        return body

    def fetch(src, dst):
        local(src, dst).wait()

    upper = pl.ds(quarter, quarter)
    per = half // BLK
    load_w.wait()
    for copy in load_far:
        copy.wait()
    lax.fori_loop(per, 2 * per, ffn, 0)
    lax.fori_loop(0, per, back(per), 0)
    part_far = send(part.at[upper, :], far_recv, pair_sems, 0, near_id)
    part_far.start()
    for copy in load_near:
        copy.wait()
    lax.fori_loop(0, 1, ffn, 0)
    part_far.wait_recv()
    fetch(far_recv, stage)
    sum_buf[...] = (part[:quarter, :].astype(F32) + stage[...].astype(F32)).astype(BF16)
    sum_far = send(sum_buf, x_recv, pair_sems, 1, far_id)
    sum_far.start()
    blocks = width // BLK

    def load_go(i):
        return local(go_in.at[:, pl.ds(i * BLK, BLK)], go.at[i % 2])

    size = rows_a.shape[1]
    steps = quarter // size

    def rows_at(i):
        return pl.ds(i * size, size)

    def load_rows(i):
        return (
            local(residual.at[rows_at(i), :], rows_a.at[i % 2]),
            local(grad_output.at[rows_at(i), :], rows_b.at[i % 2]),
        )

    coming = load_go(0)
    coming_rows = load_rows(0)
    lax.fori_loop(1, per, ffn, 0)
    part_far.wait_send()
    lax.fori_loop(0, per, back(0), 0)
    part_near = send(part.at[upper, :], near_recv, pair_sems, 2, near_id)
    part_near.start()
    load_d = local(w_d_in, w_gu.at[:, :units])

    for i in range(blocks):
        coming.wait()
        if i + 1 < blocks:
            coming = load_go(i + 1)
        grads_d[i * BLK : (i + 1) * BLK, :] = dot_tn(go[i % 2], hidden[...]).astype(BF16)
    ring_d.start(1)

    def gu_grad(i, carry):
        grads_gu[block_rows(i), :] = dot_tn(n2[:, block_rows(i)], dgu[...]).astype(BF16)
        return carry

    part_near.wait_recv()
    fetch(near_recv, stage)
    lax.fori_loop(0, EARLY, gu_grad, 0)
    gain_two[...] = jnp.zeros_like(gain_two)
    sum_far.wait_send()
    sum_far.wait_recv()
    fetch(x_recv, sum_buf)
    stores = []
    for i in range(steps):
        for copy in coming_rows:
            copy.wait()
        if i + 1 < steps:
            if i > 0:
                stores[-1].wait()
            coming_rows = load_rows(i + 1)
        mine = slice(i * size, (i + 1) * size)
        rows = rows_a[i % 2]
        grad_n = part[mine, :].astype(F32) + stage[mine, :].astype(F32) + sum_buf[mine, :].astype(F32)
        scale = lax.rsqrt(jnp.mean(rows * rows, axis=-1, keepdims=True) + EPS)
        weighted = grad_n * gains[1:2, :]
        inner = jnp.mean(rows * weighted, axis=-1, keepdims=True)
        grad = rows_b[i % 2] + scale * weighted - rows * (scale * scale * scale * inner)
        rows_b[i % 2] = grad
        ga_own[mine, :] = grad.astype(BF16)
        gain_two[0:1, :] += jnp.sum(grad_n * rows * scale, axis=0, keepdims=True)
        stores.append(local(rows_b.at[i % 2], grad_residual.at[rows_at(i), :]))

    def quarter_of(ref, j):
        return ref.at[pl.ds(j * quarter, quarter), :]

    ga_far = send(ga_own, quarter_of(ga_out, 2), pair_sems, 3, far_id)
    ga_far.start()
    ga_near = send(ga_own, quarter_of(ga_out, 1), pair_sems, 4, near_id)
    ga_near.start()
    stores_late = [local(ga_own, quarter_of(ga_out, 0))]
    ring_d.next(1)
    lax.fori_loop(EARLY, blocks, gu_grad, 0)
    ring_g.start(1)
    save_gu = local(grads_gu, grads_gu_out)
    ring_d.next(2)
    save_d = local(grads_d, down_out)
    part_near.wait_send()
    load_d.wait()

    def down_product(first):
        def body(i, carry):
            part[block_rows(i), :] = dot_nt(hidden[block_rows(i + first), :], w_gu[:, :units]).astype(BF16)
            return carry

        return body

    lax.fori_loop(0, per, down_product(per), 0)
    part_far2 = send(part.at[upper, :], far_recv2, pair_sems, 5, near_id)
    part_far2.start()
    part_far2.wait_recv()
    fetch(far_recv2, stage)
    sum_buf[...] = (part[:quarter, :].astype(F32) + stage[...].astype(F32)).astype(BF16)
    stores_late.append(local(sum_buf, ffn_sum_out))
    part_far2.wait_send()
    lax.fori_loop(0, per, down_product(0), 0)
    part_near2 = send(part.at[upper, :], near_recv2, pair_sems, 6, near_id)
    part_near2.start()
    part_near2.wait_recv()
    fetch(near_recv2, stage)
    for copy in stores[-2:]:
        copy.wait()
    stores = []
    coming = local(residual.at[rows_at(0), :], rows_a.at[0])
    for i in range(steps):
        coming.wait()
        if i + 1 < steps:
            if i > 0:
                stores[-1].wait()
            coming = local(residual.at[rows_at(i + 1), :], rows_a.at[(i + 1) % 2])
        mine = slice(i * size, (i + 1) * size)
        rows_a[i % 2] = rows_a[i % 2] + part[mine, :].astype(F32) + stage[mine, :].astype(F32)
        stores.append(local(rows_a.at[i % 2], out_part.at[rows_at(i), :]))
    stores_late += stores[-2:]

    ga_far.wait_recv()
    ga_last = send(quarter_of(ga_out, 2), quarter_of(ga_out, 3), pair_sems, 7, near_id)
    ga_last.start()
    save_d.wait()
    ring_d.add(3)
    ring_d.close(1)
    stores_late += ring_d.save((1, 0), down_out, local)
    save_gu.wait()
    ring_g.add(1)
    stores_late += ring_g.save((3, -2), grads_gu_out, local)
    ring_d.end()
    ring_g.end()
    ga_near.wait_recv()
    ga_last.wait_recv()
    for copy in stores_late:
        copy.wait()
    for copy in (ga_far, ga_near, ga_last, part_near2):
        copy.wait_send()


def middle(n_dp, n2, gh, go, w_gu, w_d, residual, grad_output, gains):
    length, width = n2.shape
    units = gh.shape[1]
    quarter = length // 4
    rows = width // 8
    vmem = pl.BlockSpec(memory_space=pltpu.VMEM)
    hbm = pl.BlockSpec(memory_space=pl.ANY)
    shape = jax.ShapeDtypeStruct
    pair = shape((quarter, width), BF16)
    return pl.pallas_call(
        functools.partial(middle_kernel, n_dp),
        in_specs=[hbm] * 7 + [vmem],
        out_specs=[hbm] * 3 + [vmem] + [hbm] * 8,
        out_shape=[
            shape((width, 2 * units), BF16),
            shape((width, units), BF16),
            shape((quarter, width), F32),
            shape((8, width), F32),
            shape((length, width), BF16),
            pair,
            shape((quarter, width), F32),
            pair,
            pair,
            pair,
            pair,
            pair,
        ],
        scratch_shapes=[
            pltpu.VMEM((width, 2 * units), BF16),
            pltpu.VMEM((length, width), BF16),
            pltpu.VMEM((2, length, BLK), BF16),
            pltpu.VMEM((length, units), BF16),
            pltpu.VMEM((length, 2 * units), BF16),
            pltpu.VMEM((length // 2, width), BF16),
            pltpu.VMEM((width, units), BF16),
            pltpu.VMEM((width, 2 * units), BF16),
            pltpu.VMEM((quarter, width), BF16),
            pltpu.VMEM((quarter, width), BF16),
            pltpu.VMEM((quarter, width), BF16),
            pltpu.VMEM((6, rows, units), BF16),
            pltpu.VMEM((2, rows, 2 * units), BF16),
            pltpu.VMEM((2, 128, width), F32),
            pltpu.VMEM((2, 128, width), F32),
            pltpu.SemaphoreType.DMA((2, 16)),
            pltpu.SemaphoreType.DMA((2, 8)),
            pltpu.SemaphoreType.DMA((72,)),
        ],
        compiler_params=pltpu.CompilerParams(
            collective_id=1, has_side_effects=True, vmem_limit_bytes=63 * MIB
        ),
        cost_estimate=pl.CostEstimate(
            flops=14 * length * width * units, bytes_accessed=64 * MIB, transcendentals=0
        ),
        name="middle",
    )(n2, gh, go, w_gu, w_d, residual, grad_output, gains)[:7]


def back_kernel(
    n_dp,
    ga_in,
    grads_gu_in,
    grads_d_in,
    ffn_sum,
    w_a_in,
    q_in,
    k_in,
    v_in,
    mixed_in,
    normed_in,
    lse,
    pos,
    valid,
    cos,
    sin,
    gains,
    gain_two,
    part_own,
    x_recv,
    near_recv,
    x_recv2,
    gate_out,
    up_out,
    down_out,
    grads_a_out,
    keyval_out,
    out_out,
    gain_out,
    far_recv,
    acts,
    w_a,
    q,
    k,
    v,
    mixed,
    do,
    dqkv,
    dk_acc,
    dv_acc,
    grads_a,
    grads_o,
    grads_d,
    grads_gu,
    part,
    stage,
    sum_buf,
    recv_g,
    recv_a,
    recv_o,
    recv_d,
    result_gu,
    result_a,
    result_o,
    result_d,
    gain_acc,
    gain_cols,
    recv_s,
    small,
    small_near,
    small_far,
    ring_sems,
    pair_sems,
    local_sems,
):
    length, width = acts.shape
    quarter = length // 4
    half = length // 2
    q_cols = q.shape[1]
    kv_at = q_cols + 2 * HEAD
    out_at = kv_at + q_cols
    units = grads_gu.shape[1] // 2
    ring = n_dp == 8
    t = lax.axis_index("tensor").astype(jnp.int32)
    place = ring_place(lax.axis_index("dp").astype(jnp.int32), n_dp)
    near_id, far_id, partners = neighbours(n_dp, t, place)
    local = Local(local_sems)
    ring_g = RingSum(grads_gu, recv_g, ring_sems, 0, n_dp, 1, place, 2)
    ring_a = RingSum(grads_a, recv_a, ring_sems, 8, n_dp, -1, place)
    ring_o = RingSum(grads_o, recv_o, ring_sems, 24, n_dp, -1, place)
    ring_d = RingSum(grads_d, recv_d, ring_sems, 32, n_dp, -1, place, 4)
    ring_s = RingSum(gain_cols, recv_s, ring_sems, 16, n_dp, 1, place)

    load_ga, load_w, load_mixed = local(ga_in, acts), local(w_a_in, w_a), local(mixed_in, mixed)
    loads = [local(src, dst) for src, dst in ((q_in, q), (k_in, k), (v_in, v))]
    greet(partners)
    ring_g.start(2, source=grads_gu_in)
    ring_d.start(4, source=grads_d_in)
    sum_far2 = send(ffn_sum, x_recv2, pair_sems, 0, far_id)
    sum_far2.start()
    if ring:
        loads += [local(grads_gu_in, grads_gu), local(grads_d_in, grads_d)]
    load_ga.wait()
    load_w.wait()

    def grad_mixed(i, carry):
        do[block_rows(i), :] = dot(acts[block_rows(i), :], w_a[:, kv_at:out_at]).astype(BF16)
        return carry

    def out_grad(i, carry):
        grads_o[block_rows(i), :] = dot_tn(acts[:, block_rows(i)], mixed[...]).astype(BF16)
        return carry

    blocks = length // BLK
    lax.fori_loop(0, blocks, grad_mixed, 0)
    load_mixed.wait()
    lax.fori_loop(0, width // BLK, out_grad, 0)
    ring_o.start(1)
    load_normed = local(normed_in, acts)
    for copy in loads:
        copy.wait()

    dk_acc[...] = jnp.zeros_like(dk_acc)
    dv_acc[...] = jnp.zeros_like(dv_acc)

    def attention(i, carry):
        attend_back(t, i, q, do, mixed, lse, k, v, pos, valid, cos, sin, dqkv, dk_acc, dv_acc)
        return carry

    lax.fori_loop(0, blocks * 4 // 8, attention, 0)
    ring_o.next(1)
    ring_g.next(2)
    lax.fori_loop(blocks * 4 // 8, blocks * 6 // 8, attention, 0)
    ring_o.next(2)
    if ring:
        result_d[...] = ring_d.result((0,))
        store_d = local(result_d, down_out)
    lax.fori_loop(blocks * 6 // 8, blocks, attention, 0)
    a = dk_acc[...] * HEAD**-0.5
    dqkv[:, q_cols : q_cols + HEAD] = (a * cos[...] - pltpu.roll(a, HEAD // 2, 1) * sin[...]).astype(BF16)
    dqkv[:, q_cols + HEAD : kv_at] = dv_acc[...].astype(BF16)
    load_normed.wait()

    gain_acc[...] = jnp.zeros_like(gain_acc)

    def grad_normed(first):
        def body(i, carry):
            mine = block_rows(i + first)
            y = dot_nt(dqkv[mine, :], w_a[:, :kv_at])
            part[block_rows(i), :] = y.astype(BF16)
            gain_acc[0:1, :] += jnp.sum(y * acts[mine, :].astype(F32), axis=0, keepdims=True)
            return carry

        return body

    def fetch(src, dst):
        local(src, dst).wait()

    upper = pl.ds(quarter, quarter)
    per = half // BLK
    lax.fori_loop(0, per, grad_normed(per), 0)
    part_far = send(part.at[upper, :], far_recv, pair_sems, 1, near_id)
    part_far.start()
    ring_o.next(3)

    def qkv_grad(i, carry):
        grads_a[block_rows(i), :] = dot_tn(acts[:, block_rows(i)], dqkv[...]).astype(BF16)
        return carry

    lax.fori_loop(0, width // BLK, qkv_grad, 0)
    ring_a.start(1)
    part_far.wait_recv()
    fetch(far_recv, stage)
    sum_buf[...] = (part[:quarter, :].astype(F32) + stage[...].astype(F32)).astype(BF16)
    sum_far = send(sum_buf, x_recv, pair_sems, 2, far_id)
    sum_far.start()
    part_far.wait_send()
    lax.fori_loop(0, per, grad_normed(0), 0)
    part_near = send(part.at[upper, :], near_recv, pair_sems, 3, near_id)
    part_near.start()
    stores = [local(part.at[pl.ds(0, quarter), :], part_own)]
    ring_g.next(3)

    both = jnp.concatenate(
        [gain_acc[0:1, :] / gains[0:1, :], gain_two[0:1, :], jnp.zeros((HEAD - 2, width), F32)], axis=0
    )
    gain_cols[...] = both.T
    ring_s.start(1)
    ring_a.next(1)
    ring_s.next(1)
    if ring:
        result_o[...] = ring_o.result()
        stores.append(local(result_o, out_out))
    ring_a.next(2)
    ring_s.next(2)
    if ring:
        result_gu[...] = ring_g.result()
        stores += [local(result_gu.at[:, :units], gate_out), local(result_gu.at[:, units:], up_out)]
    ring_a.next(3)
    ring_s.next(3)

    if ring:
        shard = ring_a.result()
        result_a[:, :q_cols] = shard[:, :q_cols]
        small[:, : 2 * HEAD] = shard[:, q_cols:kv_at].astype(BF16)
        small[:, 2 * HEAD :] = ring_s.result().astype(BF16)
        small_one = send(small, small_near, pair_sems, 4, near_id)
        small_one.start()
        small_one.wait_send()
        small_one.wait_recv()
        small[...] = (small[...].astype(F32) + small_near[...].astype(F32)).astype(BF16)
        small_two = send(small, small_far, pair_sems, 5, far_id)
        small_two.start()
        small_two.wait_send()
        small_two.wait_recv()
        both = small[...].astype(F32) + small_far[...].astype(F32)
        result_a[:, q_cols:kv_at] = both[:, : 2 * HEAD]
        ring_s.end()
        gain_cols[: both.shape[0], :] = both[:, 2 * HEAD :]
        stores.append(local(result_a.at[:, :q_cols], grads_a_out))
        stores.append(local(result_a.at[:, q_cols:], keyval_out))
        stores.append(local(gain_cols.at[pl.ds(0, both.shape[0]), :], gain_out))
    else:
        stores.append(local(grads_a, grads_a_out))
        stores.append(local(result_a.at[:, q_cols:], keyval_out))
        stores.append(local(grads_o, out_out))
        stores.append(local(gain_cols, gain_out))
    if ring:
        stores.append(store_d)
    for copy in stores:
        copy.wait()
    for each in (ring_g, ring_a, ring_o, ring_d):
        each.end()
    for copy in (sum_far2, part_near, sum_far):
        copy.wait_send()
    sum_far2.wait_recv()
    part_near.wait_recv()
    sum_far.wait_recv()


def back(n_dp, ga, grads_gu, grads_d, ffn_sum, w_a, q, k, v, mixed, normed, *rest):
    length, width = ga.shape
    units = grads_gu.shape[1] // 2
    quarter = length // 4
    rows = width // 8
    q_cols = q.shape[1]
    cols = q_cols + 2 * HEAD
    vmem = pl.BlockSpec(memory_space=pltpu.VMEM)
    hbm = pl.BlockSpec(memory_space=pl.ANY)
    shape = jax.ShapeDtypeStruct
    pair = shape((quarter, width), BF16)
    ring = n_dp == 8
    return pl.pallas_call(
        functools.partial(back_kernel, n_dp),
        in_specs=[hbm] * 10 + [vmem] * 7,
        out_specs=[hbm] * 12,
        out_shape=[
            pair,
            pair,
            pair,
            pair,
            shape((rows, units), F32),
            shape((rows, units), F32),
            shape((rows, units), F32),
            shape((rows, q_cols), F32) if ring else shape((width, cols), BF16),
            shape((rows, 2 * HEAD), F32),
            shape((rows, q_cols), F32) if ring else shape((width, q_cols), BF16),
            shape((rows if ring else width, HEAD), F32),
            pair,
        ],
        scratch_shapes=[
            pltpu.VMEM((length, width), BF16),
            pltpu.VMEM(w_a.shape, BF16),
            pltpu.VMEM((length, q_cols), BF16),
            pltpu.VMEM((length, HEAD), BF16),
            pltpu.VMEM((length, HEAD), BF16),
            pltpu.VMEM((length, q_cols), BF16),
            pltpu.VMEM((length, q_cols), BF16),
            pltpu.VMEM((length, q_cols + 2 * HEAD), BF16),
            pltpu.VMEM((length, HEAD), F32),
            pltpu.VMEM((length, HEAD), F32),
            pltpu.VMEM((width, cols), BF16),
            pltpu.VMEM((width, q_cols), BF16),
            pltpu.VMEM((width, units), BF16),
            pltpu.VMEM((width, 2 * units), BF16),
            pltpu.VMEM((length // 2, width), BF16),
            pltpu.VMEM((quarter, width), BF16),
            pltpu.VMEM((quarter, width), BF16),
            pltpu.VMEM((6, rows, 2 * units), BF16),
            pltpu.VMEM((8, rows, cols), BF16),
            pltpu.VMEM((8, rows, q_cols), BF16),
            pltpu.VMEM((2, rows, units), BF16),
            pltpu.VMEM((rows, 2 * units), F32),
            pltpu.VMEM((rows, cols), F32),
            pltpu.VMEM((rows, q_cols), F32),
            pltpu.VMEM((rows, units), F32),
            pltpu.VMEM((8, width), F32),
            pltpu.VMEM((width, HEAD), F32),
            pltpu.VMEM((8, rows, HEAD), F32),
            pltpu.VMEM((rows, 3 * HEAD), BF16),
            pltpu.VMEM((rows, 3 * HEAD), BF16),
            pltpu.VMEM((rows, 3 * HEAD), BF16),
            pltpu.SemaphoreType.DMA((2, 40)),
            pltpu.SemaphoreType.DMA((2, 8)),
            pltpu.SemaphoreType.DMA((72,)),
        ],
        compiler_params=pltpu.CompilerParams(
            collective_id=2, has_side_effects=True, vmem_limit_bytes=60 * MIB
        ),
        cost_estimate=pl.CostEstimate(
            flops=14 * length * width * q_cols, bytes_accessed=64 * MIB, transcendentals=0
        ),
        name="back",
    )(ga, grads_gu, grads_d, ffn_sum, w_a, q, k, v, mixed, normed, *rest)[:11]


def final_kernel(
    own, near, far, ffn_far, out_part, tokens, grad_residual, gains, output, grad_tokens
):
    output[...] = (out_part[...] + ffn_far[...].astype(F32)).astype(BF16)
    rows = tokens[...].astype(F32)
    grad_n = own[...].astype(F32) + near[...].astype(F32) + far[...].astype(F32)
    scale = lax.rsqrt(jnp.mean(rows * rows, axis=-1, keepdims=True) + EPS)
    weighted = grad_n * gains[0:1, :]
    inner = jnp.mean(rows * weighted, axis=-1, keepdims=True)
    grad_tokens[...] = grad_residual[...] + scale * weighted - rows * (scale * scale * scale * inner)


def final(blocks, gains):
    quarter, width = blocks[0].shape
    size = 128
    row = pl.BlockSpec((size, width), lambda i: (i, 0))
    return pl.pallas_call(
        final_kernel,
        grid=(quarter // size,),
        in_specs=[row] * 7 + [pl.BlockSpec((8, width), lambda i: (0, 0))],
        out_specs=[row, row],
        out_shape=[
            jax.ShapeDtypeStruct((quarter, width), BF16),
            jax.ShapeDtypeStruct((quarter, width), F32),
        ],
        compiler_params=pltpu.CompilerParams(vmem_limit_bytes=62 * MIB),
        name="final",
    )(*blocks, gains)


def positions_of(segments):
    places = jnp.arange(segments.shape[0], dtype=jnp.int32)
    previous = jnp.concatenate([jnp.full((1,), -1, jnp.int32), segments[:-1]])
    starts = lax.cummax(jnp.where(segments != previous, places, 0), axis=0)
    return places - starts


def per_device(
    n_dp,
    tokens,
    w_query,
    w_keyval,
    w_out,
    w_gate,
    w_up,
    w_down,
    norm_gains,
    segment_ids,
    grad_output,
):
    t = lax.axis_index("tensor").astype(jnp.int32)
    quarter, width = tokens.shape
    length = 4 * quarter
    q_cols = w_query.shape[1]
    units = w_gate.shape[1]

    gain_cols = jnp.pad(norm_gains.T, ((0, 0), (0, HEAD - 2)))
    shard_a = jnp.concatenate([w_query, w_keyval, w_out.T, gain_cols], axis=1)
    shard_d = w_down.T
    shard_g = jnp.concatenate([w_gate, w_up], axis=1)
    if n_dp != 8:
        shard_a, shard_d, shard_g = (
            lax.all_gather(w, "dp", axis=0, tiled=True) for w in (shard_a, shard_d, shard_g)
        )

    turn = t ^ jnp.arange(4, dtype=jnp.int32)
    positions = positions_of(segment_ids).reshape(4, quarter)[turn].reshape(length)
    valid = (segment_ids != 0).reshape(4, quarter)[turn].reshape(length).astype(F32)
    inverse = 10000.0 ** (-jnp.arange(HEAD // 2, dtype=F32) / (HEAD // 2))
    inverse = jnp.concatenate([inverse, inverse])[None, :]
    pos3 = positions.reshape(length // BLK, 1, BLK)
    valid3 = valid.reshape(length // BLK, 1, BLK)

    (cos, sin, w_a, w_down_t, w_gu, gains, normed, q, k, v, mixed, lse, residual, n2, go_all, gh) = front(
        n_dp, tokens, grad_output, shard_a, shard_d, shard_g, pos3, valid3, inverse, q_cols
    )
    grads_gu, grads_d, grad_residual, gain_two, ga, ffn_sum, out_part = middle(
        n_dp, n2, gh, go_all, w_gu, w_down_t, residual, grad_output, gains
    )
    part_own, part_far, part_near, ffn_far, gate, up, down, grads_a, keyval, out_grads, gain_grads = back(
        n_dp, ga, grads_gu, grads_d, ffn_sum, w_a, q, k, v, mixed, normed,
        lse, pos3, valid3, cos, sin, gains, gain_two
    )
    query = grads_a
    if n_dp != 8:

        def spread(full):
            return lax.psum_scatter(full.astype(F32), "dp", scatter_dimension=0, tiled=True)

        down, gate, up, grads_a, out_grads, gain_grads = (
            spread(w)
            for w in (grads_d, grads_gu[:, :units], grads_gu[:, units:], grads_a, out_grads, gain_grads)
        )
        keyval, gain_grads = lax.psum((grads_a[:, q_cols:], gain_grads), "tensor")
        query = grads_a[:, :q_cols]
    blocks = (part_own, part_near, part_far, ffn_far, out_part, tokens, grad_residual)
    output, grad_tokens = final(blocks, gains)

    return (
        output,
        grad_tokens,
        query,
        keyval,
        out_grads.T,
        gate,
        up,
        down.T,
        gain_grads[:, :2].T,
    )


def solution(mesh):
    return jax.shard_map(
        functools.partial(per_device, mesh.shape["dp"]),
        mesh=mesh,
        in_specs=(
            P(("dp", "tensor"), None),
            P("dp", "tensor"),
            P("dp", None),
            P("tensor", "dp"),
            P("dp", "tensor"),
            P("dp", "tensor"),
            P("tensor", "dp"),
            P(None, "dp"),
            P("dp"),
            P(("dp", "tensor"), None),
        ),
        out_specs=(
            P(("dp", "tensor"), None),
            P(("dp", "tensor"), None),
            P("dp", "tensor"),
            P("dp", None),
            P("tensor", "dp"),
            P("dp", "tensor"),
            P("dp", "tensor"),
            P("tensor", "dp"),
            P(None, "dp"),
        ),
        check_vma=False,
    )
```

```python
import functools

import jax
import jax.numpy as jnp
from jax import lax
from jax.experimental import pallas as pl
from jax.experimental.pallas import tpu as pltpu
from jax.sharding import PartitionSpec as P

WINDOW = 1024
EPS = 1e-6
MASKED = -1e30
HEAD = 128
BLK = 256
LOG2E = 1.4426950408889634
F32 = jnp.float32
BF16 = jnp.bfloat16
MIB = 1 << 20
EARLY = 2

NT = (((1,), (1,)), ((), ()))
TN = (((0,), (0,)), ((), ()))


def dot(left, right):
    return jnp.dot(left, right, preferred_element_type=F32)


def dot_nt(left, right):
    return lax.dot_general(left, right, NT, preferred_element_type=F32)


def dot_tn(left, right):
    return lax.dot_general(left, right, TN, preferred_element_type=F32)


def stacked(block, heads):
    return jnp.concatenate([block[:, h * HEAD : (h + 1) * HEAD] for h in range(heads)], axis=0)


def partner(t, j):
    rem, div = lax.rem, lax.div
    two = jnp.int32(2)
    j = jnp.int32(j)
    return rem(div(t, two) + div(j, two), two) * 2 + rem(rem(t, two) + rem(j, two), two)


def block_rows(i):
    return pl.ds(pl.multiple_of(i * BLK, BLK), BLK)


def key_row(t, kb):
    per = 512 // BLK
    return pl.multiple_of((partner(t, lax.div(kb, per)) * per + lax.rem(kb, per)) * BLK, BLK)


def query_block(t, i):
    per = 512 // BLK
    i = jnp.int32(i)
    return partner(t, lax.div(i, per)) * per + lax.rem(i, per)


def tiled3(row, heads):
    return jnp.concatenate([row] * heads, axis=1)


def attend(t, i, q, k, v, pos, valid, mixed, lse):
    cols = q.shape[1]
    heads = cols // HEAD
    wide = heads * BLK
    qb = query_block(t, i)
    mine = pl.ds(pl.multiple_of(i * BLK, BLK), BLK)
    q3 = stacked(q[mine, :], heads)
    at = qb * BLK + lax.broadcasted_iota(jnp.int32, (1, BLK), 1)
    low = at - jnp.minimum(pos[i], WINDOW - 1)
    at3, low3 = tiled3(at, heads), tiled3(low, heads)
    factor = HEAD**-0.5 * LOG2E

    def step(kb, carry):
        peak, total, acc = carry
        row = key_row(t, kb)
        s = dot_nt(k[pl.ds(row, BLK), :], q3) * factor
        u = kb * BLK + lax.broadcasted_iota(jnp.int32, (BLK, wide), 0)
        s = jnp.where((u <= at3) & (u >= low3), s, MASKED)
        new_peak = jnp.maximum(peak, jnp.max(s, axis=0, keepdims=True))
        p = jnp.exp2(s - new_peak)
        shrink = jnp.exp2(peak - new_peak)
        total = total * shrink + jnp.sum(p, axis=0, keepdims=True)
        acc = acc * shrink + dot_tn(v[pl.ds(row, BLK), :], p.astype(BF16))
        return new_peak, total, acc

    peak, total, acc = lax.fori_loop(
        jnp.maximum(qb - WINDOW // BLK, 0),
        qb + 1,
        step,
        (
            jnp.full((1, wide), MASKED, F32),
            jnp.zeros((1, wide), F32),
            jnp.zeros((HEAD, wide), F32),
        ),
    )
    lse[i] = peak + jnp.log2(total)
    acc = acc * (tiled3(valid[i], heads) / total)
    mixed[mine, :] = jnp.concatenate(
        [acc[:, h * BLK : (h + 1) * BLK].T for h in range(heads)], axis=1
    ).astype(BF16)


def ring_device(p, n):
    p = lax.rem(p + n, jnp.int32(n))
    down = lax.div(p, jnp.int32(n // 2))
    return (1 - down) * 2 * p + down * (2 * (n - 1 - p) + 1)


def ring_place(d, n):
    z, y = lax.div(d, jnp.int32(2)), lax.rem(d, jnp.int32(2))
    return z + y * (n - 1 - 2 * z)


def send(src, dst, sems, at, device):
    return pltpu.make_async_remote_copy(
        src_ref=src,
        dst_ref=dst,
        send_sem=sems.at[0, at],
        recv_sem=sems.at[1, at],
        device_id=device,
        device_id_type=pl.DeviceIdType.MESH,
    )


class Ring:
    def __init__(self, shard, full, sems, first_sem, own, n, direction):
        self.shard, self.full, self.sems, self.at, self.own = shard, full, sems, first_sem, own
        self.n, self.dir = n, direction
        self.copies = {}

    def block(self, offset, place):
        rows = self.shard.shape[0]
        at = ring_device(place + offset * self.dir, self.n) * rows
        return self.full.at[pl.ds(pl.multiple_of(at, rows & -rows), rows), :]

    def begin(self, place):
        self.place = place
        if self.n == 8:
            target = self.block(0, place)
        else:
            target = self.full
        self.local = pltpu.make_async_copy(self.shard, target, self.own)
        self.local.start()
        self.start(1)

    def start(self, s):
        if self.n != 8:
            return
        for way in (0, 1):
            if s > self.n // 2 - way:
                continue
            sign = 1 - 2 * way
            block = self.block(-sign * (s - 1), self.place)
            device = ring_device(self.place + sign * self.dir, self.n)
            src = self.shard if s == 1 else block
            at = self.at + 2 * (s - 1) + way
            copy = send(src, block, self.sems, at, {"dp": device})
            copy.start()
            self.copies[s, way] = copy

    def arrived(self, s):
        for way in (0, 1):
            if (s, way) in self.copies:
                self.copies[s, way].wait_recv()

    def next(self, s):
        self.arrived(s)
        self.start(s + 1)

    def end(self):
        for copy in self.copies.values():
            copy.wait_send()
        self.local.wait()


class RingSum:
    def __init__(self, full, recv, sems, first_sem, n, direction, place, first_hop=1):
        self.full, self.recv, self.sems, self.at = full, recv, sems, first_sem
        self.n, self.dir, self.place, self.first_hop = n, direction, place, first_hop
        self.rows = full.shape[0] // n
        self.copies = {}

    def block(self, offset):
        at = ring_device(self.place + offset * self.dir, self.n) * self.rows
        return pl.ds(pl.multiple_of(at, self.rows & -self.rows), self.rows)

    def last(self, way):
        return self.n // 2 - way

    def slot(self, s, way):
        return way * (self.recv.shape[0] // 2) + s - self.first_hop

    def start(self, s, ways=(0, 1), source=None):
        for way in ways:
            if self.n == 8 and s <= self.last(way):
                sign = 1 - 2 * way
                device = ring_device(self.place + sign * self.dir, self.n)
                rows = self.block(sign * (self.last(way) + 1 - s))
                src = (self.full if source is None else source).at[rows, :]
                slot = self.slot(s, way)
                copy = send(src, self.recv.at[slot], self.sems, self.at + slot, {"dp": device})
                copy.start()
                self.copies[s, way] = copy

    def arrived(self, s, way):
        self.copies[s, way].wait_recv()
        return self.recv[self.slot(s, way)]

    def add(self, s, start=False):
        for way in (0, 1):
            if self.n == 8 and s < self.last(way):
                far = self.last(way)
                mine = self.block((1 - 2 * way) * (far - s))
                self.full[mine, :] = self.full[mine, :] + self.arrived(s, way)
                if start:
                    self.start(s + 1, (way,))

    def next(self, s):
        self.add(s, True)

    def close(self, way):
        if self.n == 8:
            mine = self.block(0)
            self.full[mine, :] = self.full[mine, :] + self.arrived(self.last(way), way)

    def result(self, ways=(0, 1)):
        acc = self.full[self.block(0), :].astype(F32)
        for way in ways:
            acc = acc + self.arrived(self.last(way), way).astype(F32)
        return acc

    def save(self, offsets, target, local):
        if self.n != 8:
            return []
        blocks = [self.block(offset) for offset in offsets]
        return [local(self.full.at[rows, :], target.at[rows, :]) for rows in blocks]

    def end(self):
        for copy in self.copies.values():
            copy.wait_send()


def front_kernel(
    n_dp,
    tokens,
    grad_output,
    shard_a,
    shard_d,
    shard_g,
    pos,
    valid,
    inverse,
    cos_out,
    sin_out,
    w_a_out,
    w_d_out,
    w_g,
    gains,
    normed_out,
    q_out,
    k_out,
    v_out,
    mixed_out,
    lse,
    residual_out,
    n2_out,
    go_out,
    gh_out,
    cos,
    sin,
    w_a,
    w_d,
    x4,
    normed,
    q,
    k,
    v,
    mixed,
    near_recv,
    far_recv,
    x_recv,
    sum_buf,
    n2_own,
    go_buf,
    gh_buf,
    res,
    ring_sems,
    pair_sems,
    local_sems,
):
    quarter, width = tokens.shape
    q_cols = q.shape[1]
    heads = q_cols // HEAD
    kv_at = q_cols + 2 * HEAD
    gain_at = kv_at + q_cols
    t = lax.axis_index("tensor").astype(jnp.int32)
    place = ring_place(lax.axis_index("dp").astype(jnp.int32), n_dp)
    near_id, far_id = {"tensor": partner(t, 1)}, {"tensor": partner(t, 2)}

    barrier = pltpu.get_barrier_semaphore()
    partners = [near_id, far_id]
    if n_dp == 8:
        partners += [{"dp": ring_device(place + 1, n_dp)}, {"dp": ring_device(place - 1, n_dp)}]
    for device in partners:
        pl.semaphore_signal(barrier, inc=1, device_id=device, device_id_type=pl.DeviceIdType.MESH)
    pl.semaphore_wait(barrier, len(partners))

    def rows_of(ref, j, size=1):
        return ref.at[pl.ds(j * quarter, size * quarter), :]

    used = [0]

    def local(src, dst):
        copy = pltpu.make_async_copy(src, dst, local_sems.at[used[0]])
        used[0] += 1
        copy.start()
        return copy

    ring_a = Ring(shard_a, w_a, ring_sems, 0, local_sems.at[24], n_dp, 1)
    ring_d = Ring(shard_d, w_d, ring_sems, 8, local_sems.at[25], n_dp, 1)
    ring_g = Ring(shard_g, w_g, ring_sems, 16, local_sems.at[26], n_dp, -1)

    ring_a.begin(place)
    x_far = send(tokens, rows_of(x4, 2), pair_sems, 0, far_id)
    x_far.start()
    x_near = send(tokens, rows_of(x4, 1), pair_sems, 1, near_id)
    x_near.start()
    x_own = local(tokens, rows_of(x4, 0))
    go_in = local(grad_output, res)
    def tables(i, carry):
        places = jnp.broadcast_to(pos[i].astype(F32), (HEAD, BLK)).T
        angles = places * inverse[...]
        sine = jnp.sin(angles)
        lane = lax.broadcasted_iota(jnp.int32, sine.shape, 1)
        cos[block_rows(i), :] = jnp.cos(angles)
        sin[block_rows(i), :] = jnp.where(lane < HEAD // 2, -sine, sine)
        return carry

    count = pos.shape[0]
    for s in (1, 2, 3):
        lax.fori_loop(count * (s - 1) // 3, count * s // 3, tables, 0)
        ring_a.next(s)
    ring_d.begin(place)
    ring_g.begin(place)
    ring_a.arrived(4)
    ring_a.local.wait()

    gain_rows = w_a[:, gain_at : gain_at + HEAD].astype(F32).T
    gains[...] = gain_rows[:8]

    def project(i, carry):
        mine = pl.ds(pl.multiple_of(i * BLK, BLK), BLK)
        rows = x4[mine, :].astype(F32)
        scale = lax.rsqrt(jnp.mean(rows * rows, axis=-1, keepdims=True) + EPS)
        n = (rows * scale * gains[0:1, :]).astype(BF16)
        normed[mine, :] = n
        y = dot(n, w_a[:, :kv_at])
        c, s = cos[mine, :], sin[mine, :]

        def turned(a):
            return (a * c + pltpu.roll(a, HEAD // 2, 1) * s).astype(BF16)

        q[mine, :] = jnp.concatenate(
            [turned(y[:, h * HEAD : (h + 1) * HEAD]) for h in range(heads)], axis=1
        )
        k[mine, :] = turned(y[:, q_cols : q_cols + HEAD])
        v[mine, :] = y[:, q_cols + HEAD : kv_at].astype(BF16)
        return carry

    per = quarter // BLK
    x_own.wait()
    x_near.wait_recv()
    lax.fori_loop(0, 2 * per, project, 0)
    x_far.wait_recv()
    x_last = send(rows_of(x4, 2), rows_of(x4, 3), pair_sems, 2, near_id)
    x_last.start()
    go_in.wait()
    go_buf[...] = res[...].astype(BF16)
    go_far = send(go_buf, rows_of(go_out, 2), pair_sems, 3, far_id)
    go_far.start()
    go_near = send(go_buf, rows_of(go_out, 1), pair_sems, 4, near_id)
    go_near.start()
    go_own = local(go_buf, rows_of(go_out, 0))
    x_last.wait_recv()
    lax.fori_loop(2 * per, 4 * per, project, 0)
    copies = [
        local(cos, cos_out),
        local(sin, sin_out),
        local(normed, normed_out),
        local(q, q_out),
        local(k, k_out),
        local(v, v_out),
        local(w_a, w_a_out),
    ]

    def attention(i, carry):
        attend(t, i, q, k, v, pos, valid, mixed, lse)
        return carry

    part = x4

    def out_product(i, carry):
        mine = pl.ds(pl.multiple_of(i * BLK, BLK), BLK)
        part[mine, :] = dot_nt(mixed[mine, :], w_a[:, kv_at:gain_at]).astype(BF16)
        return carry

    x_last.wait_send()
    lax.fori_loop(2 * per, 4 * per, attention, 0)
    ring_d.next(1)
    lax.fori_loop(2 * per, 4 * per, out_product, 0)
    part_far = send(rows_of(part, 3), far_recv, pair_sems, 5, near_id)
    part_far.start()
    lax.fori_loop(0, 1, attention, 0)
    part_far.wait_recv()
    sum_buf[...] = (part[pl.ds(2 * quarter, quarter), :].astype(F32) + far_recv[...].astype(F32)).astype(BF16)
    sum_far = send(sum_buf, x_recv, pair_sems, 6, far_id)
    sum_far.start()
    ring_g.next(1)
    lax.fori_loop(1, 2 * per, attention, 0)
    lax.fori_loop(0, 2 * per, out_product, 0)
    part_near = send(rows_of(part, 1), near_recv, pair_sems, 7, near_id)
    part_near.start()
    copies.append(local(mixed, mixed_out))
    ring_d.next(2)
    ring_d.next(3)
    ring_g.next(2)
    go_far.wait_recv()
    go_last = send(rows_of(go_out, 2), rows_of(go_out, 3), pair_sems, 8, near_id)
    go_last.start()
    part_near.wait_recv()
    sum_far.wait_recv()

    res[...] = (
        tokens[...].astype(F32)
        + part[pl.ds(0, quarter), :].astype(F32)
        + near_recv[...].astype(F32)
        + x_recv[...].astype(F32)
    )
    scale_two = lax.rsqrt(jnp.mean(res[...] * res[...], axis=-1, keepdims=True) + EPS)
    n2_own[...] = (res[...] * scale_two * gains[1:2, :]).astype(BF16)
    n2_far = send(n2_own, rows_of(n2_out, 2), pair_sems, 9, far_id)
    n2_far.start()
    n2_near = send(n2_own, rows_of(n2_out, 1), pair_sems, 10, near_id)
    n2_near.start()
    copies.append(local(n2_own, rows_of(n2_out, 0)))
    copies.append(local(res, residual_out))

    ring_d.arrived(4)
    ring_d.local.wait()
    copies.append(local(w_d, w_d_out))
    go_far.wait_send()
    go_near.wait_send()
    go_own.wait()

    def grad_hidden(i, carry):
        mine = pl.ds(pl.multiple_of(i * BLK, BLK), BLK)
        gh_buf[mine, :] = dot(go_buf[mine, :], w_d[...]).astype(BF16)
        return carry

    for j in range(4):
        if j == 1:
            go_near.wait_recv()
        if j == 3:
            go_last.wait_recv()
        if j > 0:
            load = local(rows_of(go_out, j), go_buf)
            load.wait()
        if j > 0:
            store.wait()
        lax.fori_loop(0, per, grad_hidden, 0)
        store = local(gh_buf, rows_of(gh_out, j))
        if j == 1:
            ring_g.next(3)

    n2_far.wait_recv()
    n2_last = send(rows_of(n2_out, 2), rows_of(n2_out, 3), pair_sems, 11, near_id)
    n2_last.start()
    ring_g.arrived(4)
    store.wait()
    for copy in copies:
        copy.wait()
    for copy in (x_far, x_near, part_far, sum_far, part_near, go_last, n2_far, n2_near, n2_last):
        copy.wait_send()
    n2_near.wait_recv()
    n2_last.wait_recv()
    ring_a.copies and [c.wait_send() for c in ring_a.copies.values()]
    ring_d.copies and [c.wait_send() for c in ring_d.copies.values()]
    ring_g.end()


def front(n_dp, tokens, grad_output, shard_a, shard_d, shard_g, pos, valid, inverse, q_cols):
    quarter, width = tokens.shape
    length = 4 * quarter
    heads = q_cols // HEAD
    units = shard_d.shape[1]
    cols_a = shard_a.shape[1]
    vmem = pl.BlockSpec(memory_space=pltpu.VMEM)
    hbm = pl.BlockSpec(memory_space=pl.ANY)
    blocks = length // BLK

    def out(rows, cols, kind=BF16):
        return jax.ShapeDtypeStruct((rows, cols), kind)

    return pl.pallas_call(
        functools.partial(front_kernel, n_dp),
        in_specs=[vmem, hbm, hbm, hbm, hbm, vmem, vmem, vmem],
        out_specs=[hbm, hbm, hbm, hbm, hbm, vmem, hbm, hbm, hbm, hbm, hbm, vmem, hbm, hbm, hbm, hbm],
        out_shape=[
            out(length, HEAD, F32),
            out(length, HEAD, F32),
            out(width, cols_a),
            out(width, units),
            out(width, 2 * units),
            out(8, width, F32),
            out(length, width),
            out(length, q_cols),
            out(length, HEAD),
            out(length, HEAD),
            out(length, q_cols),
            jax.ShapeDtypeStruct((blocks, 1, heads * BLK), F32),
            out(quarter, width, F32),
            out(length, width),
            out(length, width),
            out(length, units),
        ],
        scratch_shapes=[
            pltpu.VMEM((length, HEAD), F32),
            pltpu.VMEM((length, HEAD), F32),
            pltpu.VMEM((width, cols_a), BF16),
            pltpu.VMEM((width, units), BF16),
            pltpu.VMEM((length, width), BF16),
            pltpu.VMEM((length, width), BF16),
            pltpu.VMEM((length, q_cols), BF16),
            pltpu.VMEM((length, HEAD), BF16),
            pltpu.VMEM((length, HEAD), BF16),
            pltpu.VMEM((length, q_cols), BF16),
            pltpu.VMEM((quarter, width), BF16),
            pltpu.VMEM((quarter, width), BF16),
            pltpu.VMEM((quarter, width), BF16),
            pltpu.VMEM((quarter, width), BF16),
            pltpu.VMEM((quarter, width), BF16),
            pltpu.VMEM((quarter, width), BF16),
            pltpu.VMEM((quarter, units), BF16),
            pltpu.VMEM((quarter, width), F32),
            pltpu.SemaphoreType.DMA((2, 24)),
            pltpu.SemaphoreType.DMA((2, 12)),
            pltpu.SemaphoreType.DMA((32,)),
        ],
        compiler_params=pltpu.CompilerParams(
            collective_id=0, has_side_effects=True, vmem_limit_bytes=58 * MIB
        ),
        cost_estimate=pl.CostEstimate(
            flops=12 * length * width * q_cols, bytes_accessed=64 * MIB, transcendentals=0
        ),
        name="front",
    )(tokens, grad_output, shard_a, shard_d, shard_g, pos, valid, inverse)


def attend_back(t, i, q, do, mixed, lse, k, v, pos, valid, cos, sin, dqkv, dk_acc, dv_acc):
    cols = q.shape[1]
    heads = cols // HEAD
    wide = heads * BLK
    qb = query_block(t, i)
    mine = block_rows(i)
    q3 = stacked(q[mine, :], heads)
    do3 = stacked(do[mine, :], heads)
    centre3 = do3.astype(F32) * stacked(mixed[mine, :], heads).astype(F32)
    centre = jnp.sum(centre3.T, axis=0, keepdims=True)
    at = qb * BLK + lax.broadcasted_iota(jnp.int32, (1, BLK), 1)
    low = jnp.where(valid[i] > 0.0, at - jnp.minimum(pos[i], WINDOW - 1), at + 1)
    at3, low3 = tiled3(at, heads), tiled3(low, heads)
    total = lse[i]
    factor = HEAD**-0.5 * LOG2E

    def step(kb, acc):
        row = key_row(t, kb)
        kblk = k[pl.ds(row, BLK), :]
        vblk = v[pl.ds(row, BLK), :]
        s = dot_nt(kblk, q3) * factor - total
        u = kb * BLK + lax.broadcasted_iota(jnp.int32, (BLK, wide), 0)
        p = jnp.exp2(jnp.where((u <= at3) & (u >= low3), s, MASKED))
        gp = dot_nt(vblk, do3)
        ds = (p * (gp - centre)).astype(BF16)
        dv_acc[pl.ds(row, BLK), :] += dot(p.astype(BF16), do3)
        dk_acc[pl.ds(row, BLK), :] += dot(ds, q3)
        return acc + dot_tn(kblk, ds)

    acc = lax.fori_loop(
        jnp.maximum(qb - WINDOW // BLK, 0), qb + 1, step, jnp.zeros((HEAD, wide), F32)
    )
    scale = HEAD**-0.5
    c, sn = cos[mine, :] * scale, sin[mine, :] * scale

    def turned(a):
        return (a * c - pltpu.roll(a, HEAD // 2, 1) * sn).astype(BF16)

    dqkv[mine, :cols] = jnp.concatenate(
        [turned(acc[:, h * BLK : (h + 1) * BLK].T) for h in range(heads)], axis=1
    )


def gated(y, gh, half):
    gate, up = y[:, :half], y[:, half:]
    root = (2.0 / jnp.pi) ** 0.5
    square = gate * gate
    th = jnp.tanh(root * gate * (1.0 + 0.044715 * square))
    one = 0.5 * (1.0 + th)
    act = gate * one
    slope = one + 0.5 * gate * (1.0 - th * th) * (root * (1.0 + 3.0 * 0.044715 * square))
    return (act * up).astype(BF16), (gh * up * slope).astype(BF16), (gh * act).astype(BF16)


def greet(partners):
    barrier = pltpu.get_barrier_semaphore()
    for device in partners:
        pl.semaphore_signal(barrier, inc=1, device_id=device, device_id_type=pl.DeviceIdType.MESH)
    pl.semaphore_wait(barrier, len(partners))


def neighbours(n_dp, t, place):
    near_id, far_id = {"tensor": partner(t, 1)}, {"tensor": partner(t, 2)}
    others = []
    if n_dp == 8:
        others = [{"dp": ring_device(place + 1, n_dp)}, {"dp": ring_device(place - 1, n_dp)}]
    return near_id, far_id, [near_id, far_id] + others


class Local:
    def __init__(self, sems):
        self.sems, self.used = sems, 0

    def __call__(self, src, dst):
        copy = pltpu.make_async_copy(src, dst, self.sems.at[self.used])
        self.used += 1
        copy.start()
        return copy


def middle_kernel(
    n_dp,
    n2_in,
    gh_in,
    go_in,
    w_gu_in,
    w_d_in,
    residual,
    grad_output,
    gains,
    grads_gu_out,
    down_out,
    grad_residual,
    gain_two,
    ga_out,
    ffn_sum_out,
    out_part,
    far_recv,
    x_recv,
    near_recv,
    far_recv2,
    near_recv2,
    w_gu,
    n2,
    go,
    hidden,
    dgu,
    part,
    grads_d,
    grads_gu,
    stage,
    sum_buf,
    ga_own,
    recv_d,
    recv_g,
    rows_a,
    rows_b,
    ring_sems,
    pair_sems,
    local_sems,
):
    length, width = n2.shape
    units = hidden.shape[1]
    quarter = length // 4
    half = length // 2
    t = lax.axis_index("tensor").astype(jnp.int32)
    place = ring_place(lax.axis_index("dp").astype(jnp.int32), n_dp)
    near_id, far_id, partners = neighbours(n_dp, t, place)
    local = Local(local_sems)
    ring_d = RingSum(grads_d, recv_d, ring_sems, 0, n_dp, -1, place)
    ring_g = RingSum(grads_gu, recv_g, ring_sems, 8, n_dp, 1, place)

    far_rows, near_rows = pl.ds(half, half), pl.ds(0, half)
    load_w = local(w_gu_in, w_gu)
    load_far = [local(n2_in.at[far_rows, :], n2.at[far_rows, :]), local(gh_in.at[far_rows, :], hidden.at[far_rows, :])]
    load_near = [local(n2_in.at[near_rows, :], n2.at[near_rows, :]), local(gh_in.at[near_rows, :], hidden.at[near_rows, :])]
    greet(partners)

    def ffn(i, carry):
        mine = block_rows(i)
        y = dot(n2[mine, :], w_gu[...])
        gh = hidden[mine, :].astype(F32)
        hidden[mine, :], dgu[mine, :units], dgu[mine, units:] = gated(y, gh, units)
        return carry

    def back(first):
        def body(i, carry):
            part[block_rows(i), :] = dot_nt(dgu[block_rows(i + first), :], w_gu[...]).astype(BF16)
            return carry

        return body

    def fetch(src, dst):
        local(src, dst).wait()

    upper = pl.ds(quarter, quarter)
    per = half // BLK
    load_w.wait()
    for copy in load_far:
        copy.wait()
    lax.fori_loop(per, 2 * per, ffn, 0)
    lax.fori_loop(per // 2, per, back(per), 0)
    part_far = send(part.at[upper, :], far_recv, pair_sems, 0, near_id)
    part_far.start()
    lax.fori_loop(0, per // 2, back(per), 0)
    for copy in load_near:
        copy.wait()
    part_far.wait_recv()
    fetch(far_recv, stage)
    sum_buf[...] = (part[:quarter, :].astype(F32) + stage[...].astype(F32)).astype(BF16)
    sum_far = send(sum_buf, x_recv, pair_sems, 1, far_id)
    sum_far.start()
    blocks = width // BLK

    def load_go(i):
        return local(go_in.at[:, pl.ds(i * BLK, BLK)], go.at[i % 2])

    size = rows_a.shape[1]
    steps = quarter // size

    def rows_at(i):
        return pl.ds(i * size, size)

    def load_rows(i):
        return (
            local(residual.at[rows_at(i), :], rows_a.at[i % 2]),
            local(grad_output.at[rows_at(i), :], rows_b.at[i % 2]),
        )

    coming = load_go(0)
    coming_rows = load_rows(0)
    lax.fori_loop(0, per, ffn, 0)
    part_far.wait_send()
    lax.fori_loop(0, per, back(0), 0)
    part_near = send(part.at[upper, :], near_recv, pair_sems, 2, near_id)
    part_near.start()
    load_d = local(w_d_in, w_gu.at[:, :units])

    for i in range(blocks):
        coming.wait()
        if i + 1 < blocks:
            coming = load_go(i + 1)
        grads_d[i * BLK : (i + 1) * BLK, :] = dot_tn(go[i % 2], hidden[...]).astype(BF16)
    ring_d.start(1)

    def gu_grad(i, carry):
        grads_gu[block_rows(i), :] = dot_tn(n2[:, block_rows(i)], dgu[...]).astype(BF16)
        return carry

    part_near.wait_recv()
    fetch(near_recv, stage)
    lax.fori_loop(0, EARLY, gu_grad, 0)
    gain_two[...] = jnp.zeros_like(gain_two)
    sum_far.wait_send()
    sum_far.wait_recv()
    fetch(x_recv, sum_buf)
    stores = []
    ga_far = []
    for i in range(steps):
        for copy in coming_rows:
            copy.wait()
        if i + 1 < steps:
            if i > 0:
                stores[-1].wait()
            coming_rows = load_rows(i + 1)
        mine = slice(i * size, (i + 1) * size)
        rows = rows_a[i % 2]
        grad_n = part[mine, :].astype(F32) + stage[mine, :].astype(F32) + sum_buf[mine, :].astype(F32)
        scale = lax.rsqrt(jnp.mean(rows * rows, axis=-1, keepdims=True) + EPS)
        weighted = grad_n * gains[1:2, :]
        inner = jnp.mean(rows * weighted, axis=-1, keepdims=True)
        grad = rows_b[i % 2] + scale * weighted - rows * (scale * scale * scale * inner)
        rows_b[i % 2] = grad
        ga_own[mine, :] = grad.astype(BF16)
        gain_two[0:1, :] += jnp.sum(grad_n * rows * scale, axis=0, keepdims=True)
        stores.append(local(rows_b.at[i % 2], grad_residual.at[rows_at(i), :]))
        if i % (steps // 2) == steps // 2 - 1:
            piece = len(ga_far)
            at = piece * quarter // 2
            ga_far.append(
                send(
                    ga_own.at[pl.ds(at, quarter // 2), :],
                    ga_out.at[pl.ds(2 * quarter + at, quarter // 2), :],
                    pair_sems,
                    (3, 8)[piece],
                    far_id,
                )
            )
            ga_far[piece].start()

    def quarter_of(ref, j):
        return ref.at[pl.ds(j * quarter, quarter), :]

    ga_near = send(ga_own, quarter_of(ga_out, 1), pair_sems, 4, near_id)
    ga_near.start()
    stores_late = [local(ga_own, quarter_of(ga_out, 0))]
    ring_d.next(1)
    lax.fori_loop(EARLY, blocks, gu_grad, 0)
    ring_g.start(1)
    save_gu = local(grads_gu, grads_gu_out)
    ring_d.next(2)
    save_d = local(grads_d, down_out)
    part_near.wait_send()
    load_d.wait()

    def down_product(first):
        def body(i, carry):
            part[block_rows(i), :] = dot_nt(hidden[block_rows(i + first), :], w_gu[:, :units]).astype(BF16)
            return carry

        return body

    lax.fori_loop(0, per, down_product(per), 0)
    part_far2 = send(part.at[upper, :], far_recv2, pair_sems, 5, near_id)
    part_far2.start()
    part_far2.wait_recv()
    fetch(far_recv2, stage)
    sum_buf[...] = (part[:quarter, :].astype(F32) + stage[...].astype(F32)).astype(BF16)
    stores_late.append(local(sum_buf, ffn_sum_out))
    part_far2.wait_send()
    lax.fori_loop(0, per, down_product(0), 0)
    part_near2 = send(part.at[upper, :], near_recv2, pair_sems, 6, near_id)
    part_near2.start()
    part_near2.wait_recv()
    fetch(near_recv2, stage)
    for copy in stores[-2:]:
        copy.wait()
    stores = []
    coming = local(residual.at[rows_at(0), :], rows_a.at[0])
    for i in range(steps):
        coming.wait()
        if i + 1 < steps:
            if i > 0:
                stores[-1].wait()
            coming = local(residual.at[rows_at(i + 1), :], rows_a.at[(i + 1) % 2])
        mine = slice(i * size, (i + 1) * size)
        rows_a[i % 2] = rows_a[i % 2] + part[mine, :].astype(F32) + stage[mine, :].astype(F32)
        stores.append(local(rows_a.at[i % 2], out_part.at[rows_at(i), :]))
    stores_late += stores[-2:]

    ga_last = []
    for piece in (0, 1):
        ga_far[piece].wait_recv()
        at = piece * quarter // 2
        ga_last.append(
            send(
                ga_out.at[pl.ds(2 * quarter + at, quarter // 2), :],
                ga_out.at[pl.ds(3 * quarter + at, quarter // 2), :],
                pair_sems,
                (7, 9)[piece],
                near_id,
            )
        )
        ga_last[piece].start()
    save_d.wait()
    ring_d.add(3)
    ring_d.close(1)
    stores_late += ring_d.save((1, 0), down_out, local)
    save_gu.wait()
    ring_g.add(1)
    stores_late += ring_g.save((3, -2), grads_gu_out, local)
    ring_d.end()
    ring_g.end()
    ga_near.wait_recv()
    for copy in ga_last:
        copy.wait_recv()
    for copy in stores_late:
        copy.wait()
    for copy in (*ga_far, ga_near, *ga_last, part_near2):
        copy.wait_send()


def middle(n_dp, n2, gh, go, w_gu, w_d, residual, grad_output, gains):
    length, width = n2.shape
    units = gh.shape[1]
    quarter = length // 4
    rows = width // 8
    vmem = pl.BlockSpec(memory_space=pltpu.VMEM)
    hbm = pl.BlockSpec(memory_space=pl.ANY)
    shape = jax.ShapeDtypeStruct
    pair = shape((quarter, width), BF16)
    return pl.pallas_call(
        functools.partial(middle_kernel, n_dp),
        in_specs=[hbm] * 7 + [vmem],
        out_specs=[hbm] * 3 + [vmem] + [hbm] * 8,
        out_shape=[
            shape((width, 2 * units), BF16),
            shape((width, units), BF16),
            shape((quarter, width), F32),
            shape((8, width), F32),
            shape((length, width), BF16),
            pair,
            shape((quarter, width), F32),
            pair,
            pair,
            pair,
            pair,
            pair,
        ],
        scratch_shapes=[
            pltpu.VMEM((width, 2 * units), BF16),
            pltpu.VMEM((length, width), BF16),
            pltpu.VMEM((2, length, BLK), BF16),
            pltpu.VMEM((length, units), BF16),
            pltpu.VMEM((length, 2 * units), BF16),
            pltpu.VMEM((length // 2, width), BF16),
            pltpu.VMEM((width, units), BF16),
            pltpu.VMEM((width, 2 * units), BF16),
            pltpu.VMEM((quarter, width), BF16),
            pltpu.VMEM((quarter, width), BF16),
            pltpu.VMEM((quarter, width), BF16),
            pltpu.VMEM((6, rows, units), BF16),
            pltpu.VMEM((2, rows, 2 * units), BF16),
            pltpu.VMEM((2, 128, width), F32),
            pltpu.VMEM((2, 128, width), F32),
            pltpu.SemaphoreType.DMA((2, 16)),
            pltpu.SemaphoreType.DMA((2, 10)),
            pltpu.SemaphoreType.DMA((72,)),
        ],
        compiler_params=pltpu.CompilerParams(
            collective_id=1, has_side_effects=True, vmem_limit_bytes=63 * MIB
        ),
        cost_estimate=pl.CostEstimate(
            flops=14 * length * width * units, bytes_accessed=64 * MIB, transcendentals=0
        ),
        name="middle",
    )(n2, gh, go, w_gu, w_d, residual, grad_output, gains)[:7]


def back_kernel(
    n_dp,
    ga_in,
    grads_gu_in,
    grads_d_in,
    ffn_sum,
    w_a_in,
    q_in,
    k_in,
    v_in,
    mixed_in,
    normed_in,
    lse,
    pos,
    valid,
    cos,
    sin,
    gains,
    gain_two,
    part_own,
    x_recv,
    near_recv,
    x_recv2,
    gate_out,
    up_out,
    down_out,
    grads_a_out,
    keyval_out,
    out_out,
    gain_out,
    far_recv,
    acts,
    w_a,
    q,
    k,
    v,
    mixed,
    do,
    dqkv,
    dk_acc,
    dv_acc,
    grads_a,
    grads_o,
    grads_d,
    grads_gu,
    part,
    stage,
    sum_buf,
    recv_g,
    recv_a,
    recv_o,
    recv_d,
    result_gu,
    result_a,
    result_o,
    result_d,
    gain_acc,
    gain_cols,
    recv_s,
    small,
    small_near,
    small_far,
    ring_sems,
    pair_sems,
    local_sems,
):
    length, width = acts.shape
    quarter = length // 4
    half = length // 2
    q_cols = q.shape[1]
    kv_at = q_cols + 2 * HEAD
    out_at = kv_at + q_cols
    units = grads_gu.shape[1] // 2
    ring = n_dp == 8
    t = lax.axis_index("tensor").astype(jnp.int32)
    place = ring_place(lax.axis_index("dp").astype(jnp.int32), n_dp)
    near_id, far_id, partners = neighbours(n_dp, t, place)
    local = Local(local_sems)
    ring_g = RingSum(grads_gu, recv_g, ring_sems, 0, n_dp, 1, place, 2)
    ring_a = RingSum(grads_a, recv_a, ring_sems, 8, n_dp, -1, place)
    ring_o = RingSum(grads_o, recv_o, ring_sems, 24, n_dp, -1, place)
    ring_d = RingSum(grads_d, recv_d, ring_sems, 32, n_dp, -1, place, 4)
    ring_s = RingSum(gain_cols, recv_s, ring_sems, 16, n_dp, 1, place)

    load_ga, load_w, load_mixed = local(ga_in, acts), local(w_a_in, w_a), local(mixed_in, mixed)
    loads = [local(src, dst) for src, dst in ((q_in, q), (k_in, k), (v_in, v))]
    greet(partners)
    ring_g.start(2, source=grads_gu_in)
    ring_d.start(4, source=grads_d_in)
    sum_far2 = send(ffn_sum, x_recv2, pair_sems, 0, far_id)
    sum_far2.start()
    if ring:
        loads += [local(grads_gu_in, grads_gu), local(grads_d_in, grads_d)]
    load_ga.wait()
    load_w.wait()

    def grad_mixed(i, carry):
        do[block_rows(i), :] = dot(acts[block_rows(i), :], w_a[:, kv_at:out_at]).astype(BF16)
        return carry

    def out_grad(i, carry):
        grads_o[block_rows(i), :] = dot_tn(acts[:, block_rows(i)], mixed[...]).astype(BF16)
        return carry

    blocks = length // BLK
    lax.fori_loop(0, blocks, grad_mixed, 0)
    load_mixed.wait()
    lax.fori_loop(0, width // BLK, out_grad, 0)
    ring_o.start(1)
    load_normed = local(normed_in, acts)
    for copy in loads:
        copy.wait()

    dk_acc[...] = jnp.zeros_like(dk_acc)
    dv_acc[...] = jnp.zeros_like(dv_acc)

    def attention(i, carry):
        attend_back(t, i, q, do, mixed, lse, k, v, pos, valid, cos, sin, dqkv, dk_acc, dv_acc)
        return carry

    lax.fori_loop(0, blocks * 3 // 4, attention, 0)
    ring_g.next(2)
    ring_o.next(1)
    lax.fori_loop(blocks * 3 // 4, blocks, attention, 0)
    a = dk_acc[...] * HEAD**-0.5
    dqkv[:, q_cols : q_cols + HEAD] = (a * cos[...] - pltpu.roll(a, HEAD // 2, 1) * sin[...]).astype(BF16)
    dqkv[:, q_cols + HEAD : kv_at] = dv_acc[...].astype(BF16)
    load_normed.wait()

    gain_acc[...] = jnp.zeros_like(gain_acc)

    def grad_normed(first):
        def body(i, carry):
            mine = block_rows(i + first)
            y = dot_nt(dqkv[mine, :], w_a[:, :kv_at])
            part[block_rows(i), :] = y.astype(BF16)
            gain_acc[0:1, :] += jnp.sum(y * acts[mine, :].astype(F32), axis=0, keepdims=True)
            return carry

        return body

    def fetch(src, dst):
        local(src, dst).wait()

    upper = pl.ds(quarter, quarter)
    per = half // BLK
    lax.fori_loop(0, per, grad_normed(per), 0)
    part_far = send(part.at[upper, :], far_recv, pair_sems, 1, near_id)
    part_far.start()
    ring_o.next(2)

    def qkv_grad(i, carry):
        grads_a[block_rows(i), :] = dot_tn(acts[:, block_rows(i)], dqkv[...]).astype(BF16)
        return carry

    lax.fori_loop(0, width // BLK, qkv_grad, 0)
    ring_a.start(1)
    ring_g.next(3)
    part_far.wait_recv()
    fetch(far_recv, stage)
    sum_buf[...] = (part[:quarter, :].astype(F32) + stage[...].astype(F32)).astype(BF16)
    sum_far = send(sum_buf, x_recv, pair_sems, 2, far_id)
    sum_far.start()
    part_far.wait_send()
    lax.fori_loop(0, per, grad_normed(0), 0)
    part_near = send(part.at[upper, :], near_recv, pair_sems, 3, near_id)
    part_near.start()
    stores = [local(part.at[pl.ds(0, quarter), :], part_own)]
    ring_o.next(3)

    both = jnp.concatenate(
        [gain_acc[0:1, :] / gains[0:1, :], gain_two[0:1, :], jnp.zeros((HEAD - 2, width), F32)], axis=0
    )
    gain_cols[...] = both.T
    ring_s.start(1)
    ring_a.next(1)
    ring_s.next(1)
    if ring:
        result_d[...] = ring_d.result((0,))
        stores.append(local(result_d, down_out))
    ring_a.next(2)
    ring_s.next(2)
    if ring:
        result_o[...] = ring_o.result()
        stores.append(local(result_o, out_out))
    ring_a.next(3)
    ring_s.next(3)
    if ring:
        result_gu[...] = ring_g.result()
        stores += [local(result_gu.at[:, :units], gate_out), local(result_gu.at[:, units:], up_out)]

    if ring:
        shard = ring_a.result()
        result_a[:, :q_cols] = shard[:, :q_cols]
        small[:, : 2 * HEAD] = shard[:, q_cols:kv_at].astype(BF16)
        small[:, 2 * HEAD :] = ring_s.result().astype(BF16)
        small_one = send(small, small_near, pair_sems, 4, near_id)
        small_one.start()
        small_one.wait_send()
        small_one.wait_recv()
        small[...] = (small[...].astype(F32) + small_near[...].astype(F32)).astype(BF16)
        small_two = send(small, small_far, pair_sems, 5, far_id)
        small_two.start()
        small_two.wait_send()
        small_two.wait_recv()
        both = small[...].astype(F32) + small_far[...].astype(F32)
        result_a[:, q_cols:kv_at] = both[:, : 2 * HEAD]
        ring_s.end()
        gain_cols[: both.shape[0], :] = both[:, 2 * HEAD :]
        stores.append(local(result_a.at[:, :q_cols], grads_a_out))
        stores.append(local(result_a.at[:, q_cols:], keyval_out))
        stores.append(local(gain_cols.at[pl.ds(0, both.shape[0]), :], gain_out))
    else:
        stores.append(local(grads_a, grads_a_out))
        stores.append(local(result_a.at[:, q_cols:], keyval_out))
        stores.append(local(grads_o, out_out))
        stores.append(local(gain_cols, gain_out))
    for copy in stores:
        copy.wait()
    for each in (ring_g, ring_a, ring_o, ring_d):
        each.end()
    for copy in (sum_far2, part_near, sum_far):
        copy.wait_send()
    sum_far2.wait_recv()
    part_near.wait_recv()
    sum_far.wait_recv()


def back(n_dp, ga, grads_gu, grads_d, ffn_sum, w_a, q, k, v, mixed, normed, *rest):
    length, width = ga.shape
    units = grads_gu.shape[1] // 2
    quarter = length // 4
    rows = width // 8
    q_cols = q.shape[1]
    cols = q_cols + 2 * HEAD
    vmem = pl.BlockSpec(memory_space=pltpu.VMEM)
    hbm = pl.BlockSpec(memory_space=pl.ANY)
    shape = jax.ShapeDtypeStruct
    pair = shape((quarter, width), BF16)
    ring = n_dp == 8
    return pl.pallas_call(
        functools.partial(back_kernel, n_dp),
        in_specs=[hbm] * 10 + [vmem] * 7,
        out_specs=[hbm] * 12,
        out_shape=[
            pair,
            pair,
            pair,
            pair,
            shape((rows, units), F32),
            shape((rows, units), F32),
            shape((rows, units), F32),
            shape((rows, q_cols), F32) if ring else shape((width, cols), BF16),
            shape((rows, 2 * HEAD), F32),
            shape((rows, q_cols), F32) if ring else shape((width, q_cols), BF16),
            shape((rows if ring else width, HEAD), F32),
            pair,
        ],
        scratch_shapes=[
            pltpu.VMEM((length, width), BF16),
            pltpu.VMEM(w_a.shape, BF16),
            pltpu.VMEM((length, q_cols), BF16),
            pltpu.VMEM((length, HEAD), BF16),
            pltpu.VMEM((length, HEAD), BF16),
            pltpu.VMEM((length, q_cols), BF16),
            pltpu.VMEM((length, q_cols), BF16),
            pltpu.VMEM((length, q_cols + 2 * HEAD), BF16),
            pltpu.VMEM((length, HEAD), F32),
            pltpu.VMEM((length, HEAD), F32),
            pltpu.VMEM((width, cols), BF16),
            pltpu.VMEM((width, q_cols), BF16),
            pltpu.VMEM((width, units), BF16),
            pltpu.VMEM((width, 2 * units), BF16),
            pltpu.VMEM((length // 2, width), BF16),
            pltpu.VMEM((quarter, width), BF16),
            pltpu.VMEM((quarter, width), BF16),
            pltpu.VMEM((6, rows, 2 * units), BF16),
            pltpu.VMEM((8, rows, cols), BF16),
            pltpu.VMEM((8, rows, q_cols), BF16),
            pltpu.VMEM((2, rows, units), BF16),
            pltpu.VMEM((rows, 2 * units), F32),
            pltpu.VMEM((rows, cols), F32),
            pltpu.VMEM((rows, q_cols), F32),
            pltpu.VMEM((rows, units), F32),
            pltpu.VMEM((8, width), F32),
            pltpu.VMEM((width, HEAD), F32),
            pltpu.VMEM((8, rows, HEAD), F32),
            pltpu.VMEM((rows, 3 * HEAD), BF16),
            pltpu.VMEM((rows, 3 * HEAD), BF16),
            pltpu.VMEM((rows, 3 * HEAD), BF16),
            pltpu.SemaphoreType.DMA((2, 40)),
            pltpu.SemaphoreType.DMA((2, 8)),
            pltpu.SemaphoreType.DMA((72,)),
        ],
        compiler_params=pltpu.CompilerParams(
            collective_id=2, has_side_effects=True, vmem_limit_bytes=60 * MIB
        ),
        cost_estimate=pl.CostEstimate(
            flops=14 * length * width * q_cols, bytes_accessed=64 * MIB, transcendentals=0
        ),
        name="back",
    )(ga, grads_gu, grads_d, ffn_sum, w_a, q, k, v, mixed, normed, *rest)[:11]


def final_kernel(
    own, near, far, ffn_far, out_part, tokens, grad_residual, gains, output, grad_tokens
):
    output[...] = (out_part[...] + ffn_far[...].astype(F32)).astype(BF16)
    rows = tokens[...].astype(F32)
    grad_n = own[...].astype(F32) + near[...].astype(F32) + far[...].astype(F32)
    scale = lax.rsqrt(jnp.mean(rows * rows, axis=-1, keepdims=True) + EPS)
    weighted = grad_n * gains[0:1, :]
    inner = jnp.mean(rows * weighted, axis=-1, keepdims=True)
    grad_tokens[...] = grad_residual[...] + scale * weighted - rows * (scale * scale * scale * inner)


def final(blocks, gains):
    quarter, width = blocks[0].shape
    size = 128
    row = pl.BlockSpec((size, width), lambda i: (i, 0))
    return pl.pallas_call(
        final_kernel,
        grid=(quarter // size,),
        in_specs=[row] * 7 + [pl.BlockSpec((8, width), lambda i: (0, 0))],
        out_specs=[row, row],
        out_shape=[
            jax.ShapeDtypeStruct((quarter, width), BF16),
            jax.ShapeDtypeStruct((quarter, width), F32),
        ],
        compiler_params=pltpu.CompilerParams(vmem_limit_bytes=62 * MIB),
        name="final",
    )(*blocks, gains)


def positions_of(segments):
    places = jnp.arange(segments.shape[0], dtype=jnp.int32)
    previous = jnp.concatenate([jnp.full((1,), -1, jnp.int32), segments[:-1]])
    starts = lax.cummax(jnp.where(segments != previous, places, 0), axis=0)
    return places - starts


def per_device(
    n_dp,
    tokens,
    w_query,
    w_keyval,
    w_out,
    w_gate,
    w_up,
    w_down,
    norm_gains,
    segment_ids,
    grad_output,
):
    t = lax.axis_index("tensor").astype(jnp.int32)
    quarter, width = tokens.shape
    length = 4 * quarter
    q_cols = w_query.shape[1]
    units = w_gate.shape[1]

    gain_cols = jnp.pad(norm_gains.T, ((0, 0), (0, HEAD - 2)))
    shard_a = jnp.concatenate([w_query, w_keyval, w_out.T, gain_cols], axis=1)
    shard_d = w_down.T
    shard_g = jnp.concatenate([w_gate, w_up], axis=1)
    if n_dp != 8:
        shard_a, shard_d, shard_g = (
            lax.all_gather(w, "dp", axis=0, tiled=True) for w in (shard_a, shard_d, shard_g)
        )

    turn = t ^ jnp.arange(4, dtype=jnp.int32)
    positions = positions_of(segment_ids).reshape(4, quarter)[turn].reshape(length)
    valid = (segment_ids != 0).reshape(4, quarter)[turn].reshape(length).astype(F32)
    inverse = 10000.0 ** (-jnp.arange(HEAD // 2, dtype=F32) / (HEAD // 2))
    inverse = jnp.concatenate([inverse, inverse])[None, :]
    pos3 = positions.reshape(length // BLK, 1, BLK)
    valid3 = valid.reshape(length // BLK, 1, BLK)

    (cos, sin, w_a, w_down_t, w_gu, gains, normed, q, k, v, mixed, lse, residual, n2, go_all, gh) = front(
        n_dp, tokens, grad_output, shard_a, shard_d, shard_g, pos3, valid3, inverse, q_cols
    )
    grads_gu, grads_d, grad_residual, gain_two, ga, ffn_sum, out_part = middle(
        n_dp, n2, gh, go_all, w_gu, w_down_t, residual, grad_output, gains
    )
    part_own, part_far, part_near, ffn_far, gate, up, down, grads_a, keyval, out_grads, gain_grads = back(
        n_dp, ga, grads_gu, grads_d, ffn_sum, w_a, q, k, v, mixed, normed,
        lse, pos3, valid3, cos, sin, gains, gain_two
    )
    query = grads_a
    if n_dp != 8:

        def spread(full):
            return lax.psum_scatter(full.astype(F32), "dp", scatter_dimension=0, tiled=True)

        down, gate, up, grads_a, out_grads, gain_grads = (
            spread(w)
            for w in (grads_d, grads_gu[:, :units], grads_gu[:, units:], grads_a, out_grads, gain_grads)
        )
        keyval, gain_grads = lax.psum((grads_a[:, q_cols:], gain_grads), "tensor")
        query = grads_a[:, :q_cols]
    blocks = (part_own, part_near, part_far, ffn_far, out_part, tokens, grad_residual)
    output, grad_tokens = final(blocks, gains)

    return (
        output,
        grad_tokens,
        query,
        keyval,
        out_grads.T,
        gate,
        up,
        down.T,
        gain_grads[:, :2].T,
    )


def solution(mesh):
    return jax.shard_map(
        functools.partial(per_device, mesh.shape["dp"]),
        mesh=mesh,
        in_specs=(
            P(("dp", "tensor"), None),
            P("dp", "tensor"),
            P("dp", None),
            P("tensor", "dp"),
            P("dp", "tensor"),
            P("dp", "tensor"),
            P("tensor", "dp"),
            P(None, "dp"),
            P("dp"),
            P(("dp", "tensor"), None),
        ),
        out_specs=(
            P(("dp", "tensor"), None),
            P(("dp", "tensor"), None),
            P("dp", "tensor"),
            P("dp", None),
            P("tensor", "dp"),
            P("dp", "tensor"),
            P("dp", "tensor"),
            P("tensor", "dp"),
            P(None, "dp"),
        ),
        check_vma=False,
    )
```

```python
import functools

import jax
import jax.numpy as jnp
from jax import lax
from jax.experimental import pallas as pl
from jax.experimental.pallas import tpu as pltpu
from jax.sharding import PartitionSpec as P

WINDOW = 1024
EPS = 1e-6
MASKED = -1e30
HEAD = 128
BLK = 256
LOG2E = 1.4426950408889634
F32 = jnp.float32
BF16 = jnp.bfloat16
MIB = 1 << 20
EARLY = 3

NT = (((1,), (1,)), ((), ()))
TN = (((0,), (0,)), ((), ()))


def dot(left, right):
    return jnp.dot(left, right, preferred_element_type=F32)


def dot_nt(left, right):
    return lax.dot_general(left, right, NT, preferred_element_type=F32)


def dot_tn(left, right):
    return lax.dot_general(left, right, TN, preferred_element_type=F32)


def stacked(block, heads):
    return jnp.concatenate([block[:, h * HEAD : (h + 1) * HEAD] for h in range(heads)], axis=0)


def partner(t, j):
    rem, div = lax.rem, lax.div
    two = jnp.int32(2)
    j = jnp.int32(j)
    return rem(div(t, two) + div(j, two), two) * 2 + rem(rem(t, two) + rem(j, two), two)


def block_rows(i):
    return pl.ds(pl.multiple_of(i * BLK, BLK), BLK)


def key_row(t, kb):
    per = 512 // BLK
    return pl.multiple_of((partner(t, lax.div(kb, per)) * per + lax.rem(kb, per)) * BLK, BLK)


def query_block(t, i):
    per = 512 // BLK
    i = jnp.int32(i)
    return partner(t, lax.div(i, per)) * per + lax.rem(i, per)


def tiled3(row, heads):
    return jnp.concatenate([row] * heads, axis=1)


def attend(t, i, q, k, v, pos, valid, mixed, lse):
    cols = q.shape[1]
    heads = cols // HEAD
    wide = heads * BLK
    qb = query_block(t, i)
    mine = pl.ds(pl.multiple_of(i * BLK, BLK), BLK)
    q3 = stacked(q[mine, :], heads)
    at = qb * BLK + lax.broadcasted_iota(jnp.int32, (1, BLK), 1)
    low = at - jnp.minimum(pos[i], WINDOW - 1)
    at3, low3 = tiled3(at, heads), tiled3(low, heads)
    factor = HEAD**-0.5 * LOG2E

    def step(kb, carry):
        peak, total, acc = carry
        row = key_row(t, kb)
        s = dot_nt(k[pl.ds(row, BLK), :], q3) * factor
        u = kb * BLK + lax.broadcasted_iota(jnp.int32, (BLK, wide), 0)
        s = jnp.where((u <= at3) & (u >= low3), s, MASKED)
        new_peak = jnp.maximum(peak, jnp.max(s, axis=0, keepdims=True))
        p = jnp.exp2(s - new_peak)
        shrink = jnp.exp2(peak - new_peak)
        total = total * shrink + jnp.sum(p, axis=0, keepdims=True)
        acc = acc * shrink + dot_tn(v[pl.ds(row, BLK), :], p.astype(BF16))
        return new_peak, total, acc

    peak, total, acc = lax.fori_loop(
        jnp.maximum(qb - WINDOW // BLK, 0),
        qb + 1,
        step,
        (
            jnp.full((1, wide), MASKED, F32),
            jnp.zeros((1, wide), F32),
            jnp.zeros((HEAD, wide), F32),
        ),
    )
    lse[i] = peak + jnp.log2(total)
    acc = acc * (tiled3(valid[i], heads) / total)
    mixed[mine, :] = jnp.concatenate(
        [acc[:, h * BLK : (h + 1) * BLK].T for h in range(heads)], axis=1
    ).astype(BF16)


def ring_device(p, n):
    p = lax.rem(p + n, jnp.int32(n))
    down = lax.div(p, jnp.int32(n // 2))
    return (1 - down) * 2 * p + down * (2 * (n - 1 - p) + 1)


def ring_place(d, n):
    z, y = lax.div(d, jnp.int32(2)), lax.rem(d, jnp.int32(2))
    return z + y * (n - 1 - 2 * z)


def send(src, dst, sems, at, device):
    return pltpu.make_async_remote_copy(
        src_ref=src,
        dst_ref=dst,
        send_sem=sems.at[0, at],
        recv_sem=sems.at[1, at],
        device_id=device,
        device_id_type=pl.DeviceIdType.MESH,
    )


class Ring:
    def __init__(self, shard, full, sems, first_sem, own, n, direction):
        self.shard, self.full, self.sems, self.at, self.own = shard, full, sems, first_sem, own
        self.n, self.dir = n, direction
        self.copies = {}

    def block(self, offset, place):
        rows = self.shard.shape[0]
        at = ring_device(place + offset * self.dir, self.n) * rows
        return self.full.at[pl.ds(pl.multiple_of(at, rows & -rows), rows), :]

    def begin(self, place):
        self.place = place
        if self.n == 8:
            target = self.block(0, place)
        else:
            target = self.full
        self.local = pltpu.make_async_copy(self.shard, target, self.own)
        self.local.start()
        self.start(1)

    def start(self, s):
        if self.n != 8:
            return
        for way in (0, 1):
            if s > self.n // 2 - way:
                continue
            sign = 1 - 2 * way
            block = self.block(-sign * (s - 1), self.place)
            device = ring_device(self.place + sign * self.dir, self.n)
            src = self.shard if s == 1 else block
            at = self.at + 2 * (s - 1) + way
            copy = send(src, block, self.sems, at, {"dp": device})
            copy.start()
            self.copies[s, way] = copy

    def arrived(self, s):
        for way in (0, 1):
            if (s, way) in self.copies:
                self.copies[s, way].wait_recv()

    def next(self, s):
        self.arrived(s)
        self.start(s + 1)

    def end(self):
        for copy in self.copies.values():
            copy.wait_send()
        self.local.wait()


class RingSum:
    def __init__(self, full, recv, sems, first_sem, n, direction, place, first_hop=1):
        self.full, self.recv, self.sems, self.at = full, recv, sems, first_sem
        self.n, self.dir, self.place, self.first_hop = n, direction, place, first_hop
        self.rows = full.shape[0] // n
        self.copies = {}

    def block(self, offset):
        at = ring_device(self.place + offset * self.dir, self.n) * self.rows
        return pl.ds(pl.multiple_of(at, self.rows & -self.rows), self.rows)

    def last(self, way):
        return self.n // 2 - way

    def slot(self, s, way):
        return way * (self.recv.shape[0] // 2) + s - self.first_hop

    def start(self, s, ways=(0, 1), source=None):
        for way in ways:
            if self.n == 8 and s <= self.last(way):
                sign = 1 - 2 * way
                device = ring_device(self.place + sign * self.dir, self.n)
                rows = self.block(sign * (self.last(way) + 1 - s))
                src = (self.full if source is None else source).at[rows, :]
                slot = self.slot(s, way)
                copy = send(src, self.recv.at[slot], self.sems, self.at + slot, {"dp": device})
                copy.start()
                self.copies[s, way] = copy

    def arrived(self, s, way):
        self.copies[s, way].wait_recv()
        return self.recv[self.slot(s, way)]

    def add(self, s, start=False):
        for way in (0, 1):
            if self.n == 8 and s < self.last(way):
                far = self.last(way)
                mine = self.block((1 - 2 * way) * (far - s))
                self.full[mine, :] = self.full[mine, :] + self.arrived(s, way)
                if start:
                    self.start(s + 1, (way,))

    def next(self, s):
        self.add(s, True)

    def close(self, way):
        if self.n == 8:
            mine = self.block(0)
            self.full[mine, :] = self.full[mine, :] + self.arrived(self.last(way), way)

    def result(self, ways=(0, 1)):
        acc = self.full[self.block(0), :].astype(F32)
        for way in ways:
            acc = acc + self.arrived(self.last(way), way).astype(F32)
        return acc

    def save(self, offsets, target, local):
        if self.n != 8:
            return []
        blocks = [self.block(offset) for offset in offsets]
        return [local(self.full.at[rows, :], target.at[rows, :]) for rows in blocks]

    def end(self):
        for copy in self.copies.values():
            copy.wait_send()


def front_kernel(
    n_dp,
    tokens,
    grad_output,
    shard_a,
    shard_d,
    shard_g,
    pos,
    valid,
    inverse,
    cos_out,
    sin_out,
    w_a_out,
    w_d_out,
    w_g,
    gains,
    normed_out,
    q_out,
    k_out,
    v_out,
    mixed_out,
    lse,
    residual_out,
    n2_out,
    go_out,
    gh_out,
    cos,
    sin,
    w_a,
    w_d,
    x4,
    normed,
    q,
    k,
    v,
    mixed,
    near_recv,
    far_recv,
    x_recv,
    sum_buf,
    n2_own,
    go_buf,
    gh_buf,
    res,
    ring_sems,
    pair_sems,
    local_sems,
):
    quarter, width = tokens.shape
    q_cols = q.shape[1]
    heads = q_cols // HEAD
    kv_at = q_cols + 2 * HEAD
    gain_at = kv_at + q_cols
    t = lax.axis_index("tensor").astype(jnp.int32)
    place = ring_place(lax.axis_index("dp").astype(jnp.int32), n_dp)
    near_id, far_id = {"tensor": partner(t, 1)}, {"tensor": partner(t, 2)}

    barrier = pltpu.get_barrier_semaphore()
    partners = [near_id, far_id]
    if n_dp == 8:
        partners += [{"dp": ring_device(place + 1, n_dp)}, {"dp": ring_device(place - 1, n_dp)}]
    for device in partners:
        pl.semaphore_signal(barrier, inc=1, device_id=device, device_id_type=pl.DeviceIdType.MESH)
    pl.semaphore_wait(barrier, len(partners))

    def rows_of(ref, j, size=1):
        return ref.at[pl.ds(j * quarter, size * quarter), :]

    used = [0]

    def local(src, dst):
        copy = pltpu.make_async_copy(src, dst, local_sems.at[used[0]])
        used[0] += 1
        copy.start()
        return copy

    ring_a = Ring(shard_a, w_a, ring_sems, 0, local_sems.at[24], n_dp, 1)
    ring_d = Ring(shard_d, w_d, ring_sems, 8, local_sems.at[25], n_dp, 1)
    ring_g = Ring(shard_g, w_g, ring_sems, 16, local_sems.at[26], n_dp, -1)

    ring_a.begin(place)
    x_far = send(tokens, rows_of(x4, 2), pair_sems, 0, far_id)
    x_far.start()
    x_near = send(tokens, rows_of(x4, 1), pair_sems, 1, near_id)
    x_near.start()
    x_own = local(tokens, rows_of(x4, 0))
    go_in = local(grad_output, res)
    def tables(i, carry):
        places = jnp.broadcast_to(pos[i].astype(F32), (HEAD, BLK)).T
        angles = places * inverse[...]
        sine = jnp.sin(angles)
        lane = lax.broadcasted_iota(jnp.int32, sine.shape, 1)
        cos[block_rows(i), :] = jnp.cos(angles)
        sin[block_rows(i), :] = jnp.where(lane < HEAD // 2, -sine, sine)
        return carry

    count = pos.shape[0]
    for s in (1, 2, 3):
        lax.fori_loop(count * (s - 1) // 3, count * s // 3, tables, 0)
        ring_a.next(s)
    ring_d.begin(place)
    ring_g.begin(place)
    ring_a.arrived(4)
    ring_a.local.wait()

    gain_rows = w_a[:, gain_at : gain_at + HEAD].astype(F32).T
    gains[...] = gain_rows[:8]

    def project(i, carry):
        mine = pl.ds(pl.multiple_of(i * BLK, BLK), BLK)
        rows = x4[mine, :].astype(F32)
        scale = lax.rsqrt(jnp.mean(rows * rows, axis=-1, keepdims=True) + EPS)
        n = (rows * scale * gains[0:1, :]).astype(BF16)
        normed[mine, :] = n
        y = dot(n, w_a[:, :kv_at])
        c, s = cos[mine, :], sin[mine, :]

        def turned(a):
            return (a * c + pltpu.roll(a, HEAD // 2, 1) * s).astype(BF16)

        q[mine, :] = jnp.concatenate(
            [turned(y[:, h * HEAD : (h + 1) * HEAD]) for h in range(heads)], axis=1
        )
        k[mine, :] = turned(y[:, q_cols : q_cols + HEAD])
        v[mine, :] = y[:, q_cols + HEAD : kv_at].astype(BF16)
        return carry

    per = quarter // BLK
    x_own.wait()
    x_near.wait_recv()
    lax.fori_loop(0, 2 * per, project, 0)
    x_far.wait_recv()
    x_last = send(rows_of(x4, 2), rows_of(x4, 3), pair_sems, 2, near_id)
    x_last.start()
    go_in.wait()
    go_buf[...] = res[...].astype(BF16)
    go_far = send(go_buf, rows_of(go_out, 2), pair_sems, 3, far_id)
    go_far.start()
    go_near = send(go_buf, rows_of(go_out, 1), pair_sems, 4, near_id)
    go_near.start()
    go_own = local(go_buf, rows_of(go_out, 0))
    x_last.wait_recv()
    lax.fori_loop(2 * per, 4 * per, project, 0)
    copies = [
        local(cos, cos_out),
        local(sin, sin_out),
        local(normed, normed_out),
        local(q, q_out),
        local(k, k_out),
        local(v, v_out),
        local(w_a, w_a_out),
    ]

    def attention(i, carry):
        attend(t, i, q, k, v, pos, valid, mixed, lse)
        return carry

    part = x4

    def out_product(i, carry):
        mine = pl.ds(pl.multiple_of(i * BLK, BLK), BLK)
        part[mine, :] = dot_nt(mixed[mine, :], w_a[:, kv_at:gain_at]).astype(BF16)
        return carry

    x_last.wait_send()
    lax.fori_loop(2 * per, 4 * per, attention, 0)
    ring_d.next(1)
    lax.fori_loop(2 * per, 4 * per, out_product, 0)
    part_far = send(rows_of(part, 3), far_recv, pair_sems, 5, near_id)
    part_far.start()
    lax.fori_loop(0, 1, attention, 0)
    part_far.wait_recv()
    sum_buf[...] = (part[pl.ds(2 * quarter, quarter), :].astype(F32) + far_recv[...].astype(F32)).astype(BF16)
    sum_far = send(sum_buf, x_recv, pair_sems, 6, far_id)
    sum_far.start()
    ring_g.next(1)
    lax.fori_loop(1, 2 * per, attention, 0)
    lax.fori_loop(0, 2 * per, out_product, 0)
    part_near = send(rows_of(part, 1), near_recv, pair_sems, 7, near_id)
    part_near.start()
    copies.append(local(mixed, mixed_out))
    ring_d.next(2)
    ring_d.next(3)
    ring_g.next(2)
    go_far.wait_recv()
    go_last = send(rows_of(go_out, 2), rows_of(go_out, 3), pair_sems, 8, near_id)
    go_last.start()
    part_near.wait_recv()
    sum_far.wait_recv()

    res[...] = (
        tokens[...].astype(F32)
        + part[pl.ds(0, quarter), :].astype(F32)
        + near_recv[...].astype(F32)
        + x_recv[...].astype(F32)
    )
    scale_two = lax.rsqrt(jnp.mean(res[...] * res[...], axis=-1, keepdims=True) + EPS)
    n2_own[...] = (res[...] * scale_two * gains[1:2, :]).astype(BF16)
    n2_far = send(n2_own, rows_of(n2_out, 2), pair_sems, 9, far_id)
    n2_far.start()
    n2_near = send(n2_own, rows_of(n2_out, 1), pair_sems, 10, near_id)
    n2_near.start()
    copies.append(local(n2_own, rows_of(n2_out, 0)))
    copies.append(local(res, residual_out))

    ring_d.arrived(4)
    ring_d.local.wait()
    copies.append(local(w_d, w_d_out))
    go_far.wait_send()
    go_near.wait_send()
    go_own.wait()

    def grad_hidden(i, carry):
        mine = pl.ds(pl.multiple_of(i * BLK, BLK), BLK)
        gh_buf[mine, :] = dot(go_buf[mine, :], w_d[...]).astype(BF16)
        return carry

    for j in range(4):
        if j == 1:
            go_near.wait_recv()
        if j == 3:
            go_last.wait_recv()
        if j > 0:
            load = local(rows_of(go_out, j), go_buf)
            load.wait()
        if j > 0:
            store.wait()
        lax.fori_loop(0, per, grad_hidden, 0)
        store = local(gh_buf, rows_of(gh_out, j))
        if j == 1:
            ring_g.next(3)

    n2_far.wait_recv()
    n2_last = send(rows_of(n2_out, 2), rows_of(n2_out, 3), pair_sems, 11, near_id)
    n2_last.start()
    ring_g.arrived(4)
    store.wait()
    for copy in copies:
        copy.wait()
    for copy in (x_far, x_near, part_far, sum_far, part_near, go_last, n2_far, n2_near, n2_last):
        copy.wait_send()
    n2_near.wait_recv()
    n2_last.wait_recv()
    ring_a.copies and [c.wait_send() for c in ring_a.copies.values()]
    ring_d.copies and [c.wait_send() for c in ring_d.copies.values()]
    ring_g.end()


def front(n_dp, tokens, grad_output, shard_a, shard_d, shard_g, pos, valid, inverse, q_cols):
    quarter, width = tokens.shape
    length = 4 * quarter
    heads = q_cols // HEAD
    units = shard_d.shape[1]
    cols_a = shard_a.shape[1]
    vmem = pl.BlockSpec(memory_space=pltpu.VMEM)
    hbm = pl.BlockSpec(memory_space=pl.ANY)
    blocks = length // BLK

    def out(rows, cols, kind=BF16):
        return jax.ShapeDtypeStruct((rows, cols), kind)

    return pl.pallas_call(
        functools.partial(front_kernel, n_dp),
        in_specs=[vmem, hbm, hbm, hbm, hbm, vmem, vmem, vmem],
        out_specs=[hbm, hbm, hbm, hbm, hbm, vmem, hbm, hbm, hbm, hbm, hbm, vmem, hbm, hbm, hbm, hbm],
        out_shape=[
            out(length, HEAD, F32),
            out(length, HEAD, F32),
            out(width, cols_a),
            out(width, units),
            out(width, 2 * units),
            out(8, width, F32),
            out(length, width),
            out(length, q_cols),
            out(length, HEAD),
            out(length, HEAD),
            out(length, q_cols),
            jax.ShapeDtypeStruct((blocks, 1, heads * BLK), F32),
            out(quarter, width, F32),
            out(length, width),
            out(length, width),
            out(length, units),
        ],
        scratch_shapes=[
            pltpu.VMEM((length, HEAD), F32),
            pltpu.VMEM((length, HEAD), F32),
            pltpu.VMEM((width, cols_a), BF16),
            pltpu.VMEM((width, units), BF16),
            pltpu.VMEM((length, width), BF16),
            pltpu.VMEM((length, width), BF16),
            pltpu.VMEM((length, q_cols), BF16),
            pltpu.VMEM((length, HEAD), BF16),
            pltpu.VMEM((length, HEAD), BF16),
            pltpu.VMEM((length, q_cols), BF16),
            pltpu.VMEM((quarter, width), BF16),
            pltpu.VMEM((quarter, width), BF16),
            pltpu.VMEM((quarter, width), BF16),
            pltpu.VMEM((quarter, width), BF16),
            pltpu.VMEM((quarter, width), BF16),
            pltpu.VMEM((quarter, width), BF16),
            pltpu.VMEM((quarter, units), BF16),
            pltpu.VMEM((quarter, width), F32),
            pltpu.SemaphoreType.DMA((2, 24)),
            pltpu.SemaphoreType.DMA((2, 12)),
            pltpu.SemaphoreType.DMA((32,)),
        ],
        compiler_params=pltpu.CompilerParams(
            collective_id=0, has_side_effects=True, vmem_limit_bytes=58 * MIB
        ),
        cost_estimate=pl.CostEstimate(
            flops=12 * length * width * q_cols, bytes_accessed=64 * MIB, transcendentals=0
        ),
        name="front",
    )(tokens, grad_output, shard_a, shard_d, shard_g, pos, valid, inverse)


def attend_back(t, i, q, do, mixed, lse, k, v, pos, valid, cos, sin, dqkv, dk_acc, dv_acc):
    cols = q.shape[1]
    heads = cols // HEAD
    wide = heads * BLK
    qb = query_block(t, i)
    mine = block_rows(i)
    q3 = stacked(q[mine, :], heads)
    do3 = stacked(do[mine, :], heads)
    centre3 = do3.astype(F32) * stacked(mixed[mine, :], heads).astype(F32)
    centre = jnp.sum(centre3.T, axis=0, keepdims=True)
    at = qb * BLK + lax.broadcasted_iota(jnp.int32, (1, BLK), 1)
    low = jnp.where(valid[i] > 0.0, at - jnp.minimum(pos[i], WINDOW - 1), at + 1)
    at3, low3 = tiled3(at, heads), tiled3(low, heads)
    total = lse[i]
    factor = HEAD**-0.5 * LOG2E

    def step(kb, acc):
        row = key_row(t, kb)
        kblk = k[pl.ds(row, BLK), :]
        vblk = v[pl.ds(row, BLK), :]
        s = dot_nt(kblk, q3) * factor - total
        u = kb * BLK + lax.broadcasted_iota(jnp.int32, (BLK, wide), 0)
        p = jnp.exp2(jnp.where((u <= at3) & (u >= low3), s, MASKED))
        gp = dot_nt(vblk, do3)
        ds = (p * (gp - centre)).astype(BF16)
        dv_acc[pl.ds(row, BLK), :] += dot(p.astype(BF16), do3)
        dk_acc[pl.ds(row, BLK), :] += dot(ds, q3)
        return acc + dot_tn(kblk, ds)

    acc = lax.fori_loop(
        jnp.maximum(qb - WINDOW // BLK, 0), qb + 1, step, jnp.zeros((HEAD, wide), F32)
    )
    scale = HEAD**-0.5
    c, sn = cos[mine, :] * scale, sin[mine, :] * scale

    def turned(a):
        return (a * c - pltpu.roll(a, HEAD // 2, 1) * sn).astype(BF16)

    dqkv[mine, :cols] = jnp.concatenate(
        [turned(acc[:, h * BLK : (h + 1) * BLK].T) for h in range(heads)], axis=1
    )


def gated(y, gh, half):
    gate, up = y[:, :half], y[:, half:]
    root = (2.0 / jnp.pi) ** 0.5
    square = gate * gate
    th = jnp.tanh(root * gate * (1.0 + 0.044715 * square))
    one = 0.5 * (1.0 + th)
    act = gate * one
    slope = one + 0.5 * gate * (1.0 - th * th) * (root * (1.0 + 3.0 * 0.044715 * square))
    return (act * up).astype(BF16), (gh * up * slope).astype(BF16), (gh * act).astype(BF16)


def greet(partners):
    barrier = pltpu.get_barrier_semaphore()
    for device in partners:
        pl.semaphore_signal(barrier, inc=1, device_id=device, device_id_type=pl.DeviceIdType.MESH)
    pl.semaphore_wait(barrier, len(partners))


def neighbours(n_dp, t, place):
    near_id, far_id = {"tensor": partner(t, 1)}, {"tensor": partner(t, 2)}
    others = []
    if n_dp == 8:
        others = [{"dp": ring_device(place + 1, n_dp)}, {"dp": ring_device(place - 1, n_dp)}]
    return near_id, far_id, [near_id, far_id] + others


class Local:
    def __init__(self, sems):
        self.sems, self.used = sems, 0

    def __call__(self, src, dst):
        copy = pltpu.make_async_copy(src, dst, self.sems.at[self.used])
        self.used += 1
        copy.start()
        return copy


def middle_kernel(
    n_dp,
    n2_in,
    gh_in,
    go_in,
    w_gu_in,
    w_d_in,
    residual,
    grad_output,
    gains,
    grads_gu_out,
    down_out,
    grad_residual,
    gain_two,
    ga_out,
    ffn_sum_out,
    out_part,
    far_recv,
    x_recv,
    near_recv,
    far_recv2,
    near_recv2,
    w_gu,
    n2,
    go,
    hidden,
    dgu,
    part,
    grads_d,
    grads_gu,
    stage,
    sum_buf,
    ga_own,
    recv_d,
    recv_g,
    rows_a,
    rows_b,
    ring_sems,
    pair_sems,
    local_sems,
):
    length, width = n2.shape
    units = hidden.shape[1]
    quarter = length // 4
    half = length // 2
    t = lax.axis_index("tensor").astype(jnp.int32)
    place = ring_place(lax.axis_index("dp").astype(jnp.int32), n_dp)
    near_id, far_id, partners = neighbours(n_dp, t, place)
    local = Local(local_sems)
    ring_d = RingSum(grads_d, recv_d, ring_sems, 0, n_dp, -1, place)
    ring_g = RingSum(grads_gu, recv_g, ring_sems, 8, n_dp, 1, place)

    far_rows, near_rows = pl.ds(half, half), pl.ds(0, half)
    load_w = local(w_gu_in, w_gu)
    load_far = [local(n2_in.at[far_rows, :], n2.at[far_rows, :]), local(gh_in.at[far_rows, :], hidden.at[far_rows, :])]
    load_near = [local(n2_in.at[near_rows, :], n2.at[near_rows, :]), local(gh_in.at[near_rows, :], hidden.at[near_rows, :])]
    greet(partners)

    def ffn(i, carry):
        mine = block_rows(i)
        y = dot(n2[mine, :], w_gu[...])
        gh = hidden[mine, :].astype(F32)
        hidden[mine, :], dgu[mine, :units], dgu[mine, units:] = gated(y, gh, units)
        return carry

    def back(first):
        def body(i, carry):
            part[block_rows(i), :] = dot_nt(dgu[block_rows(i + first), :], w_gu[...]).astype(BF16)
            return carry

        return body

    def fetch(src, dst):
        local(src, dst).wait()

    upper = pl.ds(quarter, quarter)
    per = half // BLK
    load_w.wait()
    for copy in load_far:
        copy.wait()
    lax.fori_loop(per, 2 * per, ffn, 0)
    lax.fori_loop(per // 2, per, back(per), 0)
    part_far = send(part.at[upper, :], far_recv, pair_sems, 0, near_id)
    part_far.start()
    lax.fori_loop(0, per // 2, back(per), 0)
    for copy in load_near:
        copy.wait()
    part_far.wait_recv()
    fetch(far_recv, stage)
    sum_buf[...] = (part[:quarter, :].astype(F32) + stage[...].astype(F32)).astype(BF16)
    sum_far = send(sum_buf, x_recv, pair_sems, 1, far_id)
    sum_far.start()
    blocks = width // BLK

    def load_go(i):
        return local(go_in.at[:, pl.ds(i * BLK, BLK)], go.at[i % 2])

    size = rows_a.shape[1]
    steps = quarter // size

    def rows_at(i):
        return pl.ds(i * size, size)

    def load_rows(i):
        return (
            local(residual.at[rows_at(i), :], rows_a.at[i % 2]),
            local(grad_output.at[rows_at(i), :], rows_b.at[i % 2]),
        )

    coming = load_go(0)
    coming_rows = load_rows(0)
    lax.fori_loop(0, per, ffn, 0)
    part_far.wait_send()
    lax.fori_loop(0, per, back(0), 0)
    part_near = send(part.at[upper, :], near_recv, pair_sems, 2, near_id)
    part_near.start()
    load_d = local(w_d_in, w_gu.at[:, :units])

    for i in range(blocks):
        coming.wait()
        if i + 1 < blocks:
            coming = load_go(i + 1)
        grads_d[i * BLK : (i + 1) * BLK, :] = dot_tn(go[i % 2], hidden[...]).astype(BF16)
    ring_d.start(1)

    def gu_grad(i, carry):
        grads_gu[block_rows(i), :] = dot_tn(n2[:, block_rows(i)], dgu[...]).astype(BF16)
        return carry

    part_near.wait_recv()
    fetch(near_recv, stage)
    lax.fori_loop(0, EARLY, gu_grad, 0)
    gain_two[...] = jnp.zeros_like(gain_two)
    sum_far.wait_send()
    sum_far.wait_recv()
    fetch(x_recv, sum_buf)
    stores = []
    ga_far = []
    for i in range(steps):
        for copy in coming_rows:
            copy.wait()
        if i + 1 < steps:
            if i > 0:
                stores[-1].wait()
            coming_rows = load_rows(i + 1)
        mine = slice(i * size, (i + 1) * size)
        rows = rows_a[i % 2]
        grad_n = part[mine, :].astype(F32) + stage[mine, :].astype(F32) + sum_buf[mine, :].astype(F32)
        scale = lax.rsqrt(jnp.mean(rows * rows, axis=-1, keepdims=True) + EPS)
        weighted = grad_n * gains[1:2, :]
        inner = jnp.mean(rows * weighted, axis=-1, keepdims=True)
        grad = rows_b[i % 2] + scale * weighted - rows * (scale * scale * scale * inner)
        rows_b[i % 2] = grad
        ga_own[mine, :] = grad.astype(BF16)
        gain_two[0:1, :] += jnp.sum(grad_n * rows * scale, axis=0, keepdims=True)
        stores.append(local(rows_b.at[i % 2], grad_residual.at[rows_at(i), :]))
        if i % (steps // 2) == steps // 2 - 1:
            piece = len(ga_far)
            at = piece * quarter // 2
            ga_far.append(
                send(
                    ga_own.at[pl.ds(at, quarter // 2), :],
                    ga_out.at[pl.ds(2 * quarter + at, quarter // 2), :],
                    pair_sems,
                    (3, 8)[piece],
                    far_id,
                )
            )
            ga_far[piece].start()

    def quarter_of(ref, j):
        return ref.at[pl.ds(j * quarter, quarter), :]

    ga_near = send(ga_own, quarter_of(ga_out, 1), pair_sems, 4, near_id)
    ga_near.start()
    stores_late = [local(ga_own, quarter_of(ga_out, 0))]
    ring_d.next(1)
    lax.fori_loop(EARLY, blocks, gu_grad, 0)
    ring_g.start(1)
    save_gu = local(grads_gu, grads_gu_out)
    ring_d.next(2)
    save_d = local(grads_d, down_out)
    part_near.wait_send()
    load_d.wait()

    def down_product(first):
        def body(i, carry):
            part[block_rows(i), :] = dot_nt(hidden[block_rows(i + first), :], w_gu[:, :units]).astype(BF16)
            return carry

        return body

    lax.fori_loop(0, per, down_product(per), 0)
    part_far2 = send(part.at[upper, :], far_recv2, pair_sems, 5, near_id)
    part_far2.start()
    part_far2.wait_recv()
    fetch(far_recv2, stage)
    sum_buf[...] = (part[:quarter, :].astype(F32) + stage[...].astype(F32)).astype(BF16)
    stores_late.append(local(sum_buf, ffn_sum_out))
    part_far2.wait_send()
    lax.fori_loop(0, per, down_product(0), 0)
    part_near2 = send(part.at[upper, :], near_recv2, pair_sems, 6, near_id)
    part_near2.start()
    part_near2.wait_recv()
    fetch(near_recv2, stage)
    for copy in stores[-2:]:
        copy.wait()
    stores = []
    coming = local(residual.at[rows_at(0), :], rows_a.at[0])
    for i in range(steps):
        coming.wait()
        if i + 1 < steps:
            if i > 0:
                stores[-1].wait()
            coming = local(residual.at[rows_at(i + 1), :], rows_a.at[(i + 1) % 2])
        mine = slice(i * size, (i + 1) * size)
        rows_a[i % 2] = rows_a[i % 2] + part[mine, :].astype(F32) + stage[mine, :].astype(F32)
        stores.append(local(rows_a.at[i % 2], out_part.at[rows_at(i), :]))
    stores_late += stores[-2:]

    ga_last = []
    for piece in (0, 1):
        ga_far[piece].wait_recv()
        at = piece * quarter // 2
        ga_last.append(
            send(
                ga_out.at[pl.ds(2 * quarter + at, quarter // 2), :],
                ga_out.at[pl.ds(3 * quarter + at, quarter // 2), :],
                pair_sems,
                (7, 9)[piece],
                near_id,
            )
        )
        ga_last[piece].start()
    save_d.wait()
    ring_d.add(3)
    ring_d.close(1)
    stores_late += ring_d.save((1, 0), down_out, local)
    save_gu.wait()
    ring_g.add(1)
    stores_late += ring_g.save((3, -2), grads_gu_out, local)
    ring_d.end()
    ring_g.end()
    ga_near.wait_recv()
    for copy in ga_last:
        copy.wait_recv()
    for copy in stores_late:
        copy.wait()
    for copy in (*ga_far, ga_near, *ga_last, part_near2):
        copy.wait_send()


def middle(n_dp, n2, gh, go, w_gu, w_d, residual, grad_output, gains):
    length, width = n2.shape
    units = gh.shape[1]
    quarter = length // 4
    rows = width // 8
    vmem = pl.BlockSpec(memory_space=pltpu.VMEM)
    hbm = pl.BlockSpec(memory_space=pl.ANY)
    shape = jax.ShapeDtypeStruct
    pair = shape((quarter, width), BF16)
    return pl.pallas_call(
        functools.partial(middle_kernel, n_dp),
        in_specs=[hbm] * 7 + [vmem],
        out_specs=[hbm] * 3 + [vmem] + [hbm] * 8,
        out_shape=[
            shape((width, 2 * units), BF16),
            shape((width, units), BF16),
            shape((quarter, width), F32),
            shape((8, width), F32),
            shape((length, width), BF16),
            pair,
            shape((quarter, width), F32),
            pair,
            pair,
            pair,
            pair,
            pair,
        ],
        scratch_shapes=[
            pltpu.VMEM((width, 2 * units), BF16),
            pltpu.VMEM((length, width), BF16),
            pltpu.VMEM((2, length, BLK), BF16),
            pltpu.VMEM((length, units), BF16),
            pltpu.VMEM((length, 2 * units), BF16),
            pltpu.VMEM((length // 2, width), BF16),
            pltpu.VMEM((width, units), BF16),
            pltpu.VMEM((width, 2 * units), BF16),
            pltpu.VMEM((quarter, width), BF16),
            pltpu.VMEM((quarter, width), BF16),
            pltpu.VMEM((quarter, width), BF16),
            pltpu.VMEM((6, rows, units), BF16),
            pltpu.VMEM((2, rows, 2 * units), BF16),
            pltpu.VMEM((2, 128, width), F32),
            pltpu.VMEM((2, 128, width), F32),
            pltpu.SemaphoreType.DMA((2, 16)),
            pltpu.SemaphoreType.DMA((2, 10)),
            pltpu.SemaphoreType.DMA((72,)),
        ],
        compiler_params=pltpu.CompilerParams(
            collective_id=1, has_side_effects=True, vmem_limit_bytes=63 * MIB
        ),
        cost_estimate=pl.CostEstimate(
            flops=14 * length * width * units, bytes_accessed=64 * MIB, transcendentals=0
        ),
        name="middle",
    )(n2, gh, go, w_gu, w_d, residual, grad_output, gains)[:7]


def back_kernel(
    n_dp,
    ga_in,
    grads_gu_in,
    grads_d_in,
    ffn_sum,
    w_a_in,
    q_in,
    k_in,
    v_in,
    mixed_in,
    normed_in,
    lse,
    pos,
    valid,
    cos,
    sin,
    gains,
    gain_two,
    part_own,
    x_recv,
    near_recv,
    x_recv2,
    gate_out,
    up_out,
    down_out,
    grads_a_out,
    keyval_out,
    out_out,
    gain_out,
    far_recv,
    acts,
    w_a,
    q,
    k,
    v,
    mixed,
    do,
    dqkv,
    dk_acc,
    dv_acc,
    grads_a,
    grads_o,
    grads_d,
    grads_gu,
    part,
    stage,
    sum_buf,
    recv_g,
    recv_a,
    recv_o,
    recv_d,
    result_gu,
    result_a,
    result_o,
    result_d,
    gain_acc,
    gain_cols,
    recv_s,
    small,
    small_near,
    small_far,
    ring_sems,
    pair_sems,
    local_sems,
):
    length, width = acts.shape
    quarter = length // 4
    half = length // 2
    q_cols = q.shape[1]
    kv_at = q_cols + 2 * HEAD
    out_at = kv_at + q_cols
    units = grads_gu.shape[1] // 2
    ring = n_dp == 8
    t = lax.axis_index("tensor").astype(jnp.int32)
    place = ring_place(lax.axis_index("dp").astype(jnp.int32), n_dp)
    near_id, far_id, partners = neighbours(n_dp, t, place)
    local = Local(local_sems)
    ring_g = RingSum(grads_gu, recv_g, ring_sems, 0, n_dp, 1, place, 2)
    ring_a = RingSum(grads_a, recv_a, ring_sems, 8, n_dp, -1, place)
    ring_o = RingSum(grads_o, recv_o, ring_sems, 24, n_dp, -1, place)
    ring_d = RingSum(grads_d, recv_d, ring_sems, 32, n_dp, -1, place, 4)
    ring_s = RingSum(gain_cols, recv_s, ring_sems, 16, n_dp, 1, place)

    load_ga, load_w, load_mixed = local(ga_in, acts), local(w_a_in, w_a), local(mixed_in, mixed)
    loads = [local(src, dst) for src, dst in ((q_in, q), (k_in, k), (v_in, v))]
    greet(partners)
    ring_g.start(2, source=grads_gu_in)
    ring_d.start(4, source=grads_d_in)
    sum_far2 = send(ffn_sum, x_recv2, pair_sems, 0, far_id)
    sum_far2.start()
    if ring:
        loads += [local(grads_gu_in, grads_gu), local(grads_d_in, grads_d)]
    load_ga.wait()
    load_w.wait()

    def grad_mixed(i, carry):
        do[block_rows(i), :] = dot(acts[block_rows(i), :], w_a[:, kv_at:out_at]).astype(BF16)
        return carry

    def out_grad(i, carry):
        grads_o[block_rows(i), :] = dot_tn(acts[:, block_rows(i)], mixed[...]).astype(BF16)
        return carry

    blocks = length // BLK
    lax.fori_loop(0, blocks, grad_mixed, 0)
    load_mixed.wait()
    lax.fori_loop(0, width // BLK, out_grad, 0)
    ring_o.start(1)
    load_normed = local(normed_in, acts)
    for copy in loads:
        copy.wait()

    dk_acc[...] = jnp.zeros_like(dk_acc)
    dv_acc[...] = jnp.zeros_like(dv_acc)

    def attention(i, carry):
        attend_back(t, i, q, do, mixed, lse, k, v, pos, valid, cos, sin, dqkv, dk_acc, dv_acc)
        return carry

    lax.fori_loop(0, blocks * 3 // 4, attention, 0)
    ring_g.next(2)
    ring_o.next(1)
    lax.fori_loop(blocks * 3 // 4, blocks, attention, 0)
    a = dk_acc[...] * HEAD**-0.5
    dqkv[:, q_cols : q_cols + HEAD] = (a * cos[...] - pltpu.roll(a, HEAD // 2, 1) * sin[...]).astype(BF16)
    dqkv[:, q_cols + HEAD : kv_at] = dv_acc[...].astype(BF16)
    load_normed.wait()

    gain_acc[...] = jnp.zeros_like(gain_acc)

    def grad_normed(first):
        def body(i, carry):
            mine = block_rows(i + first)
            y = dot_nt(dqkv[mine, :], w_a[:, :kv_at])
            part[block_rows(i), :] = y.astype(BF16)
            gain_acc[0:1, :] += jnp.sum(y * acts[mine, :].astype(F32), axis=0, keepdims=True)
            return carry

        return body

    def fetch(src, dst):
        local(src, dst).wait()

    upper = pl.ds(quarter, quarter)
    per = half // BLK
    lax.fori_loop(0, per, grad_normed(per), 0)
    part_far = send(part.at[upper, :], far_recv, pair_sems, 1, near_id)
    part_far.start()
    ring_o.next(2)

    def qkv_grad(i, carry):
        grads_a[block_rows(i), :] = dot_tn(acts[:, block_rows(i)], dqkv[...]).astype(BF16)
        return carry

    lax.fori_loop(0, width // BLK, qkv_grad, 0)
    ring_a.start(1)
    ring_g.next(3)
    part_far.wait_recv()
    fetch(far_recv, stage)
    sum_buf[...] = (part[:quarter, :].astype(F32) + stage[...].astype(F32)).astype(BF16)
    sum_far = send(sum_buf, x_recv, pair_sems, 2, far_id)
    sum_far.start()
    part_far.wait_send()
    lax.fori_loop(0, per, grad_normed(0), 0)
    part_near = send(part.at[upper, :], near_recv, pair_sems, 3, near_id)
    part_near.start()
    stores = [local(part.at[pl.ds(0, quarter), :], part_own)]
    ring_o.next(3)

    both = jnp.concatenate(
        [gain_acc[0:1, :] / gains[0:1, :], gain_two[0:1, :], jnp.zeros((HEAD - 2, width), F32)], axis=0
    )
    gain_cols[...] = both.T
    ring_s.start(1)
    ring_a.next(1)
    ring_s.next(1)
    if ring:
        result_d[...] = ring_d.result((0,))
        stores.append(local(result_d, down_out))
    ring_a.next(2)
    ring_s.next(2)
    if ring:
        result_o[...] = ring_o.result()
        stores.append(local(result_o, out_out))
    ring_a.next(3)
    ring_s.next(3)
    if ring:
        result_gu[...] = ring_g.result()
        stores += [local(result_gu.at[:, :units], gate_out), local(result_gu.at[:, units:], up_out)]

    if ring:
        shard = ring_a.result()
        result_a[:, :q_cols] = shard[:, :q_cols]
        small[:, : 2 * HEAD] = shard[:, q_cols:kv_at].astype(BF16)
        small[:, 2 * HEAD :] = ring_s.result().astype(BF16)
        small_one = send(small, small_near, pair_sems, 4, near_id)
        small_one.start()
        small_one.wait_send()
        small_one.wait_recv()
        small[...] = (small[...].astype(F32) + small_near[...].astype(F32)).astype(BF16)
        small_two = send(small, small_far, pair_sems, 5, far_id)
        small_two.start()
        small_two.wait_send()
        small_two.wait_recv()
        both = small[...].astype(F32) + small_far[...].astype(F32)
        result_a[:, q_cols:kv_at] = both[:, : 2 * HEAD]
        ring_s.end()
        gain_cols[: both.shape[0], :] = both[:, 2 * HEAD :]
        stores.append(local(result_a.at[:, :q_cols], grads_a_out))
        stores.append(local(result_a.at[:, q_cols:], keyval_out))
        stores.append(local(gain_cols.at[pl.ds(0, both.shape[0]), :], gain_out))
    else:
        stores.append(local(grads_a, grads_a_out))
        stores.append(local(result_a.at[:, q_cols:], keyval_out))
        stores.append(local(grads_o, out_out))
        stores.append(local(gain_cols, gain_out))
    for copy in stores:
        copy.wait()
    for each in (ring_g, ring_a, ring_o, ring_d):
        each.end()
    for copy in (sum_far2, part_near, sum_far):
        copy.wait_send()
    sum_far2.wait_recv()
    part_near.wait_recv()
    sum_far.wait_recv()


def back(n_dp, ga, grads_gu, grads_d, ffn_sum, w_a, q, k, v, mixed, normed, *rest):
    length, width = ga.shape
    units = grads_gu.shape[1] // 2
    quarter = length // 4
    rows = width // 8
    q_cols = q.shape[1]
    cols = q_cols + 2 * HEAD
    vmem = pl.BlockSpec(memory_space=pltpu.VMEM)
    hbm = pl.BlockSpec(memory_space=pl.ANY)
    shape = jax.ShapeDtypeStruct
    pair = shape((quarter, width), BF16)
    ring = n_dp == 8
    return pl.pallas_call(
        functools.partial(back_kernel, n_dp),
        in_specs=[hbm] * 10 + [vmem] * 7,
        out_specs=[hbm] * 12,
        out_shape=[
            pair,
            pair,
            pair,
            pair,
            shape((rows, units), F32),
            shape((rows, units), F32),
            shape((rows, units), F32),
            shape((rows, q_cols), F32) if ring else shape((width, cols), BF16),
            shape((rows, 2 * HEAD), F32),
            shape((rows, q_cols), F32) if ring else shape((width, q_cols), BF16),
            shape((rows if ring else width, HEAD), F32),
            pair,
        ],
        scratch_shapes=[
            pltpu.VMEM((length, width), BF16),
            pltpu.VMEM(w_a.shape, BF16),
            pltpu.VMEM((length, q_cols), BF16),
            pltpu.VMEM((length, HEAD), BF16),
            pltpu.VMEM((length, HEAD), BF16),
            pltpu.VMEM((length, q_cols), BF16),
            pltpu.VMEM((length, q_cols), BF16),
            pltpu.VMEM((length, q_cols + 2 * HEAD), BF16),
            pltpu.VMEM((length, HEAD), F32),
            pltpu.VMEM((length, HEAD), F32),
            pltpu.VMEM((width, cols), BF16),
            pltpu.VMEM((width, q_cols), BF16),
            pltpu.VMEM((width, units), BF16),
            pltpu.VMEM((width, 2 * units), BF16),
            pltpu.VMEM((length // 2, width), BF16),
            pltpu.VMEM((quarter, width), BF16),
            pltpu.VMEM((quarter, width), BF16),
            pltpu.VMEM((6, rows, 2 * units), BF16),
            pltpu.VMEM((8, rows, cols), BF16),
            pltpu.VMEM((8, rows, q_cols), BF16),
            pltpu.VMEM((2, rows, units), BF16),
            pltpu.VMEM((rows, 2 * units), F32),
            pltpu.VMEM((rows, cols), F32),
            pltpu.VMEM((rows, q_cols), F32),
            pltpu.VMEM((rows, units), F32),
            pltpu.VMEM((8, width), F32),
            pltpu.VMEM((width, HEAD), F32),
            pltpu.VMEM((8, rows, HEAD), F32),
            pltpu.VMEM((rows, 3 * HEAD), BF16),
            pltpu.VMEM((rows, 3 * HEAD), BF16),
            pltpu.VMEM((rows, 3 * HEAD), BF16),
            pltpu.SemaphoreType.DMA((2, 40)),
            pltpu.SemaphoreType.DMA((2, 8)),
            pltpu.SemaphoreType.DMA((72,)),
        ],
        compiler_params=pltpu.CompilerParams(
            collective_id=2, has_side_effects=True, vmem_limit_bytes=60 * MIB
        ),
        cost_estimate=pl.CostEstimate(
            flops=14 * length * width * q_cols, bytes_accessed=64 * MIB, transcendentals=0
        ),
        name="back",
    )(ga, grads_gu, grads_d, ffn_sum, w_a, q, k, v, mixed, normed, *rest)[:11]


def final_kernel(
    own, near, far, ffn_far, out_part, tokens, grad_residual, gains, output, grad_tokens
):
    output[...] = (out_part[...] + ffn_far[...].astype(F32)).astype(BF16)
    rows = tokens[...].astype(F32)
    grad_n = own[...].astype(F32) + near[...].astype(F32) + far[...].astype(F32)
    scale = lax.rsqrt(jnp.mean(rows * rows, axis=-1, keepdims=True) + EPS)
    weighted = grad_n * gains[0:1, :]
    inner = jnp.mean(rows * weighted, axis=-1, keepdims=True)
    grad_tokens[...] = grad_residual[...] + scale * weighted - rows * (scale * scale * scale * inner)


def final(blocks, gains):
    quarter, width = blocks[0].shape
    size = 128
    row = pl.BlockSpec((size, width), lambda i: (i, 0))
    return pl.pallas_call(
        final_kernel,
        grid=(quarter // size,),
        in_specs=[row] * 7 + [pl.BlockSpec((8, width), lambda i: (0, 0))],
        out_specs=[row, row],
        out_shape=[
            jax.ShapeDtypeStruct((quarter, width), BF16),
            jax.ShapeDtypeStruct((quarter, width), F32),
        ],
        compiler_params=pltpu.CompilerParams(vmem_limit_bytes=62 * MIB),
        name="final",
    )(*blocks, gains)


def positions_of(segments):
    places = jnp.arange(segments.shape[0], dtype=jnp.int32)
    previous = jnp.concatenate([jnp.full((1,), -1, jnp.int32), segments[:-1]])
    starts = lax.cummax(jnp.where(segments != previous, places, 0), axis=0)
    return places - starts


def per_device(
    n_dp,
    tokens,
    w_query,
    w_keyval,
    w_out,
    w_gate,
    w_up,
    w_down,
    norm_gains,
    segment_ids,
    grad_output,
):
    t = lax.axis_index("tensor").astype(jnp.int32)
    quarter, width = tokens.shape
    length = 4 * quarter
    q_cols = w_query.shape[1]
    units = w_gate.shape[1]

    gain_cols = jnp.pad(norm_gains.T, ((0, 0), (0, HEAD - 2)))
    shard_a = jnp.concatenate([w_query, w_keyval, w_out.T, gain_cols], axis=1)
    shard_d = w_down.T
    shard_g = jnp.concatenate([w_gate, w_up], axis=1)
    if n_dp != 8:
        shard_a, shard_d, shard_g = (
            lax.all_gather(w, "dp", axis=0, tiled=True) for w in (shard_a, shard_d, shard_g)
        )

    turn = t ^ jnp.arange(4, dtype=jnp.int32)
    positions = positions_of(segment_ids).reshape(4, quarter)[turn].reshape(length)
    valid = (segment_ids != 0).reshape(4, quarter)[turn].reshape(length).astype(F32)
    inverse = 10000.0 ** (-jnp.arange(HEAD // 2, dtype=F32) / (HEAD // 2))
    inverse = jnp.concatenate([inverse, inverse])[None, :]
    pos3 = positions.reshape(length // BLK, 1, BLK)
    valid3 = valid.reshape(length // BLK, 1, BLK)

    (cos, sin, w_a, w_down_t, w_gu, gains, normed, q, k, v, mixed, lse, residual, n2, go_all, gh) = front(
        n_dp, tokens, grad_output, shard_a, shard_d, shard_g, pos3, valid3, inverse, q_cols
    )
    grads_gu, grads_d, grad_residual, gain_two, ga, ffn_sum, out_part = middle(
        n_dp, n2, gh, go_all, w_gu, w_down_t, residual, grad_output, gains
    )
    part_own, part_far, part_near, ffn_far, gate, up, down, grads_a, keyval, out_grads, gain_grads = back(
        n_dp, ga, grads_gu, grads_d, ffn_sum, w_a, q, k, v, mixed, normed,
        lse, pos3, valid3, cos, sin, gains, gain_two
    )
    query = grads_a
    if n_dp != 8:

        def spread(full):
            return lax.psum_scatter(full.astype(F32), "dp", scatter_dimension=0, tiled=True)

        down, gate, up, grads_a, out_grads, gain_grads = (
            spread(w)
            for w in (grads_d, grads_gu[:, :units], grads_gu[:, units:], grads_a, out_grads, gain_grads)
        )
        keyval, gain_grads = lax.psum((grads_a[:, q_cols:], gain_grads), "tensor")
        query = grads_a[:, :q_cols]
    blocks = (part_own, part_near, part_far, ffn_far, out_part, tokens, grad_residual)
    output, grad_tokens = final(blocks, gains)

    return (
        output,
        grad_tokens,
        query,
        keyval,
        out_grads.T,
        gate,
        up,
        down.T,
        gain_grads[:, :2].T,
    )


def solution(mesh):
    return jax.shard_map(
        functools.partial(per_device, mesh.shape["dp"]),
        mesh=mesh,
        in_specs=(
            P(("dp", "tensor"), None),
            P("dp", "tensor"),
            P("dp", None),
            P("tensor", "dp"),
            P("dp", "tensor"),
            P("dp", "tensor"),
            P("tensor", "dp"),
            P(None, "dp"),
            P("dp"),
            P(("dp", "tensor"), None),
        ),
        out_specs=(
            P(("dp", "tensor"), None),
            P(("dp", "tensor"), None),
            P("dp", "tensor"),
            P("dp", None),
            P("tensor", "dp"),
            P("dp", "tensor"),
            P("dp", "tensor"),
            P("tensor", "dp"),
            P(None, "dp"),
        ),
        check_vma=False,
    )
```
